32 devices in a mesh: seq: 8 (over z, x), grp: 4 (over y, core).
Axes of the slice: x: 2, y: 2, z: 4, core: 2. Of those that a mesh axis runs over, the one named last changes fastest.
Arguments:
- tokens: bfloat16 [8, 4096, 768], P('grp', 'seq')
- seq_lengths: int32 [8], P('grp'), may hold values from 2048 to 4096, as said below
- answer_mask: int32 [8, 4096], P('grp', 'seq'), may hold values from 0 to 1, as said below
- out_grad: bfloat16 [8, 4096, 768], P('grp', 'seq'), may hold values from -6 to 6
- qkv_weight: float32 [768, 2304], P(('seq', 'grp')), may hold values from -0.21875 to 0.21875
- merge_weight: float32 [768, 768], P(('seq', 'grp')), may hold values from -0.875 to 0.875
- expand_weight: float32 [768, 3072], P(('seq', 'grp')), may hold values from -0.21875 to 0.21875
- shrink_weight: float32 [3072, 768], P(('seq', 'grp')), may hold values from -0.109375 to 0.109375
- small_params: float32 [768, 14], P(('seq', 'grp'))
- qkv_rows: float32 [768], P(('seq', 'grp')), may hold values from 3.5267696e-08 to 1.4107079e-07
- qkv_cols: float32 [2304], replicated, may hold values from 3.5267696e-08 to 1.4107079e-07
- merge_rows: float32 [768], P(('seq', 'grp')), may hold values from 3.5267696e-08 to 1.4107079e-07
- merge_cols: float32 [768], replicated, may hold values from 3.5267696e-08 to 1.4107079e-07
- expand_rows: float32 [768], P(('seq', 'grp')), may hold values from 3.5267696e-08 to 1.4107079e-07
- expand_cols: float32 [3072], replicated, may hold values from 3.5267696e-08 to 1.4107079e-07
- shrink_rows: float32 [3072], P(('seq', 'grp')), may hold values from 3.5267696e-08 to 1.4107079e-07
- shrink_cols: float32 [768], replicated, may hold values from 3.5267696e-08 to 1.4107079e-07
- small_moment: float32 [768, 14], P(('seq', 'grp')), may hold values from 3.5267696e-08 to 1.4107079e-07
Outputs:
- block_out: bfloat16 [8, 4096, 768], P('grp', 'seq')
- input_grad: float32 [8, 4096, 768], P('grp', 'seq')
- grad_norm: float32 [], replicated
- qkv_grad: float32 [768, 2304], P(('seq', 'grp'))
- qkv_rows_new: float32 [768], P(('seq', 'grp'))
- qkv_cols_new: float32 [2304], replicated
- qkv_new: float32 [768, 2304], P(('seq', 'grp'))
- qkv_low: bfloat16 [768, 2304], P(('seq', 'grp'))
- merge_grad: float32 [768, 768], P(('seq', 'grp'))
- merge_rows_new: float32 [768], P(('seq', 'grp'))
- merge_cols_new: float32 [768], replicated
- merge_new: float32 [768, 768], P(('seq', 'grp'))
- merge_low: bfloat16 [768, 768], P(('seq', 'grp'))
- expand_grad: float32 [768, 3072], P(('seq', 'grp'))
- expand_rows_new: float32 [768], P(('seq', 'grp'))
- expand_cols_new: float32 [3072], replicated
- expand_new: float32 [768, 3072], P(('seq', 'grp'))
- expand_low: bfloat16 [768, 3072], P(('seq', 'grp'))
- shrink_grad: float32 [3072, 768], P(('seq', 'grp'))
- shrink_rows_new: float32 [3072], P(('seq', 'grp'))
- shrink_cols_new: float32 [768], replicated
- shrink_new: float32 [3072, 768], P(('seq', 'grp'))
- shrink_low: bfloat16 [3072, 768], P(('seq', 'grp'))
- small_grad: float32 [768, 14], P(('seq', 'grp'))
- small_moment_new: float32 [768, 14], P(('seq', 'grp'))
- small_new: float32 [768, 14], P(('seq', 'grp'))
- small_low: bfloat16 [768, 14], P(('seq', 'grp'))
The draws below stay inside these ranges and needn't reach their ends.
Inputs may be any that keep to these rules, and one draw needn't show every extreme that they name: `seq_lengths`: each group of 2 consecutive sequences holds one of length 4096. `answer_mask`: 1 on the positions of answer spans, 0 elsewhere.
All inputs are finite; a program needn't handle non-finite values.
Results may differ from the reference program's by a relative error of at most 0.015.
The reference program's roundings to bfloat16 on the way count: a program that leaves them out, or rounds other values in their place, can miss the bound.
Values may be sent and summed in bfloat16 or wider, within the bound.
No kernel may reach another device: no remote copies, remote signals or barrier semaphores. Data moves between devices by JAX's collectives and lax.ppermute only.
A program may use at most 256 MiB of HBM per device.

```python
import math
import jax
import jax.numpy as jnp
from jax import lax

D = 768
HEADS = 12
HEAD_DIM = 64
FF = 3072
WIN = 64
PWIN = 64
PIECE = 512
SEQ_GRP = 2
SEQS = 8
LEN = 4096
N_SEQ = 8
N_GRP = 4


def rising(base):
    feature = jnp.arange(D, dtype=jnp.int32)
    owner = feature // (D // (N_SEQ * N_GRP))
    slow_part = (owner // N_GRP).astype(jnp.float32) / (N_SEQ - 1)
    fast_part = (owner % N_GRP).astype(jnp.float32) / (N_GRP - 1)
    return base ** (slow_part + fast_part - 1.0)


def draw_tokens(key, part):
    key = jax.random.fold_in(key, 11)
    values = jax.random.normal(key, (SEQS, LEN, D), jnp.float32) * rising(3.0)
    return values.astype(jnp.bfloat16)


def draw_small_params(key, part):
    key = jax.random.fold_in(key, 12)
    keys = jax.random.split(key, 5)
    gain_one = rising(3.0) * jax.random.uniform(keys[0], (D,), jnp.float32, 0.8, 1.25)
    bias_one = 0.3 * jax.random.normal(keys[1], (D,), jnp.float32)
    bias_two = 0.3 * jax.random.normal(keys[3], (D,), jnp.float32)
    gain_two = jax.random.uniform(keys[2], (D,), jnp.float32, 0.6, 1.5)
    taps = jax.random.uniform(keys[4], (D, 10), jnp.float32, 0.1, 0.5)
    return jnp.concatenate([gain_one[:, None], bias_one[:, None], gain_two[:, None], bias_two[:, None], taps], axis=1)


def draw_seq_lengths(key, part):
    key = jax.random.fold_in(key, 13)
    first, second = jax.random.split(key)
    drawn = jax.random.randint(first, (N_GRP, SEQ_GRP), LEN // 2, LEN + 1)
    chosen = jax.random.randint(second, (N_GRP, 1), 0, SEQ_GRP)
    whole = jnp.arange(SEQ_GRP, dtype=jnp.int32)[None, :] == chosen
    return jnp.where(whole, LEN, drawn).reshape(SEQS).astype(jnp.int32)


def draw_answer_mask(key, part):
    key = jax.random.fold_in(key, 14)
    first, second = jax.random.split(key)
    spans = LEN // 64
    starts = jax.random.randint(first, (SEQS, spans), 0, LEN)
    widths = jax.random.randint(second, (SEQS, spans), 8, 65)
    places = jnp.arange(LEN, dtype=jnp.int32)
    inside = (places[None, :, None] >= starts[:, None, :]) & (places[None, :, None] < starts[:, None, :] + widths[:, None, :])
    return jnp.any(inside, axis=-1).astype(jnp.int32)


def steps_of(rng, dims, shards, smallest, high):
    level = 1.0
    for axis_at, parts in shards:
        draws = jax.random.uniform(jax.random.fold_in(jax.random.fold_in(rng, 6), axis_at), (parts,), jnp.float32, smallest / len(shards), high / len(shards))
        level = level * jnp.repeat(jnp.exp(draws), dims[axis_at] // parts).reshape((-1,) + (1,) * (len(dims) - 1 - axis_at))
    return level


def noise(own_key, shape, scale, most, pieces=(), held_as=jnp.bfloat16):
    values = scale * jax.random.normal(own_key, shape, jnp.float32)
    if pieces:
        values = values * steps_of(own_key, shape, pieces, -0.22, 0.18)
    return jnp.clip(values, -most, most).astype(held_as)


def setup_inputs(seed: int = 0) -> dict:
    seeds = jax.random.split(jax.random.key(seed), 19)
    return {
        "tokens": draw_tokens(jax.random.fold_in(seeds[18], 71), 0),
        "seq_lengths": draw_seq_lengths(jax.random.fold_in(seeds[18], 71), 0),
        "answer_mask": draw_answer_mask(jax.random.fold_in(seeds[18], 71), 0),
        "out_grad": noise(seeds[3], (SEQS, LEN, D), 1.0, 6.0, ((0, 4), (1, 8))),
        "qkv_weight": noise(seeds[4], (D, 3 * D), D ** -0.5, 0.21875, ((0, 32),), jnp.float32),
        "merge_weight": noise(seeds[5], (D, D), (D // 16) ** -0.5, 0.875, ((0, 32),), jnp.float32),
        "expand_weight": noise(seeds[6], (D, FF), D ** -0.5, 0.21875, ((0, 32),), jnp.float32),
        "shrink_weight": noise(seeds[7], (FF, D), FF ** -0.5, 0.109375, ((0, 32),), jnp.float32),
        "small_params": draw_small_params(jax.random.fold_in(seeds[18], 71), 0),
        "qkv_rows": jnp.clip(jnp.exp(math.log(1.410707852755877e-07) - 1.3862944 * jax.random.uniform(seeds[9], (D,), jnp.float32) ** steps_of(seeds[9], (D,), ((0, 32),), -0.2, 0.2)), 3.5267696318896924e-08, 1.410707852755877e-07),
        "qkv_cols": jnp.clip(jnp.exp(jax.random.uniform(seeds[10], (3 * D,), jnp.float32, math.log(3.5267696318896924e-08), math.log(1.410707852755877e-07))), 3.5267696318896924e-08, 1.410707852755877e-07),
        "merge_rows": jnp.clip(jnp.exp(math.log(1.410707852755877e-07) - 1.3862944 * jax.random.uniform(seeds[11], (D,), jnp.float32) ** steps_of(seeds[11], (D,), ((0, 32),), -0.2, 0.2)), 3.5267696318896924e-08, 1.410707852755877e-07),
        "merge_cols": jnp.clip(jnp.exp(jax.random.uniform(seeds[12], (D,), jnp.float32, math.log(3.5267696318896924e-08), math.log(1.410707852755877e-07))), 3.5267696318896924e-08, 1.410707852755877e-07),
        "expand_rows": jnp.clip(jnp.exp(math.log(1.410707852755877e-07) - 1.3862944 * jax.random.uniform(seeds[13], (D,), jnp.float32) ** steps_of(seeds[13], (D,), ((0, 32),), -0.2, 0.2)), 3.5267696318896924e-08, 1.410707852755877e-07),
        "expand_cols": jnp.clip(jnp.exp(jax.random.uniform(seeds[14], (FF,), jnp.float32, math.log(3.5267696318896924e-08), math.log(1.410707852755877e-07))), 3.5267696318896924e-08, 1.410707852755877e-07),
        "shrink_rows": jnp.clip(jnp.exp(math.log(1.410707852755877e-07) - 1.3862944 * jax.random.uniform(seeds[15], (FF,), jnp.float32) ** steps_of(seeds[15], (FF,), ((0, 32),), -0.2, 0.2)), 3.5267696318896924e-08, 1.410707852755877e-07),
        "shrink_cols": jnp.clip(jnp.exp(jax.random.uniform(seeds[16], (D,), jnp.float32, math.log(3.5267696318896924e-08), math.log(1.410707852755877e-07))), 3.5267696318896924e-08, 1.410707852755877e-07),
        "small_moment": jnp.clip(jnp.exp(math.log(1.410707852755877e-07) - 1.3862944 * jax.random.uniform(seeds[17], (D, 14), jnp.float32) ** steps_of(seeds[17], (D, 14), ((0, 32),), -0.2, 0.2)), 3.5267696318896924e-08, 1.410707852755877e-07),
    }


EPS_NORM = 1e-05
EPS_FACTOR = 1e-30
DECAY = 0.5
RATE = 0.08
CLIP = 1.0
NEG = -1e+30
HIGH = lax.Precision.HIGHEST

@jax.custom_vjp
def low(v):
    return lax.optimization_barrier(v.astype(jnp.bfloat16)).astype(jnp.float32)

@jax.custom_vjp
def low_back(v):
    return v

def low_keep(v):
    return (low(v), None)

def low_pass(kept, grad):
    return (grad,)

def back_keep(v):
    return (v, None)

def back_low(kept, grad):
    return (low(grad),)
low.defvjp(low_keep, low_pass)
low_back.defvjp(back_keep, back_low)

def product(left, right):
    return jnp.dot(left, right, precision=HIGH)

def normalize(values):
    centred = values - lax.optimization_barrier(jnp.mean(values, axis=-1, keepdims=True))
    inverse = lax.rsqrt(lax.optimization_barrier(jnp.mean(centred * centred, axis=-1, keepdims=True)) + EPS_NORM)
    return (centred * inverse, inverse)

def pool_rows(window, taps, count):
    shape = (taps.shape[0],) + (1,) * (window.ndim - 2) + (taps.shape[-1],)
    result = taps[:, 0].reshape(shape) * window[..., 0:4 * count:4, :]
    for offset in range(1, 5):
        result = result + taps[:, offset].reshape(shape) * window[..., offset:offset + 4 * count:4, :]
    return result

def window_valid(query_pos, key_start, key_count, lengths, total):
    key_pos = key_start + jnp.arange(key_count, dtype=jnp.int32)
    near = (jnp.abs(query_pos[:, None] - key_pos[None, :]) <= WIN) & (key_pos[None, :] >= 0) & (key_pos[None, :] < total)
    live = (key_pos[None, None, :] < lengths[:, None, None]) | (key_pos[None, :] == query_pos[:, None])[None]
    return near[None] & live

def pooled_valid(query_pos, key_start, key_count, lengths, total):
    key_pos = key_start + jnp.arange(key_count, dtype=jnp.int32)
    coarse = query_pos // 4
    near = (jnp.abs(coarse[:, None] - key_pos[None, :]) <= PWIN) & (key_pos[None, :] >= 0) & (key_pos[None, :] < total // 4)
    live = (4 * key_pos[None, None, :] < lengths[:, None, None]) | (key_pos[None, :] == coarse[:, None])[None]
    return near[None] & live

def softmax_probs(scores, valid):
    masked = jnp.where(valid, scores, NEG)
    top = lax.optimization_barrier(jnp.max(masked, axis=-1, keepdims=True))
    raised = jnp.where(valid, jnp.exp(masked - top), 0.0)
    return raised / lax.optimization_barrier(jnp.sum(raised, axis=-1, keepdims=True))

def attend(query, pair, valid):
    scale = HEAD_DIM ** (-0.5)
    scores = low_back(jnp.einsum('qhd,khd->hqk', query, pair[0], precision=HIGH) * scale)
    probs = low(softmax_probs(scores, valid))
    return jnp.einsum('hqk,khd->qhd', probs, pair[1], precision=HIGH)

def forward_one(tokens, length, params):
    qkv_weight, merge_weight, expand_weight, shrink_weight, small = [low(entry) for entry in params]
    total, width = tokens.shape
    qkv = low(low_back(product(tokens, qkv_weight)))
    query = qkv[:, :width]
    pair = jnp.stack([qkv[:, width:2 * width], qkv[:, 2 * width:]])
    taps = jnp.stack([small[:, 4:9].T, small[:, 9:14].T])
    pooled = low(pool_rows(jnp.pad(pair, ((0, 0), (2, 2), (0, 0))), taps, total // 4))
    near = jnp.pad(pair, ((0, 0), (WIN, WIN), (0, 0)))
    far = jnp.pad(pooled, ((0, 0), (PWIN, PWIN), (0, 0)))
    lengths = length.reshape(1)

    def one_block(index):
        start = index * PIECE
        pool_start = index * (PIECE // 4)
        query_blk = lax.dynamic_slice_in_dim(query, start, PIECE, 0).reshape(PIECE, HEADS, HEAD_DIM)
        pair_blk = lax.dynamic_slice_in_dim(near, start, PIECE + 2 * WIN, 1).reshape(2, PIECE + 2 * WIN, HEADS, HEAD_DIM)
        far_blk = lax.dynamic_slice_in_dim(far, pool_start, PIECE // 4 + 2 * PWIN, 1).reshape(2, PIECE // 4 + 2 * PWIN, HEADS, HEAD_DIM)
        query_pos = start + jnp.arange(PIECE, dtype=jnp.int32)
        near_ok = window_valid(query_pos, start - WIN, PIECE + 2 * WIN, lengths, total)
        far_ok = pooled_valid(query_pos, pool_start - PWIN, PIECE // 4 + 2 * PWIN, lengths, total)
        mixed = attend(query_blk, pair_blk, near_ok) + attend(query_blk, far_blk, far_ok)
        return mixed.reshape(PIECE, width)
    attended = lax.map(jax.checkpoint(one_block), jnp.arange(total // PIECE, dtype=jnp.int32))
    attended = low(low_back(attended.reshape(total, width)))
    mixed = low_back(product(attended, merge_weight))
    first_norm = normalize(tokens + mixed)[0]
    hidden = first_norm * small[:, 0] + small[:, 1]
    up = low_back(product(low(low_back(hidden)), expand_weight))
    active = low(jax.nn.gelu(up, approximate=False))
    branch = low_back(product(active, shrink_weight))
    second_norm = normalize(hidden + branch)[0]
    return second_norm * small[:, 2] + small[:, 3]

def reference(tokens, seq_lengths, answer_mask, out_grad, qkv_weight, merge_weight, expand_weight, shrink_weight, small_params, qkv_rows, qkv_cols, merge_rows, merge_cols, expand_rows, expand_cols, shrink_rows, shrink_cols, small_moment):
    params = (qkv_weight, merge_weight, expand_weight, shrink_weight, small_params)

    def per_sequence(totals, inputs):
        seq_tokens, length, mask, cotangent = inputs

        def run(values, weights):
            return forward_one(values, length, weights)
        outcome, pullback = jax.vjp(run, seq_tokens.astype(jnp.float32), params)
        masked_grad = cotangent.astype(jnp.float32) * mask.astype(jnp.float32)[:, None]
        token_grad, weight_grads = pullback(masked_grad)
        totals = jax.tree.map(lambda left, right: left + right, totals, weight_grads)
        return (totals, (outcome.astype(jnp.bfloat16), token_grad))
    zeros = jax.tree.map(jnp.zeros_like, params)
    grads, outputs = lax.scan(per_sequence, zeros, (tokens, seq_lengths, answer_mask, out_grad))
    block_out, input_grad = outputs
    grad_norm = jnp.sqrt(sum((jnp.sum(entry * entry) for entry in grads)))
    clip = CLIP / jnp.maximum(grad_norm, CLIP)
    clipped = [entry * clip for entry in grads]
    states = ((qkv_rows, qkv_cols), (merge_rows, merge_cols), (expand_rows, expand_cols), (shrink_rows, shrink_cols))
    results = []
    for index in range(4):
        squares = clipped[index] * clipped[index] + EPS_FACTOR
        rows_new = DECAY * states[index][0] + (1.0 - DECAY) * lax.optimization_barrier(jnp.mean(squares, axis=1))
        cols_new = DECAY * states[index][1] + (1.0 - DECAY) * lax.optimization_barrier(jnp.mean(squares, axis=0))
        estimate = rows_new[:, None] * cols_new[None, :] / jnp.mean(rows_new)
        master = params[index] - RATE * clipped[index] * lax.rsqrt(estimate)
        results.append((clipped[index], rows_new, cols_new, master, master.astype(jnp.bfloat16)))
    moment_new = DECAY * small_moment + (1.0 - DECAY) * (clipped[4] * clipped[4] + EPS_FACTOR)
    small_new = small_params - RATE * clipped[4] * lax.rsqrt(moment_new)
    return (block_out, input_grad, grad_norm, results[0][0], results[0][1], results[0][2], results[0][3], results[0][4], results[1][0], results[1][1], results[1][2], results[1][3], results[1][4], results[2][0], results[2][1], results[2][2], results[2][3], results[2][4], results[3][0], results[3][1], results[3][2], results[3][3], results[3][4], clipped[4], moment_new, small_new, small_new.astype(jnp.bfloat16))
```

```python
import functools

import jax
import jax.numpy as jnp
from jax import lax
from jax.experimental import pallas as pl
from jax.experimental.pallas import tpu as pltpu
from jax.sharding import PartitionSpec as P

D = 768
HEAD_DIM = 64
FF = 3072
WIN = 64
PWIN = 64
TILE = 128
LANES = 128
LOW = 272
HIGH = 256
NEAR = TILE + 2 * WIN
FAR = TILE // 4 + 2 * PWIN
GROUPS = D // LANES

EPS_NORM = 1e-05
EPS_FACTOR = 1e-30
DECAY = 0.5
RATE = 0.08
CLIP = 1.0
NEG = -1e30
BIG = 3e38
SCALE = HEAD_DIM ** (-0.5)

TAIL_STEP = 0.31
TAIL = (
    0.12367211422929353,
    0.12367030785161068,
    0.11185922254891491,
    0.08691510254396204,
    0.06423540557821411,
    -0.014525970624111314,
    0.08814037010576171,
    -0.154963171944524,
    0.08860162861073731,
    -0.017604979368020673,
)
INV_ROOT = 0.3989422804014327

F32 = jnp.float32
BF16 = jnp.bfloat16
CUT = 1280
VMEM_LIMIT = 60 * 1024 * 1024


def nn(left, right):
    return jnp.dot(left, right, preferred_element_type=F32)


def nt(left, right):
    return lax.dot_general(left, right, (((1,), (1,)), ((), ())), preferred_element_type=F32)


def outer(left, right):
    return lax.dot_general(left, right, (((0,), (0,)), ((), ())), preferred_element_type=F32)


def from_behind(value, axis, by):
    size = lax.axis_size(axis)
    pairs = [(i, i + by) for i in range(size) if 0 <= i + by < size]
    return lax.ppermute(value, axis, pairs)


def params(**extra):
    return pltpu.CompilerParams(vmem_limit_bytes=VMEM_LIMIT, **extra)


def cost(micros):
    return pl.CostEstimate(flops=int(micros * 8e8), bytes_accessed=0, transcendentals=0)


def fixed(shape):
    zeros = (0,) * len(shape)
    return pl.BlockSpec(shape, lambda *_: zeros, pipeline_mode=pl.Buffered(1))


def lanes_of(index, width=LANES):
    return slice(index * width, (index + 1) * width)


def fill_caps(start, total, length, first, caps):
    key = start - WIN + first + lax.broadcasted_iota(jnp.int32, (NEAR, TILE), 0)
    query = start + first + lax.broadcasted_iota(jnp.int32, (NEAR, TILE), 1)
    near = (jnp.abs(query - key) <= WIN) & (key >= 0) & (key < total)
    cap = jnp.where(near & ((key < length) | (key == query)), BIG, NEG)
    caps[:NEAR, :TILE] = cap
    caps[:NEAR, TILE:] = cap
    pooled = start // 4 - PWIN + first // 4 + lax.broadcasted_iota(jnp.int32, (FAR, TILE), 0)
    coarse = (start + first + lax.broadcasted_iota(jnp.int32, (FAR, TILE), 1)) // 4
    far = (jnp.abs(coarse - pooled) <= PWIN) & (pooled >= 0) & (pooled < total // 4)
    cap = jnp.where(far & ((4 * pooled < length) | (pooled == coarse)), BIG, NEG)
    caps[NEAR:, :TILE] = cap
    caps[NEAR:, TILE:] = cap


def split_pair(pair):
    lane = lax.broadcasted_iota(jnp.int32, pair.shape, 1)
    zero = jnp.zeros_like(pair)
    return jnp.concatenate(
        [jnp.where(lane < HEAD_DIM, pair, zero), jnp.where(lane < HEAD_DIM, zero, pair)], axis=0
    )


LEVELS = ((0, NEAR), (NEAR, NEAR + FAR))


def join_pair(stacked):
    row = lax.broadcasted_iota(jnp.int32, (LANES, TILE), 0)
    return jnp.where(row < HEAD_DIM, stacked[:, :TILE], stacked[:, TILE:])


def attend_kernel(
    info, beside, own, across, weight_a, weight_b, att, query, key, value, pkey, pvalue, lse,
    vectors, wide, caps,
):
    piece = own.shape[1]
    which = pl.program_id(0)
    start, total, length = (info[0], info[1], info[2 + which])
    even = (info[0] // piece) % 2 == 0
    low = jnp.where(even, across[0], beside[0])
    high = jnp.where(even, beside[0, :HIGH], across[0, :HIGH])
    small = weight_b[:, 3 * D - CUT :].astype(F32).T
    vectors[...] = small[:16]
    taps = small[4:14]

    def weight_chunk(chunk):
        if chunk < CUT // 256:
            return weight_a[:, lanes_of(chunk, 256)]
        return weight_b[:, lanes_of(chunk - CUT // 256, 256)]

    for chunk in range(3):
        cols = lanes_of(chunk, 256)
        query[0, :, cols] = (nn(own[0], weight_chunk(chunk)) * SCALE).astype(BF16)
    for chunk in range(6):
        target = key if chunk < 3 else value
        cols = lanes_of(chunk % 3, 256)
        block = weight_chunk(3 + chunk)
        for source, base, count in ((low, 0, LOW), (own[0], LOW, piece), (high, LOW + piece, HIGH)):
            rounded = nn(source, block).astype(BF16)
            held = rounded.astype(F32)
            wide[2 * chunk, base : base + count, :] = held[:, :LANES]
            wide[2 * chunk + 1, base : base + count, :] = held[:, LANES:]
            if base == 0:
                target[0, :WIN, cols] = rounded[LOW - WIN :]
            elif base == LOW:
                target[0, WIN : WIN + piece, cols] = rounded
            else:
                target[0, WIN + piece :, cols] = rounded[:WIN]
    pools = pkey.shape[1]
    lead = LOW - 2 - 4 * PWIN
    for group in range(2 * GROUPS):
        which_taps = 0 if group < GROUPS else 5
        target = pkey if group < GROUPS else pvalue
        cols = lanes_of(group % GROUPS)
        pooled = None
        for tap in range(5):
            term = taps[which_taps + tap : which_taps + tap + 1, cols] * wide[
                group, pl.ds(lead + tap, pools, stride=4), :
            ]
            pooled = term if pooled is None else pooled + term
        target[0, :, cols] = pooled.astype(BF16)

    def tile_step(tile, carry):
        first = pl.multiple_of(tile * TILE, TILE)
        coarse = pl.multiple_of(tile * (TILE // 4), TILE // 4)
        fill_caps(start, total, length, first, caps)
        for pair in range(GROUPS):
            cols = lanes_of(pair)
            queries = split_pair(query[0, pl.ds(first, TILE), cols])
            mixed = None
            for level, (begin, end) in enumerate(LEVELS):
                if level == 0:
                    keys = key[0, pl.ds(first, NEAR), cols]
                    values = value[0, pl.ds(first, NEAR), cols]
                else:
                    keys = pkey[0, pl.ds(coarse, FAR), cols]
                    values = pvalue[0, pl.ds(coarse, FAR), cols]
                row = 2 * pair + level
                probs = []
                for head in range(2):
                    scores = nt(keys, queries[head * TILE : (head + 1) * TILE])
                    scores = jnp.minimum(scores, caps[begin:end, :TILE])
                    top = jnp.max(scores, axis=0, keepdims=True)
                    raised = jnp.exp(scores - top)
                    norm = jnp.sum(raised, axis=0, keepdims=True)
                    lse[0, tile, row : row + 1, lanes_of(head)] = top + jnp.log(norm)
                    probs.append((raised * (1.0 / norm)).astype(BF16))
                part = nn(values.T, jnp.concatenate(probs, axis=1))
                mixed = part if mixed is None else mixed + part
            att[0, pl.ds(first, TILE), cols] = join_pair(mixed).T.astype(BF16)
        return carry

    lax.fori_loop(0, piece // TILE, tile_step, 0)


def attend(info, beside, own, across, weight_a, weight_b):
    seqs, piece, width = own.shape
    pools = piece // 4 + 2 * PWIN
    tiles = piece // TILE
    extent = piece + 2 * WIN

    def seq_block(*shape):
        return pl.BlockSpec((1,) + shape, lambda s: (s,) + (0,) * len(shape))

    def out(shape, dtype):
        return jax.ShapeDtypeStruct((seqs,) + shape, dtype)

    shapes = [
        ((piece, width), BF16),
        ((piece, width), BF16),
        ((extent, width), BF16),
        ((extent, width), BF16),
        ((pools, width), BF16),
        ((pools, width), BF16),
        ((tiles, 16, 2 * TILE), F32),
    ]
    return pl.pallas_call(
        attend_kernel,
        grid=(seqs,),
        in_specs=[
            pl.BlockSpec(memory_space=pltpu.SMEM),
            seq_block(LOW, width),
            seq_block(piece, width),
            seq_block(LOW, width),
            fixed(weight_a.shape),
            fixed(weight_b.shape),
        ],
        out_specs=[seq_block(*shape) for shape, _ in shapes]
        + [pl.BlockSpec((16, width), lambda s: (0, 0))],
        out_shape=[out(shape, dtype) for shape, dtype in shapes]
        + [jax.ShapeDtypeStruct((16, width), F32)],
        scratch_shapes=[
            pltpu.VMEM((2 * GROUPS, LOW + piece + HIGH, LANES), F32),
            pltpu.VMEM((NEAR + FAR, 2 * TILE), F32),
        ],
        compiler_params=params(),
        cost_estimate=cost(29),
        name="attend",
    )(info, beside, own, across, weight_a, weight_b)


def layer_stats(values):
    centred = values - jnp.mean(values, axis=-1, keepdims=True)
    inverse = lax.rsqrt(jnp.mean(centred * centred, axis=-1, keepdims=True) + EPS_NORM)
    return (centred * inverse, inverse)


def layer_back(grad, normed, inverse):
    return inverse * (
        grad
        - jnp.mean(grad, axis=-1, keepdims=True)
        - normed * jnp.mean(grad * normed, axis=-1, keepdims=True)
    )


def gelu_parts(up):
    size = jnp.abs(up)
    bell = jnp.exp(-0.5 * (up * up))
    near = 1.0 / (1.0 + TAIL_STEP * size)
    poly = jnp.full_like(up, TAIL[-1])
    for factor in TAIL[-2::-1]:
        poly = poly * near + factor
    tail = bell * (near * poly)
    phi = jnp.where(up >= 0.0, 1.0 - tail, tail)
    return (up * phi, phi + up * (bell * INV_ROOT))


def feed_kernel(
    tokens, att, cot, packed, vectors, block_out, first_grad, hidden_low, active,
    up_grad, branch_grad, mixed_grad, att_grad, sums, slope,
):
    step = pl.program_id(0)
    gain_one, bias_one, gain_two, bias_two = [vectors[i : i + 1, :] for i in range(4)]
    def merge():
        return packed[:, :D]

    def expand(chunk):
        return packed[:, lanes_of(1 + chunk, D)]

    def shrink(chunk):
        return packed[:, lanes_of(1 + FF // D + chunk, D)]

    first_norm, first_inv = layer_stats(tokens[...].astype(F32) + nn(att[...], merge()))
    hidden = first_norm * gain_one + bias_one
    low = hidden.astype(BF16)
    hidden_low[...] = low
    branch = None
    for chunk in range(FF // D):
        cols = lanes_of(chunk, D)
        wide, steep = gelu_parts(nn(low, expand(chunk)))
        narrow = wide.astype(BF16)
        active[:, cols] = narrow
        slope[:, cols] = steep
        term = nn(narrow, shrink(chunk))
        branch = term if branch is None else branch + term
    second_norm, second_inv = layer_stats(hidden + branch)
    block_out[...] = (second_norm * gain_two + bias_two).astype(BF16)
    cotangent = cot[...].astype(F32)

    @pl.when(step == 0)
    def clear():
        sums[...] = jnp.zeros_like(sums)

    def add_sum(row, value):
        sums[row : row + 1, :] += jnp.sum(value, axis=0, keepdims=True)

    add_sum(2, cotangent * second_norm)
    add_sum(3, cotangent)
    second_grad = layer_back(cotangent * gain_two, second_norm, second_inv)
    second_low = second_grad.astype(BF16)
    branch_grad[...] = second_low
    feed = None
    for chunk in range(FF // D):
        cols = lanes_of(chunk, D)
        narrow = (nt(second_low, shrink(chunk)) * slope[:, cols]).astype(BF16)
        up_grad[:, cols] = narrow
        term = nt(narrow, expand(chunk))
        feed = term if feed is None else feed + term
    hidden_grad = second_grad + feed.astype(BF16).astype(F32)
    add_sum(0, hidden_grad * first_norm)
    add_sum(1, hidden_grad)
    grad = layer_back(hidden_grad * gain_one, first_norm, first_inv)
    first_grad[...] = grad
    grad_low = grad.astype(BF16)
    mixed_grad[...] = grad_low
    att_grad[...] = nt(grad_low, merge()).astype(BF16)


def feed(tokens, att, cot, packed, vectors):
    rows, width = tokens.shape
    block = 256
    ff = FF

    def row_block(cols):
        return pl.BlockSpec((block, cols), lambda i: (i, 0))

    outs = [
        (width, BF16),
        (width, F32),
        (width, BF16),
        (ff, BF16),
        (ff, BF16),
        (width, BF16),
        (width, BF16),
        (width, BF16),
    ]
    return pl.pallas_call(
        feed_kernel,
        grid=(rows // block,),
        in_specs=[row_block(width)] * 3
        + [fixed(packed.shape), fixed(vectors.shape)],
        out_specs=[row_block(cols) for cols, _ in outs] + [pl.BlockSpec((8, width), lambda i: (0, 0))],
        out_shape=[jax.ShapeDtypeStruct((rows, cols), dtype) for cols, dtype in outs]
        + [jax.ShapeDtypeStruct((8, width), F32)],
        scratch_shapes=[pltpu.VMEM((block, ff), F32)],
        compiler_params=params(),
        cost_estimate=cost(48),
        name="feed",
    )(tokens, att, cot, packed, vectors)


def back_kernel(
    which, info, query, key, value, pkey, pvalue, grad, lse, query_grad, near_grad,
    far_grad, rim_near, rim_across, caps,
):
    piece = query.shape[1]
    even = (info[0] // piece) % 2 == 0
    start, total, length = (info[0], info[1], info[2 + which])
    near_grad[...] = jnp.zeros_like(near_grad)
    far_grad[...] = jnp.zeros_like(far_grad)

    def tile_step(tile, carry):
        first = pl.multiple_of(tile * TILE, TILE)
        coarse = pl.multiple_of(tile * (TILE // 4), TILE // 4)
        fill_caps(start, total, length, first, caps)
        for pair in range(GROUPS):
            cols = lanes_of(pair)
            near_rows, far_rows = (pl.ds(first, NEAR), pl.ds(coarse, FAR))
            queries = split_pair(query[0, pl.ds(first, TILE), cols])
            grads = split_pair(grad[0, pl.ds(first, TILE), cols])
            keys = jnp.concatenate([key[0, near_rows, cols], pkey[0, far_rows, cols]], axis=0)
            values = jnp.concatenate([value[0, near_rows, cols], pvalue[0, far_rows, cols]], axis=0)
            scores = nt(keys, queries)
            prob_grad = nt(values, grads)
            probs = []
            score_grads = []
            for level, (begin, end) in enumerate(LEVELS):
                row = 2 * pair + level
                capped = jnp.minimum(scores[begin:end], caps[begin:end, :])
                prob = jnp.exp(capped - lse[0, tile, row : row + 1, :])
                weighted = prob * prob_grad[begin:end]
                inner = jnp.sum(weighted, axis=0, keepdims=True)
                score_grads.append((weighted - prob * inner).astype(BF16))
                probs.append(prob.astype(BF16))
            score_grad = jnp.concatenate(score_grads, axis=0)
            key_part = nn(score_grad, queries)
            value_part = nn(jnp.concatenate(probs, axis=0), grads)
            near_grad[0, 0, near_rows, cols] += key_part[:NEAR]
            far_grad[0, 0, far_rows, cols] += key_part[NEAR:]
            near_grad[0, 1, near_rows, cols] += value_part[:NEAR]
            far_grad[0, 1, far_rows, cols] += value_part[NEAR:]
            total_query = nn(keys.T, score_grad)
            query_grad[0, pl.ds(first, TILE), cols] = (
                (join_pair(total_query) * SCALE).T.astype(BF16)
            )
        return carry

    lax.fori_loop(0, piece // TILE, tile_step, 0)
    pools = far_grad.shape[2]
    blank = jnp.zeros((16, far_grad.shape[3]), BF16)
    for part in range(2):
        low = [near_grad[0, part, :WIN, :], far_grad[0, part, : PWIN + 16, :]]
        low = [entry.astype(BF16) for entry in low]
        high = [near_grad[0, part, WIN + piece :, :], far_grad[0, part, pools - PWIN :, :]]
        high = [entry.astype(BF16) for entry in high]

        @pl.when(even)
        def even_side():
            rim_near[0, part, :WIN, :] = high[0]
            rim_near[0, part, WIN : WIN + PWIN, :] = high[1]
            rim_near[0, part, WIN + PWIN :, :] = blank
            rim_across[0, part, :WIN, :] = low[0]
            rim_across[0, part, WIN:, :] = low[1]

        @pl.when(jnp.logical_not(even))
        def odd_side():
            rim_across[0, part, :WIN, :] = high[0]
            rim_across[0, part, WIN : WIN + PWIN, :] = high[1]
            rim_across[0, part, WIN + PWIN :, :] = blank
            rim_near[0, part, :WIN, :] = low[0]
            rim_near[0, part, WIN:, :] = low[1]


def seq_slice(shape, which):
    return pl.BlockSpec((1,) + tuple(shape[1:]), lambda _: (which,) + (0,) * (len(shape) - 1))


def back(which, info, query, key, value, pkey, pvalue, grad, lse):
    _, piece, width = query.shape
    extent, pools = (key.shape[1], pkey.shape[1])
    operands = (query, key, value, pkey, pvalue, grad, lse)
    shapes = [
        ((1, piece, width), BF16),
        ((1, 2, extent, width), F32),
        ((1, 2, pools, width), F32),
        ((1, 2, WIN + PWIN + 16, width), BF16),
        ((1, 2, WIN + PWIN + 16, width), BF16),
    ]
    return pl.pallas_call(
        functools.partial(back_kernel, which),
        grid=(1,),
        in_specs=[pl.BlockSpec(memory_space=pltpu.SMEM)]
        + [seq_slice(entry.shape, which) for entry in operands],
        out_specs=[seq_slice(shape, 0) for shape, _ in shapes],
        out_shape=[jax.ShapeDtypeStruct(shape, dtype) for shape, dtype in shapes],
        scratch_shapes=[pltpu.VMEM((NEAR + FAR, 2 * TILE), F32)],
        compiler_params=params(),
        cost_estimate=cost(0.01 if which else 30),
        name="back",
    )(info, *operands)


def pool_back_kernel(
    first, last, info, query_grad, near_grad, far_grad, beside, across, key, value, taps, turned, *rest
):
    rest = list(rest)
    before, taps_before = (None, None) if first else (rest.pop(0), rest.pop(0))
    sums = rest.pop(0) if last else None
    full_grad = rest.pop(0)
    outs = [rest.pop(0), rest.pop(0)]
    held, spread, window, taps_grad = rest
    piece = full_grad.shape[1]
    pools = piece // 4
    even = (info[0] // piece) % 2 == 0
    full_grad[0, :, :D] = query_grad[0]
    if first:
        taps_grad[...] = jnp.zeros_like(taps_grad)
    else:
        taps_grad[...] = taps_before[...]

    def product(chunk):
        cols = lanes_of(chunk, 256)
        total = nn(turned[...], full_grad[0, :, cols])
        if not first:
            total = total + before[:, cols]
        if not last:
            outs[0][:, cols] = total
        elif chunk < CUT // 256:
            outs[0][:, cols] = total.astype(BF16)
        else:
            outs[1][:, lanes_of(chunk - CUT // 256, 256)] = total.astype(BF16)

    for group in range(2 * GROUPS):
        if group % 4 == 0:
            product(group // 4)
        part = group // GROUPS
        cols = lanes_of(group % GROUPS)
        source = key if part == 0 else value
        pair = [entry[0, part, :, cols].astype(F32) for entry in (beside, across)]
        from_high = jnp.where(even, pair[0], pair[1])
        from_low = jnp.where(even, pair[1], pair[0])
        tap = [taps[4 + 5 * part + t : 5 + 5 * part + t, cols] for t in range(5)]
        held[0:pools, :] = far_grad[0, part, PWIN : PWIN + pools, cols]
        held[0:PWIN, :] += from_low[WIN : WIN + PWIN]
        held[pools - PWIN : pools, :] += from_high[WIN : WIN + PWIN]
        held[pools : pools + 16, :] = (
            far_grad[0, part, PWIN + pools : PWIN + pools + 16, cols] + from_high[WIN + PWIN :]
        )
        now = held[0:pools, :]
        later = held[1 : pools + 1, :]
        spread[pl.ds(0, pools, stride=4), :] = tap[2] * now
        spread[pl.ds(1, pools, stride=4), :] = tap[3] * now
        spread[pl.ds(2, pools, stride=4), :] = tap[4] * now + tap[0] * later
        spread[pl.ds(3, pools, stride=4), :] = tap[1] * later
        spread[0:WIN, :] += from_low[:WIN]
        spread[piece - WIN : piece, :] += from_high[:WIN]
        total = near_grad[0, part, WIN : WIN + piece, cols] + spread[...]
        full_grad[0, :, lanes_of(GROUPS + group)] = total.astype(BF16)
        window[...] = source[0, WIN - 16 : WIN + piece + 16, cols].astype(F32)
        for t in range(5):
            row = 5 * part + t
            taps_grad[row : row + 1, cols] += jnp.sum(
                now * window[pl.ds(14 + t, pools, stride=4), :], axis=0, keepdims=True
            )
        if group % 2 == 1:
            product((GROUPS + group) // 2)
    if last:
        zeros = jnp.zeros((LANES - 14, D), F32)
        small = jnp.concatenate([sums[0:4, :], taps_grad[0:10, :], zeros], axis=0)
        outs[1][:, 3 * D - CUT :] = small.T.astype(BF16)
    else:
        outs[1][...] = taps_grad[...]


def pool_back(which, seqs, info, entries, key, value, taps, turned, before, sums):
    near_grad = entries[1]
    _, _, extent, width = near_grad.shape
    piece = extent - 2 * WIN
    pools = piece // 4
    first, last = (which == 0, which == seqs - 1)
    extra = (() if first else tuple(before)) + ((sums,) if last else ())
    if last:
        outs = [((width, CUT), BF16), ((width, 3 * width + LANES - CUT), BF16)]
    else:
        outs = [((width, 3 * width), F32), ((16, width), F32)]
    return pl.pallas_call(
        functools.partial(pool_back_kernel, first, last),
        grid=(1,),
        in_specs=[pl.BlockSpec(memory_space=pltpu.SMEM)]
        + [seq_slice(entry.shape, 0) for entry in entries]
        + [seq_slice(entry.shape, which) for entry in (key, value)]
        + [fixed(taps.shape), pl.BlockSpec((width, piece), lambda _: (0, which))]
        + [fixed(entry.shape) for entry in extra],
        out_specs=[seq_slice((1, piece, 3 * width), 0)] + [fixed(shape) for shape, _ in outs],
        out_shape=[jax.ShapeDtypeStruct((1, piece, 3 * width), BF16)]
        + [jax.ShapeDtypeStruct(shape, dtype) for shape, dtype in outs],
        scratch_shapes=[
            pltpu.VMEM((pools + 16, LANES), F32),
            pltpu.VMEM((piece, LANES), F32),
            pltpu.VMEM((piece + 32, LANES), F32),
            pltpu.VMEM((16, width), F32),
        ],
        compiler_params=params(),
        cost_estimate=cost(0.01 if which else 30),
        name="pool_back",
    )(info, *entries, key, value, taps, turned, *extra)


def unmix(width):
    row = lax.broadcasted_iota(jnp.int32, (4 * width, 4 * width), 0)
    col = lax.broadcasted_iota(jnp.int32, (4 * width, 4 * width), 1)
    return jnp.where(row == 4 * (col % width) + col // width, 1.0, 0.0)


def exact(left, right):
    return jnp.dot(left, right, precision=lax.Precision.HIGHEST, preferred_element_type=F32)


def exact_nt(left, right):
    return lax.dot_general(
        left, right, (((1,), (1,)), ((), ())), precision=lax.Precision.HIGHEST, preferred_element_type=F32
    )


def pack_kernel(merge, expand, shrink, out, held):
    rows = merge.shape[0]
    mixer = unmix(LANES).astype(BF16)
    out[:, :D] = merge[...].astype(BF16)
    for group in range(FF // (4 * LANES)):
        block = nn(expand[:, lanes_of(group, 4 * LANES)].astype(BF16), mixer).astype(BF16)
        for j in range(4):
            first = D + j * D + group * LANES
            out[:, first : first + LANES] = block[:, lanes_of(j)]
    for group in range(GROUPS):
        held[group] = shrink[:, lanes_of(group)]
        for j in range(4):
            first = (5 + j) * D + group * LANES
            out[:, first : first + LANES] = held[group, pl.ds(j, rows, stride=4), :].astype(BF16)


def squares(block):
    return jnp.sum(block * block, axis=0, keepdims=True)


def late_kernel(expand_in, late, *rest):
    olds, (out, expand, shrink, held) = (rest[:4], rest[4:])
    rows = expand_in.shape[0]
    mixer = unmix(LANES).astype(BF16)
    for group in range(FF // (4 * LANES)):
        pieces = []
        for j in range(4):
            first = j * D + group * LANES
            pieces.append(expand_in[:, first : first + LANES])
        left = jnp.concatenate(pieces, axis=1)
        total = None
        for _ in range(3):
            top = left.astype(BF16)
            left = left - top.astype(F32)
            term = nt(top, mixer)
            total = term if total is None else total + term
        expand[:, lanes_of(group, 4 * LANES)] = total
    for group in range(GROUPS):
        for j in range(4):
            held[group, pl.ds(j, rows, stride=4), :] = late[j, :, lanes_of(group)]
        shrink[:, lanes_of(group)] = held[group]
    out[:, : 3 * D] = jnp.zeros((1, 3 * D), F32)
    out[:, 3 * D : 4 * D] = squares(late[4])
    for j in range(FF // D):
        out[:, (4 + j) * D : (5 + j) * D] = squares(expand[:, lanes_of(j, D)])
    out[:, 8 * D : 9 * D] = squares(shrink[...])
    lane = lax.broadcasted_iota(jnp.int32, (1, LANES), 1)
    tail = jnp.zeros((1, LANES), F32)
    for slot, entry in enumerate(olds):
        tail = jnp.where(lane == slot + 1, jnp.sum(entry[...], axis=1, keepdims=True), tail)
    out[:, 9 * D :] = tail


def stats_kernel(early, base, out):
    out[:, : 3 * D] = squares(early[:, : 3 * D])
    out[:, 3 * D : 9 * D] = base[:, 3 * D : 9 * D]
    lane = lax.broadcasted_iota(jnp.int32, (1, LANES), 1)
    small = jnp.sum(squares(early[:, 3 * D :]), axis=1, keepdims=True)
    out[:, 9 * D :] = base[:, 9 * D :] + jnp.where(lane == 0, small, 0.0)


def update_kernel(
    total, early, late, expand, shrink, rows_0, rows_1, rows_2, rows_3, cols_0, cols_1,
    cols_2, cols_3, weight_0, weight_1, weight_2, weight_3, small, moment,
    norm_out, grad_0, rows_new_0, cols_new_0, new_0, low_0, grad_1, rows_new_1, cols_new_1, new_1,
    low_1, grad_2, rows_new_2, cols_new_2, new_2, low_2, grad_3, rows_new_3, cols_new_3, new_3,
    low_3, small_grad, moment_new, small_new, small_low,
):
    smalls = small.shape[0]
    tail = total[:, 9 * D :]
    spans = ((0, 3 * D), (3 * D, 4 * D), (4 * D, 8 * D), (8 * D, 9 * D))
    matrix_sums = [jnp.sum(total[:, a:b], axis=1, keepdims=True) for a, b in spans]
    norm = jnp.sqrt(matrix_sums[0] + matrix_sums[1] + matrix_sums[2] + matrix_sums[3] + tail[:, 0:1])
    clip = CLIP / jnp.maximum(norm, CLIP)
    norm_out[...] = norm
    parts = (
        [early[:, lanes_of(j, D)] for j in range(3)],
        [late[4]],
        [expand[:, lanes_of(j, D)] for j in range(FF // D)],
        [shrink[...]],
    )
    heights = (D, D, D, FF)
    olds = (
        (rows_0, cols_0, weight_0, grad_0, rows_new_0, cols_new_0, new_0, low_0),
        (rows_1, cols_1, weight_1, grad_1, rows_new_1, cols_new_1, new_1, low_1),
        (rows_2, cols_2, weight_2, grad_2, rows_new_2, cols_new_2, new_2, low_2),
        (rows_3, cols_3, weight_3, grad_3, rows_new_3, cols_new_3, new_3, low_3),
    )
    for index in range(4):
        old_rows, old_cols, weight, grad, rows_new, cols_new, new, low = olds[index]
        begin, end = spans[index]
        width, height = (end - begin, heights[index])
        mean_cols = (total[:, begin:end] * clip) * clip / height + EPS_FACTOR
        fresh_cols = DECAY * old_cols[...] + (1.0 - DECAY) * mean_cols
        for group in range(width // LANES):
            cols_new[group : group + 1, :] = fresh_cols[:, lanes_of(group)]
        squared = sum(part * part for part in parts[index])
        row_sum = exact_nt(jnp.ones((8, D), F32), squared)[:1]
        mean_rows = (row_sum * clip) * clip / width + EPS_FACTOR
        fresh_rows = DECAY * old_rows[...] + (1.0 - DECAY) * mean_rows
        rows_new[...] = fresh_rows
        row = lax.broadcasted_iota(jnp.int32, (weight.shape[0], weight.shape[0]), 0)
        col = lax.broadcasted_iota(jnp.int32, (weight.shape[0], weight.shape[0]), 1)
        down = jnp.sum(jnp.where(row == col, fresh_rows, 0.0), axis=1, keepdims=True)
        mean_all = (matrix_sums[index] * clip) * clip / (width * height) + EPS_FACTOR
        row_mean = DECAY * (tail[:, 1 + index : 2 + index] / height) + (1.0 - DECAY) * mean_all
        for j, part in enumerate(parts[index]):
            cols = lanes_of(j, D)
            clipped = part * clip
            grad[:, cols] = clipped
            estimate = down * fresh_cols[:, cols] / row_mean
            fresh = weight[:, cols] - RATE * clipped * lax.rsqrt(estimate)
            new[:, cols] = fresh
            low[:, cols] = fresh.astype(BF16)
    row = lax.broadcasted_iota(jnp.int32, (16, LANES), 0)
    col = lax.broadcasted_iota(jnp.int32, (16, LANES), 1)
    turned = exact_nt(jnp.where(row == col, 1.0, 0.0), early[:, 3 * D :])
    clipped = turned[:smalls] * clip
    small_grad[...] = clipped
    fresh_moment = DECAY * moment[...] + (1.0 - DECAY) * (clipped * clipped + EPS_FACTOR)
    moment_new[...] = fresh_moment
    fresh = small[...] - RATE * clipped * lax.rsqrt(fresh_moment)
    small_new[...] = fresh
    small_low[...] = fresh.astype(BF16)


def whole_call(body, outs, operands, name, micros, scratch=()):
    return pl.pallas_call(
        body,
        out_shape=[jax.ShapeDtypeStruct(shape, dtype) for shape, dtype in outs],
        in_specs=[pl.BlockSpec(memory_space=pltpu.VMEM)] * len(operands),
        out_specs=[pl.BlockSpec(memory_space=pltpu.VMEM)] * len(outs),
        scratch_shapes=list(scratch),
        compiler_params=params(),
        cost_estimate=cost(micros),
        name=name,
    )(*operands)


def swap(value, axis, bit):
    size = lax.axis_size(axis)
    return lax.ppermute(value, axis, [(i, i ^ (1 << bit)) for i in range(size)])


def bits_of(axis):
    return lax.axis_size(axis).bit_length() - 1


def side(axis, bit):
    return (lax.axis_index(axis) >> bit) & 1


def doubled(value, axis, bit, dim):
    other = swap(value, axis, bit)
    mine = side(axis, bit)
    return jnp.where(
        mine == 0, jnp.stack([value, other], axis=dim), jnp.stack([other, value], axis=dim)
    )


def halves(value, axis, bit, dim):
    mine = side(axis, bit)
    away = lax.dynamic_index_in_dim(value, 1 - mine, dim, keepdims=False)
    return [lax.dynamic_index_in_dim(value, mine, dim, keepdims=False), swap(away, axis, bit)]


def quarters(value, axis, bit, dim):
    size = lax.axis_size(axis)
    mine = (lax.axis_index(axis) >> bit) & 3
    value = value.reshape(value.shape[:dim] + (4,) + value.shape[dim + 2 :])
    blocks = [lax.dynamic_index_in_dim(value, mine, dim, keepdims=False)]
    for step in range(1, 4):
        away = lax.dynamic_index_in_dim(value, mine ^ step, dim, keepdims=False)
        blocks.append(lax.ppermute(away, axis, [(i, i ^ (step << bit)) for i in range(size)]))
    return blocks


def added(blocks, dtype):
    return sum(block.astype(F32) for block in blocks).astype(dtype)


def place_of(done, step):
    return sum(1 for other in done if other > step)


def order_key(axis, bit):
    return (1 if axis == "seq" else 0, bit)


def gather_pairs(value, steps):
    done = []
    for axis, bit in steps:
        at = order_key(axis, bit)
        value = doubled(value, axis, bit, place_of(done, at))
        done.append(at)
    return (value, done)


def scatter_begin(value, steps, lead=0):
    left = [(axis, bit + k) for axis, bit, count in steps for k in range(count)]
    left = sorted((order_key(axis, bit) for axis, bit in left), reverse=True)
    value = value.reshape(value.shape[:lead] + (2,) * len(left) + value.shape[lead + 1 :])
    return (value, left, list(steps), lead)


def scatter_step(state, gate=None):
    value, left, steps, lead = state
    axis, bit, count = steps[0]
    gone = [order_key(axis, bit + k) for k in range(count)]
    dtype = F32 if len(steps) == 1 else BF16
    dim = lead + min(left.index(entry) for entry in gone)
    blocks = (halves if count == 1 else quarters)(value, axis, bit, dim)
    if gate is not None:
        blocks, _ = lax.optimization_barrier((blocks, gate))
    value = added(blocks, dtype)
    return (value, [other for other in left if other not in gone], steps[1:], lead)


def scatter_end(state, gate=None):
    while state[2]:
        state = scatter_step(state, gate)
    return state[0]


def after(states, values):
    blocks, values = lax.optimization_barrier(([state[0] for state in states], values))
    return ([(block,) + tuple(state[1:]) for block, state in zip(blocks, states)], values)


def gather_far(shard):
    steps = [("seq", bit) for bit in reversed(range(1, bits_of("seq")))]
    return gather_pairs(shard, steps)


def gather_near(part, done, first):
    side_bits = [("grp", bit) for bit in range(1, bits_of("grp"))]
    middle = [("seq", 0)] + side_bits if first == "seq" else side_bits + [("seq", 0)]
    done = list(done)
    for axis, bit in middle + [("grp", 0)]:
        at = order_key(axis, bit)
        part = doubled(part, axis, bit, place_of(done, at))
        done.append(at)
    return part.reshape(-1, part.shape[-1])


def near_swap(even, odd):
    mine = side("seq", 0)
    return swap(jnp.where(mine == 0, even, odd), "seq", 0)


def across_swap(value):
    size = lax.axis_size("seq")
    pairs = [(i, i - 1 if i % 2 == 0 else i + 1) for i in range(size)]
    return lax.ppermute(value, "seq", [(i, j) for i, j in pairs if 0 <= j < size])


def diagonal_swap(even, odd):
    return across_swap(jnp.where(side("seq", 0) == 0, even, odd))


def scatter_steps(first, most=2, far_first=False):
    count = bits_of("seq")
    far_bits = [("seq", bit, min(most, count - bit)) for bit in range(1, count, most)]
    side_bits = [("grp", bit, 1) for bit in range(1, bits_of("grp"))]
    middle = [("seq", 0, 1)] + side_bits if first == "seq" else side_bits + [("seq", 0, 1)]
    if far_first:
        return [("grp", 0, 1)] + far_bits + middle
    return [("grp", 0, 1)] + middle + far_bits


def summed_all(value):
    for axis in ("grp", "seq"):
        count, size = (bits_of(axis), lax.axis_size(axis))
        for bit in range(0, count, 2):
            others = [
                lax.ppermute(value, axis, [(i, i ^ (step << bit)) for i in range(size)])
                for step in range(1, 4 if bit + 1 < count else 2)
            ]
            value = value + others[0]
            if len(others) == 3:
                value = value + (others[1] + others[2])
    return value


def local(
    tokens,
    seq_lengths,
    answer_mask,
    out_grad,
    qkv_weight,
    merge_weight,
    expand_weight,
    shrink_weight,
    small_params,
    qkv_rows,
    qkv_cols,
    merge_rows,
    merge_cols,
    expand_rows,
    expand_cols,
    shrink_rows,
    shrink_cols,
    small_moment,
):
    seqs, piece, width = tokens.shape
    axes = ("seq", "grp")
    devices = lax.axis_size("seq") * lax.axis_size("grp")
    rows = qkv_weight.shape[0]
    ff_rows = shrink_weight.shape[0]
    chunks = FF // D
    total = piece * lax.axis_size("seq")
    start = lax.axis_index("seq") * piece
    info = jnp.concatenate(
        [jnp.stack([start, jnp.int32(total)]).astype(jnp.int32), seq_lengths.astype(jnp.int32)]
    )
    smalls = small_params.shape[1]

    packed = whole_call(
        pack_kernel,
        [((rows, 9 * D), BF16)],
        (merge_weight, expand_weight, shrink_weight),
        "pack",
        2,
        [pltpu.VMEM((GROUPS, ff_rows, LANES), F32)],
    )[0]
    packed = lax.all_gather(packed, axes, axis=0, tiled=True)
    early = jnp.concatenate(
        [qkv_weight.astype(BF16), jnp.pad(small_params.astype(BF16), ((0, 0), (0, LANES - smalls)))],
        axis=1,
    )
    last = tokens[:, piece - LOW :]
    ahead = jnp.pad(tokens[:, :HIGH], ((0, 0), (0, LOW - HIGH), (0, 0)))
    beside = near_swap(last, ahead)
    early, done = gather_far(early)
    last, ahead, early = lax.optimization_barrier((last, ahead, early))
    across = diagonal_swap(ahead, last)
    weight_a = gather_near(early[..., :CUT], done, "grp")
    weight_b = gather_near(early[..., CUT:], done, "seq")
    flat = tokens.reshape(seqs * piece, width)
    cot = (out_grad * answer_mask[:, :, None].astype(BF16)).reshape(seqs * piece, width)

    turned = flat.T
    turned, info = lax.optimization_barrier((turned, info))
    att, query, key, value, pkey, pvalue, lse, vectors = attend(
        info, beside, tokens, across, weight_a, weight_b
    )
    att_flat = att.reshape(seqs * piece, width)
    (
        block_out, first_grad, hidden_low, active, up_grad, branch_grad, mixed_grad, att_grad, sums,
    ) = feed(flat, att_flat, cot, packed, vectors)

    shrink_local = outer(active, branch_grad).astype(BF16).reshape(chunks, devices, rows, D)
    merge_local = outer(att_flat, mixed_grad).astype(BF16).reshape(1, devices, rows, D)
    shrink_local, merge_local, up_grad = lax.optimization_barrier((shrink_local, merge_local, up_grad))
    shrink_chain = scatter_step(scatter_begin(shrink_local, scatter_steps("grp", 1), 1))
    merge_chain = scatter_step(scatter_begin(merge_local, scatter_steps("grp", 1), 1))
    late_chain = (jnp.concatenate([shrink_chain[0], merge_chain[0]], axis=0),) + shrink_chain[1:]
    expand_local = outer(hidden_low, up_grad).astype(BF16).reshape(devices, rows, FF)
    expand_chain = scatter_begin(expand_local, scatter_steps("seq", 1, True))
    chains = [late_chain, scatter_step(expand_chain)]

    def seq_rows(value, which):
        return value[which * piece : (which + 1) * piece]

    def advance(states, gate):
        return [scatter_step(state, gate) if len(state[2]) > 1 else state for state in states]

    att_grad = att_grad.reshape(seqs, piece, width)
    chains, info = after(chains, info)
    full_parts, parts, rims = ([], [], [])
    for which in range(seqs):
        parts.append(back(which, info, query, key, value, pkey, pvalue, att_grad, lse))
        info, _ = lax.optimization_barrier((info, parts[which][0]))
    for which in range(seqs):
        query_part, near_grad, far_grad, rim_near, rim_across = parts[which]
        if which:
            rim_near, rim_across, _ = lax.optimization_barrier((rim_near, rim_across, rims[which - 1][3:]))
        rims.append((query_part, near_grad, far_grad, swap(rim_near, "seq", 0), across_swap(rim_across)))
    chains = advance(chains, parts[-1][0])
    chains, vectors = after(chains, vectors)
    before = None
    for which in range(seqs):
        full_part, *before = pool_back(
            which, seqs, info, rims[which], key, value, vectors, turned, before, sums
        )
        full_parts.append(full_part.reshape(piece, 3 * width))
    chains = advance(chains, None)
    chains, before = after(chains, before)
    gate = [state[0] for state in chains]
    early_chains = [
        scatter_step(scatter_begin(entry.reshape(devices, rows, -1), scatter_steps(first)), gate)
        for entry, first in zip(before, ("seq", "grp"))
    ]
    for _ in range(bits_of("grp")):
        chains = advance(chains, early_chains[0][0])
        gate = [state[0] for state in chains]
        early_chains = [scatter_step(state, gate) for state in early_chains]
    early_chain = (
        jnp.concatenate([state[0] for state in early_chains], axis=-1),
    ) + early_chains[0][1:]
    late_sum, expand_in = [scatter_end(state, early_chain[0]) for state in chains]
    early_sum = scatter_end(early_chain)
    full_parts, _ = lax.optimization_barrier((full_parts, early_chain[0]))
    input_grad = jnp.stack(
        [
            seq_rows(first_grad, which)
            + nt(full_parts[which][:, :CUT], weight_a)
            + nt(full_parts[which][:, CUT:], weight_b[:, : 3 * D - CUT])
            for which in range(seqs)
        ]
    )

    old_rows = [entry[None, :] for entry in (qkv_rows, merge_rows, expand_rows, shrink_rows)]
    old_cols = [entry[None, :] for entry in (qkv_cols, merge_cols, expand_cols, shrink_cols)]
    masters = (qkv_weight, merge_weight, expand_weight, shrink_weight)
    base, expand_sum, shrink_sum = whole_call(
        late_kernel,
        [((1, 9 * D + LANES), F32), ((rows, FF), F32), ((ff_rows, D), F32)],
        (expand_in, late_sum) + tuple(old_rows),
        "late_stats",
        3,
        [pltpu.VMEM((GROUPS, ff_rows, LANES), F32)],
    )
    payload = whole_call(
        stats_kernel, [((1, 9 * D + LANES), F32)], (early_sum, base), "stats", 1
    )[0]
    payload = summed_all(payload)
    outs = [((1, 1), F32)]
    for master in masters:
        high, wide = master.shape
        outs += [((high, wide), F32), ((1, high), F32), ((wide // LANES, LANES), F32), ((high, wide), F32)]
        outs += [((high, wide), BF16)]
    outs += [((smalls, rows), F32)] * 3 + [((smalls, rows), BF16)]
    fresh = whole_call(
        update_kernel,
        outs,
        (payload, early_sum, late_sum, expand_sum, shrink_sum)
        + tuple(old_rows)
        + tuple(old_cols)
        + masters
        + (small_params.T, small_moment.T),
        "update",
        5,
    )
    results = []
    for index in range(4):
        grad, rows_new, cols_new, new, low_new = fresh[1 + 5 * index : 6 + 5 * index]
        results += [grad, rows_new.reshape(-1), cols_new.reshape(-1), new, low_new]
    return (
        block_out.reshape(seqs, piece, width),
        input_grad,
        fresh[0].reshape(()),
        *results,
        *[entry.T for entry in fresh[21:]],
    )


def solution(mesh):
    whole = ("seq", "grp")
    matrix = P(whole, None)
    vector = P(whole)
    in_specs = (
        P("grp", "seq", None),
        P("grp"),
        P("grp", "seq"),
        P("grp", "seq", None),
        *[matrix] * 5,
        *[vector, P()] * 4,
        matrix,
    )
    out_specs = (
        P("grp", "seq", None),
        P("grp", "seq", None),
        P(),
        *[matrix, vector, P(), matrix, matrix] * 4,
        *[matrix] * 4,
    )
    return jax.shard_map(local, mesh=mesh, in_specs=in_specs, out_specs=out_specs, check_vma=False)
```

```python
import functools

import jax
import jax.numpy as jnp
from jax import lax
from jax.experimental import pallas as pl
from jax.experimental.pallas import tpu as pltpu
from jax.sharding import PartitionSpec as P

D = 768
HEAD_DIM = 64
FF = 3072
WIN = 64
PWIN = 64
TILE = 128
LANES = 128
NEAR = TILE + 2 * WIN
FAR = TILE // 4 + 2 * PWIN
GROUPS = D // LANES

EPS_NORM = 1e-05
EPS_FACTOR = 1e-30
DECAY = 0.5
RATE = 0.08
CLIP = 1.0
NEG = -1e30
BIG = 3e38
SCALE = HEAD_DIM ** (-0.5)

TAIL_STEP = 0.31
TAIL = (
    0.12367211422929353,
    0.12367030785161068,
    0.11185922254891491,
    0.08691510254396204,
    0.06423540557821411,
    -0.014525970624111314,
    0.08814037010576171,
    -0.154963171944524,
    0.08860162861073731,
    -0.017604979368020673,
)
INV_ROOT = 0.3989422804014327

F32 = jnp.float32
BF16 = jnp.bfloat16
CUT = 1280
TOGETHER = 3
BACK_TOGETHER = 2
VMEM_LIMIT = 60 * 1024 * 1024


def nn(left, right):
    return jnp.dot(left, right, preferred_element_type=F32)


def nt(left, right):
    return lax.dot_general(left, right, (((1,), (1,)), ((), ())), preferred_element_type=F32)


def outer(left, right):
    return lax.dot_general(left, right, (((0,), (0,)), ((), ())), preferred_element_type=F32)


def from_behind(value, axis, by):
    size = lax.axis_size(axis)
    pairs = [(i, i + by) for i in range(size) if 0 <= i + by < size]
    return lax.ppermute(value, axis, pairs)


def params(**extra):
    return pltpu.CompilerParams(vmem_limit_bytes=VMEM_LIMIT, **extra)


def cost(micros):
    return pl.CostEstimate(flops=int(micros * 8e8), bytes_accessed=0, transcendentals=0)


def fixed(shape):
    zeros = (0,) * len(shape)
    return pl.BlockSpec(shape, lambda *_: zeros, pipeline_mode=pl.Buffered(1))


def lanes_of(index, width=LANES):
    return slice(index * width, (index + 1) * width)


def near_cap(start, total, length, first):
    key = start - WIN + first + lax.broadcasted_iota(jnp.int32, (NEAR, TILE), 0)
    query = start + first + lax.broadcasted_iota(jnp.int32, (NEAR, TILE), 1)
    near = (jnp.abs(query - key) <= WIN) & (key >= 0) & (key < total)
    return jnp.where(near & ((key < length) | (key == query)), BIG, NEG)


def far_cap(start, total, length, first):
    pooled = start // 4 - PWIN + first // 4 + lax.broadcasted_iota(jnp.int32, (FAR, TILE), 0)
    coarse = (start + first + lax.broadcasted_iota(jnp.int32, (FAR, TILE), 1)) // 4
    far = (jnp.abs(coarse - pooled) <= PWIN) & (pooled >= 0) & (pooled < total // 4)
    return jnp.where(far & ((4 * pooled < length) | (pooled == coarse)), BIG, NEG)


def split_pair(pair):
    lane = lax.broadcasted_iota(jnp.int32, pair.shape, 1)
    zero = jnp.zeros_like(pair)
    return jnp.concatenate(
        [jnp.where(lane < HEAD_DIM, pair, zero), jnp.where(lane < HEAD_DIM, zero, pair)], axis=0
    )


LEVELS = ((0, NEAR), (NEAR, NEAR + FAR))


def join_pair(stacked):
    row = lax.broadcasted_iota(jnp.int32, (LANES, TILE), 0)
    return jnp.where(row < HEAD_DIM, stacked[:, :TILE], stacked[:, TILE:])


def project_kernel(
    info, beside, own, across, weight_a, weight_b, query, key, value, pool, rim_near, rim_across,
    vectors, wide,
):
    piece = own.shape[1]
    pools = piece // 4
    even = (info[0] // piece) % 2 == 0
    low = jnp.where(even, across[0], beside[0])
    high = jnp.where(even, beside[0], across[0])
    small = weight_b[:, 3 * D - CUT :].astype(F32).T
    vectors[...] = small[:16]
    taps = small[4:14]

    def weight_chunk(chunk):
        if chunk < CUT // 256:
            return weight_a[:, lanes_of(chunk, 256)]
        return weight_b[:, lanes_of(chunk - CUT // 256, 256)]

    for chunk in range(3):
        cols = lanes_of(chunk, 256)
        query[0, :, cols] = (nn(own[0], weight_chunk(chunk)) * SCALE).astype(BF16)
    for chunk in range(6):
        target = key if chunk < 3 else value
        cols = lanes_of(chunk % 3, 256)
        block = weight_chunk(3 + chunk)
        for source, base, count in ((low, 0, WIN), (own[0], WIN, piece), (high, WIN + piece, WIN)):
            rounded = nn(source, block).astype(BF16)
            held = rounded.astype(F32)
            wide[2 * chunk, base : base + count, :] = held[:, :LANES]
            wide[2 * chunk + 1, base : base + count, :] = held[:, LANES:]
            target[0, base : base + count, cols] = rounded
    for group in range(2 * GROUPS):
        part = group // GROUPS
        cols = lanes_of(group % GROUPS)
        pooled = None
        for tap in range(5):
            term = taps[5 * part + tap : 5 * part + tap + 1, cols] * wide[
                group, pl.ds(WIN - 2 + tap, pools, stride=4), :
            ]
            pooled = term if pooled is None else pooled + term
        pooled = pooled.astype(BF16)
        pool[0, part, :, cols] = pooled
        first, last = (pooled[:PWIN], pooled[pools - PWIN :])
        rim_near[0, part, :, cols] = jnp.where(even, last, first)
        rim_across[0, part, :, cols] = jnp.where(even, first, last)


def level_mixed(queries, keys, values, cap, lse, tile, pairs):
    heads = [(at, head) for at in range(len(pairs)) for head in range(2)]
    scores = [nt(keys[at], queries[at][head * TILE : (head + 1) * TILE]) for at, head in heads]
    scores = [jnp.minimum(entry, cap[...]) for entry in scores]
    tops = [jnp.max(entry, axis=0, keepdims=True) for entry in scores]
    raised = [jnp.exp(entry - top) for entry, top in zip(scores, tops)]
    norms = [jnp.sum(entry, axis=0, keepdims=True) for entry in raised]
    for (at, head), top, norm in zip(heads, tops, norms):
        lse[0, tile, pairs[at] : pairs[at] + 1, lanes_of(head)] = top + jnp.log(norm)
    probs = [(entry * (1.0 / norm)).astype(BF16) for entry, norm in zip(raised, norms)]
    turned = [entry.T for entry in values]
    mixed = [
        nn(entry, jnp.concatenate(probs[2 * at : 2 * at + 2], axis=1)) for at, entry in enumerate(turned)
    ]
    return [join_pair(entry).T for entry in mixed]


def near_kernel(info, query, key, value, mixed, lse, cap):
    piece = query.shape[1]
    which = pl.program_id(0)
    start, total, length = (info[0], info[1], info[2 + which])

    def tile_step(tile, carry):
        first = pl.multiple_of(tile * TILE, TILE)
        cap[...] = near_cap(start, total, length, first)
        for begin in range(0, GROUPS, TOGETHER):
            pairs = range(begin, begin + TOGETHER)
            queries = [split_pair(query[0, pl.ds(first, TILE), lanes_of(pair)]) for pair in pairs]
            keys = [key[0, pl.ds(first, NEAR), lanes_of(pair)] for pair in pairs]
            values = [value[0, pl.ds(first, NEAR), lanes_of(pair)] for pair in pairs]
            parts = level_mixed(queries, keys, values, cap, lse, tile, pairs)
            for pair, part in zip(pairs, parts):
                mixed[0, pl.ds(first, TILE), lanes_of(pair)] = part
        return carry

    lax.fori_loop(0, piece // TILE, tile_step, 0)


def far_kernel(info, query, pool, beside, across, mixed, att, pkey, pvalue, lse, cap):
    piece = query.shape[1]
    pools = piece // 4
    which = pl.program_id(0)
    start, total, length = (info[0], info[1], info[2 + which])
    even = (start // piece) % 2 == 0
    for part, target in enumerate((pkey, pvalue)):
        target[0, :PWIN, :] = jnp.where(even, across[0, part], beside[0, part])
        target[0, PWIN : PWIN + pools, :] = pool[0, part]
        target[0, PWIN + pools :, :] = jnp.where(even, beside[0, part], across[0, part])

    def tile_step(tile, carry):
        first = pl.multiple_of(tile * TILE, TILE)
        coarse = pl.multiple_of(tile * (TILE // 4), TILE // 4)
        cap[...] = far_cap(start, total, length, first)
        for begin in range(0, GROUPS, TOGETHER):
            pairs = range(begin, begin + TOGETHER)
            queries = [split_pair(query[0, pl.ds(first, TILE), lanes_of(pair)]) for pair in pairs]
            keys = [pkey[0, pl.ds(coarse, FAR), lanes_of(pair)] for pair in pairs]
            values = [pvalue[0, pl.ds(coarse, FAR), lanes_of(pair)] for pair in pairs]
            parts = level_mixed(queries, keys, values, cap, lse, tile, pairs)
            for pair, part in zip(pairs, parts):
                place = (0, pl.ds(first, TILE), lanes_of(pair))
                att[place] = (mixed[place] + part).astype(BF16)
        return carry

    lax.fori_loop(0, piece // TILE, tile_step, 0)


def per_seq(body, operands, shapes, micros, name, shared=0, common=(), scratch=()):
    info, *rest = operands
    seqs = rest[0].shape[0]
    split = len(rest) - shared

    def seq_block(shape):
        return pl.BlockSpec((1,) + tuple(shape), lambda s: (s,) + (0,) * len(shape))

    return pl.pallas_call(
        body,
        grid=(seqs,),
        in_specs=[pl.BlockSpec(memory_space=pltpu.SMEM)]
        + [seq_block(entry.shape[1:]) for entry in rest[:split]]
        + [fixed(entry.shape) for entry in rest[split:]],
        out_specs=[seq_block(shape) for shape, _ in shapes]
        + [pl.BlockSpec(shape, lambda s: (0,) * len(shape)) for shape, _ in common],
        out_shape=[jax.ShapeDtypeStruct((seqs,) + shape, dtype) for shape, dtype in shapes]
        + [jax.ShapeDtypeStruct(shape, dtype) for shape, dtype in common],
        scratch_shapes=list(scratch),
        compiler_params=params(),
        cost_estimate=cost(micros),
        name=name,
    )(*operands)


def project(info, beside, own, across, weight_a, weight_b):
    _, piece, width = own.shape
    extent, pools = (piece + 2 * WIN, piece // 4)
    return per_seq(
        project_kernel,
        (info, beside, own, across, weight_a, weight_b),
        [
            ((piece, width), BF16),
            ((extent, width), BF16),
            ((extent, width), BF16),
            ((2, pools, width), BF16),
            ((2, PWIN, width), BF16),
            ((2, PWIN, width), BF16),
        ],
        10,
        "project",
        shared=2,
        common=[((16, width), F32)],
        scratch=[pltpu.VMEM((2 * GROUPS, extent, LANES), F32)],
    )


def near_attend(info, query, key, value):
    _, piece, width = query.shape
    return per_seq(
        near_kernel,
        (info, query, key, value),
        [((piece, width), F32), ((piece // TILE, 8, 2 * TILE), F32)],
        30,
        "near",
        scratch=[pltpu.VMEM((NEAR, TILE), F32)],
    )


def far_attend(info, query, pool, beside, across, mixed):
    _, piece, width = query.shape
    pools = piece // 4 + 2 * PWIN
    return per_seq(
        far_kernel,
        (info, query, pool, beside, across, mixed),
        [
            ((piece, width), BF16),
            ((pools, width), BF16),
            ((pools, width), BF16),
            ((piece // TILE, 8, 2 * TILE), F32),
        ],
        12,
        "far",
        scratch=[pltpu.VMEM((FAR, TILE), F32)],
    )


def layer_stats(values):
    centred = values - jnp.mean(values, axis=-1, keepdims=True)
    inverse = lax.rsqrt(jnp.mean(centred * centred, axis=-1, keepdims=True) + EPS_NORM)
    return (centred * inverse, inverse)


def layer_back(grad, normed, inverse):
    return inverse * (
        grad
        - jnp.mean(grad, axis=-1, keepdims=True)
        - normed * jnp.mean(grad * normed, axis=-1, keepdims=True)
    )


def gelu_parts(up):
    size = jnp.abs(up)
    bell = jnp.exp(-0.5 * (up * up))
    near = 1.0 / (1.0 + TAIL_STEP * size)
    poly = jnp.full_like(up, TAIL[-1])
    for factor in TAIL[-2::-1]:
        poly = poly * near + factor
    tail = bell * (near * poly)
    phi = jnp.where(up >= 0.0, 1.0 - tail, tail)
    return (up * phi, phi + up * (bell * INV_ROOT))


def feed_kernel(
    tokens, att, cot, packed, vectors, block_out, first_grad, hidden_low, active,
    up_grad, branch_grad, mixed_grad, att_grad, sums, slope,
):
    step = pl.program_id(0)
    gain_one, bias_one, gain_two, bias_two = [vectors[i : i + 1, :] for i in range(4)]
    def merge():
        return packed[:, :D]

    def expand(chunk):
        return packed[:, lanes_of(1 + chunk, D)]

    def shrink(chunk):
        return packed[:, lanes_of(1 + FF // D + chunk, D)]

    first_norm, first_inv = layer_stats(tokens[...].astype(F32) + nn(att[...], merge()))
    hidden = first_norm * gain_one + bias_one
    low = hidden.astype(BF16)
    hidden_low[...] = low
    branch = None
    for chunk in range(FF // D):
        cols = lanes_of(chunk, D)
        wide, steep = gelu_parts(nn(low, expand(chunk)))
        narrow = wide.astype(BF16)
        active[:, cols] = narrow
        slope[:, cols] = steep
        term = nn(narrow, shrink(chunk))
        branch = term if branch is None else branch + term
    second_norm, second_inv = layer_stats(hidden + branch)
    block_out[...] = (second_norm * gain_two + bias_two).astype(BF16)
    cotangent = cot[...].astype(F32)

    @pl.when(step == 0)
    def clear():
        sums[...] = jnp.zeros_like(sums)

    def add_sum(row, value):
        sums[row : row + 1, :] += jnp.sum(value, axis=0, keepdims=True)

    add_sum(2, cotangent * second_norm)
    add_sum(3, cotangent)
    second_grad = layer_back(cotangent * gain_two, second_norm, second_inv)
    second_low = second_grad.astype(BF16)
    branch_grad[...] = second_low
    feed = None
    for chunk in range(FF // D):
        cols = lanes_of(chunk, D)
        narrow = (nt(second_low, shrink(chunk)) * slope[:, cols]).astype(BF16)
        up_grad[:, cols] = narrow
        term = nt(narrow, expand(chunk))
        feed = term if feed is None else feed + term
    hidden_grad = second_grad + feed.astype(BF16).astype(F32)
    add_sum(0, hidden_grad * first_norm)
    add_sum(1, hidden_grad)
    grad = layer_back(hidden_grad * gain_one, first_norm, first_inv)
    first_grad[...] = grad
    grad_low = grad.astype(BF16)
    mixed_grad[...] = grad_low
    att_grad[...] = nt(grad_low, merge()).astype(BF16)


def feed(tokens, att, cot, packed, vectors):
    rows, width = tokens.shape
    block = 256
    ff = FF

    def row_block(cols):
        return pl.BlockSpec((block, cols), lambda i: (i, 0))

    outs = [
        (width, BF16),
        (width, F32),
        (width, BF16),
        (ff, BF16),
        (ff, BF16),
        (width, BF16),
        (width, BF16),
        (width, BF16),
    ]
    return pl.pallas_call(
        feed_kernel,
        grid=(rows // block,),
        in_specs=[row_block(width)] * 3
        + [fixed(packed.shape), fixed(vectors.shape)],
        out_specs=[row_block(cols) for cols, _ in outs] + [pl.BlockSpec((8, width), lambda i: (0, 0))],
        out_shape=[jax.ShapeDtypeStruct((rows, cols), dtype) for cols, dtype in outs]
        + [jax.ShapeDtypeStruct((8, width), F32)],
        scratch_shapes=[pltpu.VMEM((block, ff), F32)],
        compiler_params=params(),
        cost_estimate=cost(48),
        name="feed",
    )(tokens, att, cot, packed, vectors)


def back_kernel(
    which, info, query, key, value, pkey, pvalue, grad, near_lse, far_lse, query_grad, near_grad,
    far_grad, rim_near, rim_across, caps,
):
    piece = query.shape[1]
    even = (info[0] // piece) % 2 == 0
    start, total, length = (info[0], info[1], info[2 + which])
    near_grad[...] = jnp.zeros_like(near_grad)
    far_grad[...] = jnp.zeros_like(far_grad)

    def tile_step(tile, carry):
        first = pl.multiple_of(tile * TILE, TILE)
        coarse = pl.multiple_of(tile * (TILE // 4), TILE // 4)
        for cap, (begin, end) in zip((near_cap, far_cap), LEVELS):
            block = cap(start, total, length, first)
            caps[begin:end, :TILE] = block
            caps[begin:end, TILE:] = block
        near_rows, far_rows = (pl.ds(first, NEAR), pl.ds(coarse, FAR))
        place = pl.ds(first, TILE)
        for start_pair in range(0, GROUPS, BACK_TOGETHER):
            pairs = range(start_pair, start_pair + BACK_TOGETHER)
            many = range(BACK_TOGETHER)
            spans = [lanes_of(pair) for pair in pairs]
            queries = [split_pair(query[0, place, cols]) for cols in spans]
            grads = [split_pair(grad[0, place, cols]) for cols in spans]
            keys = [
                jnp.concatenate([key[0, near_rows, cols], pkey[0, far_rows, cols]], axis=0)
                for cols in spans
            ]
            values = [
                jnp.concatenate([value[0, near_rows, cols], pvalue[0, far_rows, cols]], axis=0)
                for cols in spans
            ]
            scores = [nt(keys[at], queries[at]) for at in many]
            prob_grads = [nt(values[at], grads[at]) for at in many]
            probs = [[] for _ in many]
            score_grads = [[] for _ in many]
            for level, (begin, end) in enumerate(LEVELS):
                lse = (near_lse, far_lse)[level]
                exact_probs = [
                    jnp.exp(
                        jnp.minimum(scores[at][begin:end], caps[begin:end, :])
                        - lse[0, tile, pairs[at] : pairs[at] + 1, :]
                    )
                    for at in many
                ]
                weighted = [exact_probs[at] * prob_grads[at][begin:end] for at in many]
                inner = [jnp.sum(entry, axis=0, keepdims=True) for entry in weighted]
                for at in many:
                    score_grads[at].append((weighted[at] - exact_probs[at] * inner[at]).astype(BF16))
                    probs[at].append(exact_probs[at].astype(BF16))
            score_grads = [jnp.concatenate(entry, axis=0) for entry in score_grads]
            key_parts = [nn(score_grads[at], queries[at]) for at in many]
            value_parts = [nn(jnp.concatenate(probs[at], axis=0), grads[at]) for at in many]
            turned = [entry.T for entry in keys]
            query_parts = [nn(turned[at], score_grads[at]) for at in many]
            for at, cols in enumerate(spans):
                near_grad[0, 0, near_rows, cols] += key_parts[at][:NEAR]
                far_grad[0, 0, far_rows, cols] += key_parts[at][NEAR:]
                near_grad[0, 1, near_rows, cols] += value_parts[at][:NEAR]
                far_grad[0, 1, far_rows, cols] += value_parts[at][NEAR:]
                query_grad[0, place, cols] = (join_pair(query_parts[at]) * SCALE).T.astype(BF16)
        return carry

    lax.fori_loop(0, piece // TILE, tile_step, 0)
    pools = far_grad.shape[2]
    blank = jnp.zeros((16, far_grad.shape[3]), BF16)
    for part in range(2):
        low = [near_grad[0, part, :WIN, :], far_grad[0, part, : PWIN + 16, :]]
        low = [entry.astype(BF16) for entry in low]
        high = [near_grad[0, part, WIN + piece :, :], far_grad[0, part, pools - PWIN :, :]]
        high = [entry.astype(BF16) for entry in high]

        @pl.when(even)
        def even_side():
            rim_near[0, part, :WIN, :] = high[0]
            rim_near[0, part, WIN : WIN + PWIN, :] = high[1]
            rim_near[0, part, WIN + PWIN :, :] = blank
            rim_across[0, part, :WIN, :] = low[0]
            rim_across[0, part, WIN:, :] = low[1]

        @pl.when(jnp.logical_not(even))
        def odd_side():
            rim_across[0, part, :WIN, :] = high[0]
            rim_across[0, part, WIN : WIN + PWIN, :] = high[1]
            rim_across[0, part, WIN + PWIN :, :] = blank
            rim_near[0, part, :WIN, :] = low[0]
            rim_near[0, part, WIN:, :] = low[1]


def seq_slice(shape, which):
    return pl.BlockSpec((1,) + tuple(shape[1:]), lambda _: (which,) + (0,) * (len(shape) - 1))


def back(which, info, query, key, value, pkey, pvalue, grad, near_lse, far_lse):
    _, piece, width = query.shape
    extent, pools = (key.shape[1], pkey.shape[1])
    operands = (query, key, value, pkey, pvalue, grad, near_lse, far_lse)
    shapes = [
        ((1, piece, width), BF16),
        ((1, 2, extent, width), F32),
        ((1, 2, pools, width), F32),
        ((1, 2, WIN + PWIN + 16, width), BF16),
        ((1, 2, WIN + PWIN + 16, width), BF16),
    ]
    return pl.pallas_call(
        functools.partial(back_kernel, which),
        grid=(1,),
        in_specs=[pl.BlockSpec(memory_space=pltpu.SMEM)]
        + [seq_slice(entry.shape, which) for entry in operands],
        out_specs=[seq_slice(shape, 0) for shape, _ in shapes],
        out_shape=[jax.ShapeDtypeStruct(shape, dtype) for shape, dtype in shapes],
        scratch_shapes=[pltpu.VMEM((NEAR + FAR, 2 * TILE), F32)],
        compiler_params=params(),
        cost_estimate=cost(0.01 if which else 30),
        name="back",
    )(info, *operands)


def pool_back_kernel(
    first, last, info, query_grad, near_grad, far_grad, beside, across, key, value, taps, turned, *rest
):
    rest = list(rest)
    before, taps_before = (None, None) if first else (rest.pop(0), rest.pop(0))
    sums = rest.pop(0) if last else None
    full_grad = rest.pop(0)
    outs = [rest.pop(0), rest.pop(0)]
    held, spread, window, taps_grad = rest
    piece = full_grad.shape[1]
    pools = piece // 4
    even = (info[0] // piece) % 2 == 0
    full_grad[0, :, :D] = query_grad[0]
    if first:
        taps_grad[...] = jnp.zeros_like(taps_grad)
    else:
        taps_grad[...] = taps_before[...]

    def product(chunk):
        cols = lanes_of(chunk, 256)
        total = nn(turned[...], full_grad[0, :, cols])
        if not first:
            total = total + before[:, cols]
        if not last:
            outs[0][:, cols] = total
        elif chunk < CUT // 256:
            outs[0][:, cols] = total.astype(BF16)
        else:
            outs[1][:, lanes_of(chunk - CUT // 256, 256)] = total.astype(BF16)

    for group in range(2 * GROUPS):
        if group % 4 == 0:
            product(group // 4)
        part = group // GROUPS
        cols = lanes_of(group % GROUPS)
        source = key if part == 0 else value
        pair = [entry[0, part, :, cols].astype(F32) for entry in (beside, across)]
        from_high = jnp.where(even, pair[0], pair[1])
        from_low = jnp.where(even, pair[1], pair[0])
        tap = [taps[4 + 5 * part + t : 5 + 5 * part + t, cols] for t in range(5)]
        held[0:pools, :] = far_grad[0, part, PWIN : PWIN + pools, cols]
        held[0:PWIN, :] += from_low[WIN : WIN + PWIN]
        held[pools - PWIN : pools, :] += from_high[WIN : WIN + PWIN]
        held[pools : pools + 16, :] = (
            far_grad[0, part, PWIN + pools : PWIN + pools + 16, cols] + from_high[WIN + PWIN :]
        )
        now = held[0:pools, :]
        later = held[1 : pools + 1, :]
        spread[pl.ds(0, pools, stride=4), :] = tap[2] * now
        spread[pl.ds(1, pools, stride=4), :] = tap[3] * now
        spread[pl.ds(2, pools, stride=4), :] = tap[4] * now + tap[0] * later
        spread[pl.ds(3, pools, stride=4), :] = tap[1] * later
        spread[0:WIN, :] += from_low[:WIN]
        spread[piece - WIN : piece, :] += from_high[:WIN]
        total = near_grad[0, part, WIN : WIN + piece, cols] + spread[...]
        full_grad[0, :, lanes_of(GROUPS + group)] = total.astype(BF16)
        window[...] = source[0, WIN - 16 : WIN + piece + 16, cols].astype(F32)
        for t in range(5):
            row = 5 * part + t
            taps_grad[row : row + 1, cols] += jnp.sum(
                now * window[pl.ds(14 + t, pools, stride=4), :], axis=0, keepdims=True
            )
        if group % 2 == 1:
            product((GROUPS + group) // 2)
    if last:
        zeros = jnp.zeros((LANES - 14, D), F32)
        small = jnp.concatenate([sums[0:4, :], taps_grad[0:10, :], zeros], axis=0)
        outs[1][:, 3 * D - CUT :] = small.T.astype(BF16)
    else:
        outs[1][...] = taps_grad[...]


def pool_back(which, seqs, info, entries, key, value, taps, turned, before, sums):
    near_grad = entries[1]
    _, _, extent, width = near_grad.shape
    piece = extent - 2 * WIN
    pools = piece // 4
    first, last = (which == 0, which == seqs - 1)
    extra = (() if first else tuple(before)) + ((sums,) if last else ())
    if last:
        outs = [((width, CUT), BF16), ((width, 3 * width + LANES - CUT), BF16)]
    else:
        outs = [((width, 3 * width), F32), ((16, width), F32)]
    return pl.pallas_call(
        functools.partial(pool_back_kernel, first, last),
        grid=(1,),
        in_specs=[pl.BlockSpec(memory_space=pltpu.SMEM)]
        + [seq_slice(entry.shape, 0) for entry in entries]
        + [seq_slice(entry.shape, which) for entry in (key, value)]
        + [fixed(taps.shape), pl.BlockSpec((width, piece), lambda _: (0, which))]
        + [fixed(entry.shape) for entry in extra],
        out_specs=[seq_slice((1, piece, 3 * width), 0)] + [fixed(shape) for shape, _ in outs],
        out_shape=[jax.ShapeDtypeStruct((1, piece, 3 * width), BF16)]
        + [jax.ShapeDtypeStruct(shape, dtype) for shape, dtype in outs],
        scratch_shapes=[
            pltpu.VMEM((pools + 16, LANES), F32),
            pltpu.VMEM((piece, LANES), F32),
            pltpu.VMEM((piece + 32, LANES), F32),
            pltpu.VMEM((16, width), F32),
        ],
        compiler_params=params(),
        cost_estimate=cost(0.01 if which else 30),
        name="pool_back",
    )(info, *entries, key, value, taps, turned, *extra)


def unmix(width):
    row = lax.broadcasted_iota(jnp.int32, (4 * width, 4 * width), 0)
    col = lax.broadcasted_iota(jnp.int32, (4 * width, 4 * width), 1)
    return jnp.where(row == 4 * (col % width) + col // width, 1.0, 0.0)


def exact(left, right):
    return jnp.dot(left, right, precision=lax.Precision.HIGHEST, preferred_element_type=F32)


def exact_nt(left, right):
    return lax.dot_general(
        left, right, (((1,), (1,)), ((), ())), precision=lax.Precision.HIGHEST, preferred_element_type=F32
    )


def pack_kernel(merge, expand, shrink, out, held):
    rows = merge.shape[0]
    mixer = unmix(LANES).astype(BF16)
    out[:, :D] = merge[...].astype(BF16)
    for group in range(FF // (4 * LANES)):
        block = nn(expand[:, lanes_of(group, 4 * LANES)].astype(BF16), mixer).astype(BF16)
        for j in range(4):
            first = D + j * D + group * LANES
            out[:, first : first + LANES] = block[:, lanes_of(j)]
    for group in range(GROUPS):
        held[group] = shrink[:, lanes_of(group)]
        for j in range(4):
            first = (5 + j) * D + group * LANES
            out[:, first : first + LANES] = held[group, pl.ds(j, rows, stride=4), :].astype(BF16)


def squares(block):
    return jnp.sum(block * block, axis=0, keepdims=True)


def late_kernel(late, *rest):
    olds, (out, expand, shrink, held) = (rest[:4], rest[4:])
    rows = late.shape[0]
    mixer = unmix(LANES).astype(BF16)
    for group in range(FF // (4 * LANES)):
        pieces = []
        for j in range(4):
            first = (5 + j) * D + group * LANES
            pieces.append(late[:, first : first + LANES])
        left = jnp.concatenate(pieces, axis=1)
        total = None
        for _ in range(3):
            top = left.astype(BF16)
            left = left - top.astype(F32)
            term = nt(top, mixer)
            total = term if total is None else total + term
        expand[:, lanes_of(group, 4 * LANES)] = total
    for group in range(GROUPS):
        for j in range(4):
            held[group, pl.ds(j, rows, stride=4), :] = late[:, lanes_of(j * GROUPS + group)]
        shrink[:, lanes_of(group)] = held[group]
    out[:, : 3 * D] = jnp.zeros((1, 3 * D), F32)
    out[:, 3 * D : 4 * D] = squares(late[:, 4 * D : 5 * D])
    for j in range(FF // D):
        out[:, (4 + j) * D : (5 + j) * D] = squares(expand[:, lanes_of(j, D)])
    out[:, 8 * D : 9 * D] = squares(shrink[...])
    lane = lax.broadcasted_iota(jnp.int32, (1, LANES), 1)
    tail = jnp.zeros((1, LANES), F32)
    for slot, entry in enumerate(olds):
        tail = jnp.where(lane == slot + 1, jnp.sum(entry[...], axis=1, keepdims=True), tail)
    out[:, 9 * D :] = tail


def stats_kernel(early, base, out):
    out[:, : 3 * D] = squares(early[:, : 3 * D])
    out[:, 3 * D : 9 * D] = base[:, 3 * D : 9 * D]
    lane = lax.broadcasted_iota(jnp.int32, (1, LANES), 1)
    small = jnp.sum(squares(early[:, 3 * D :]), axis=1, keepdims=True)
    out[:, 9 * D :] = base[:, 9 * D :] + jnp.where(lane == 0, small, 0.0)


def update_kernel(
    total, early, late, expand, shrink, rows_0, rows_1, rows_2, rows_3, cols_0, cols_1,
    cols_2, cols_3, weight_0, weight_1, weight_2, weight_3, small, moment,
    norm_out, grad_0, rows_new_0, cols_new_0, new_0, low_0, grad_1, rows_new_1, cols_new_1, new_1,
    low_1, grad_2, rows_new_2, cols_new_2, new_2, low_2, grad_3, rows_new_3, cols_new_3, new_3,
    low_3, small_grad, moment_new, small_new, small_low,
):
    smalls = small.shape[0]
    tail = total[:, 9 * D :]
    spans = ((0, 3 * D), (3 * D, 4 * D), (4 * D, 8 * D), (8 * D, 9 * D))
    matrix_sums = [jnp.sum(total[:, a:b], axis=1, keepdims=True) for a, b in spans]
    norm = jnp.sqrt(matrix_sums[0] + matrix_sums[1] + matrix_sums[2] + matrix_sums[3] + tail[:, 0:1])
    clip = CLIP / jnp.maximum(norm, CLIP)
    norm_out[...] = norm
    parts = (
        [early[:, lanes_of(j, D)] for j in range(3)],
        [late[:, 4 * D : 5 * D]],
        [expand[:, lanes_of(j, D)] for j in range(FF // D)],
        [shrink[...]],
    )
    heights = (D, D, D, FF)
    olds = (
        (rows_0, cols_0, weight_0, grad_0, rows_new_0, cols_new_0, new_0, low_0),
        (rows_1, cols_1, weight_1, grad_1, rows_new_1, cols_new_1, new_1, low_1),
        (rows_2, cols_2, weight_2, grad_2, rows_new_2, cols_new_2, new_2, low_2),
        (rows_3, cols_3, weight_3, grad_3, rows_new_3, cols_new_3, new_3, low_3),
    )
    for index in range(4):
        old_rows, old_cols, weight, grad, rows_new, cols_new, new, low = olds[index]
        begin, end = spans[index]
        width, height = (end - begin, heights[index])
        mean_cols = (total[:, begin:end] * clip) * clip / height + EPS_FACTOR
        fresh_cols = DECAY * old_cols[...] + (1.0 - DECAY) * mean_cols
        for group in range(width // LANES):
            cols_new[group : group + 1, :] = fresh_cols[:, lanes_of(group)]
        squared = sum(part * part for part in parts[index])
        row_sum = exact_nt(jnp.ones((8, D), F32), squared)[:1]
        mean_rows = (row_sum * clip) * clip / width + EPS_FACTOR
        fresh_rows = DECAY * old_rows[...] + (1.0 - DECAY) * mean_rows
        rows_new[...] = fresh_rows
        row = lax.broadcasted_iota(jnp.int32, (weight.shape[0], weight.shape[0]), 0)
        col = lax.broadcasted_iota(jnp.int32, (weight.shape[0], weight.shape[0]), 1)
        down = jnp.sum(jnp.where(row == col, fresh_rows, 0.0), axis=1, keepdims=True)
        mean_all = (matrix_sums[index] * clip) * clip / (width * height) + EPS_FACTOR
        row_mean = DECAY * (tail[:, 1 + index : 2 + index] / height) + (1.0 - DECAY) * mean_all
        for j, part in enumerate(parts[index]):
            cols = lanes_of(j, D)
            clipped = part * clip
            grad[:, cols] = clipped
            estimate = down * fresh_cols[:, cols] / row_mean
            fresh = weight[:, cols] - RATE * clipped * lax.rsqrt(estimate)
            new[:, cols] = fresh
            low[:, cols] = fresh.astype(BF16)
    row = lax.broadcasted_iota(jnp.int32, (16, LANES), 0)
    col = lax.broadcasted_iota(jnp.int32, (16, LANES), 1)
    turned = exact_nt(jnp.where(row == col, 1.0, 0.0), early[:, 3 * D :])
    clipped = turned[:smalls] * clip
    small_grad[...] = clipped
    fresh_moment = DECAY * moment[...] + (1.0 - DECAY) * (clipped * clipped + EPS_FACTOR)
    moment_new[...] = fresh_moment
    fresh = small[...] - RATE * clipped * lax.rsqrt(fresh_moment)
    small_new[...] = fresh
    small_low[...] = fresh.astype(BF16)


def whole_call(body, outs, operands, name, micros, scratch=()):
    return pl.pallas_call(
        body,
        out_shape=[jax.ShapeDtypeStruct(shape, dtype) for shape, dtype in outs],
        in_specs=[pl.BlockSpec(memory_space=pltpu.VMEM)] * len(operands),
        out_specs=[pl.BlockSpec(memory_space=pltpu.VMEM)] * len(outs),
        scratch_shapes=list(scratch),
        compiler_params=params(),
        cost_estimate=cost(micros),
        name=name,
    )(*operands)


def swap(value, axis, bit):
    size = lax.axis_size(axis)
    return lax.ppermute(value, axis, [(i, i ^ (1 << bit)) for i in range(size)])


def bits_of(axis):
    return lax.axis_size(axis).bit_length() - 1


def side(axis, bit):
    return (lax.axis_index(axis) >> bit) & 1


def doubled(value, axis, bit, dim):
    other = swap(value, axis, bit)
    mine = side(axis, bit)
    return jnp.where(
        mine == 0, jnp.stack([value, other], axis=dim), jnp.stack([other, value], axis=dim)
    )


def halves(value, axis, bit, dim):
    mine = side(axis, bit)
    away = lax.dynamic_index_in_dim(value, 1 - mine, dim, keepdims=False)
    return [lax.dynamic_index_in_dim(value, mine, dim, keepdims=False), swap(away, axis, bit)]


def quarters(value, axis, bit, dim):
    size = lax.axis_size(axis)
    mine = (lax.axis_index(axis) >> bit) & 3
    value = value.reshape(value.shape[:dim] + (4,) + value.shape[dim + 2 :])
    blocks = [lax.dynamic_index_in_dim(value, mine, dim, keepdims=False)]
    for step in range(1, 4):
        away = lax.dynamic_index_in_dim(value, mine ^ step, dim, keepdims=False)
        blocks.append(lax.ppermute(away, axis, [(i, i ^ (step << bit)) for i in range(size)]))
    return blocks


def added(blocks, dtype):
    return sum(block.astype(F32) for block in blocks).astype(dtype)


def place_of(done, step):
    return sum(1 for other in done if other > step)


def order_key(axis, bit):
    return (1 if axis == "seq" else 0, bit)


def gather_pairs(value, steps):
    done = []
    for axis, bit in steps:
        at = order_key(axis, bit)
        value = doubled(value, axis, bit, place_of(done, at))
        done.append(at)
    return (value, done)


def scatter_begin(value, steps, lead=0):
    left = [(axis, bit + k) for axis, bit, count in steps for k in range(count)]
    left = sorted((order_key(axis, bit) for axis, bit in left), reverse=True)
    value = value.reshape(value.shape[:lead] + (2,) * len(left) + value.shape[lead + 1 :])
    return (value, left, list(steps), lead)


def scatter_step(state, gate=None):
    value, left, steps, lead = state
    axis, bit, count = steps[0]
    gone = [order_key(axis, bit + k) for k in range(count)]
    dtype = F32 if len(steps) == 1 else BF16
    dim = lead + min(left.index(entry) for entry in gone)
    blocks = (halves if count == 1 else quarters)(value, axis, bit, dim)
    if gate is not None:
        blocks, _ = lax.optimization_barrier((blocks, gate))
    value = added(blocks, dtype)
    return (value, [other for other in left if other not in gone], steps[1:], lead)


def scatter_end(state, gate=None):
    while state[2]:
        state = scatter_step(state, gate)
    return state[0]


def after(states, values):
    blocks, values = lax.optimization_barrier(([state[0] for state in states], values))
    return ([(block,) + tuple(state[1:]) for block, state in zip(blocks, states)], values)


def gather_far(shard):
    steps = [("seq", bit) for bit in reversed(range(1, bits_of("seq")))]
    return gather_pairs(shard, steps)


def gather_near(part, done, first):
    side_bits = [("grp", bit) for bit in range(1, bits_of("grp"))]
    middle = [("seq", 0)] + side_bits if first == "seq" else side_bits + [("seq", 0)]
    done = list(done)
    for axis, bit in middle + [("grp", 0)]:
        at = order_key(axis, bit)
        part = doubled(part, axis, bit, place_of(done, at))
        done.append(at)
    return part.reshape(-1, part.shape[-1])


def near_swap(even, odd):
    mine = side("seq", 0)
    return swap(jnp.where(mine == 0, even, odd), "seq", 0)


def across_swap(value):
    size = lax.axis_size("seq")
    pairs = [(i, i - 1 if i % 2 == 0 else i + 1) for i in range(size)]
    return lax.ppermute(value, "seq", [(i, j) for i, j in pairs if 0 <= j < size])


def diagonal_swap(even, odd):
    return across_swap(jnp.where(side("seq", 0) == 0, even, odd))


def late_steps(side_first):
    side_bits = [("grp", bit, 1) for bit in range(1, bits_of("grp"))]
    far_bits = [("seq", bit, 1) for bit in range(1, bits_of("seq"))]
    start = side_bits + far_bits[:1] if side_first else far_bits[:1] + side_bits
    return [("grp", 0, 1)] + start + [("seq", 0, 1)] + far_bits[1:]


def scatter_steps(first, most=2):
    count = bits_of("seq")
    far_bits = [("seq", bit, min(most, count - bit)) for bit in range(1, count, most)]
    side_bits = [("grp", bit, 1) for bit in range(1, bits_of("grp"))]
    middle = [("seq", 0, 1)] + side_bits if first == "seq" else side_bits + [("seq", 0, 1)]
    return [("grp", 0, 1)] + middle + far_bits


def summed_all(value):
    for axis in ("grp", "seq"):
        count, size = (bits_of(axis), lax.axis_size(axis))
        for bit in range(0, count, 2):
            others = [
                lax.ppermute(value, axis, [(i, i ^ (step << bit)) for i in range(size)])
                for step in range(1, 4 if bit + 1 < count else 2)
            ]
            value = value + others[0]
            if len(others) == 3:
                value = value + (others[1] + others[2])
    return value


def local(
    tokens,
    seq_lengths,
    answer_mask,
    out_grad,
    qkv_weight,
    merge_weight,
    expand_weight,
    shrink_weight,
    small_params,
    qkv_rows,
    qkv_cols,
    merge_rows,
    merge_cols,
    expand_rows,
    expand_cols,
    shrink_rows,
    shrink_cols,
    small_moment,
):
    seqs, piece, width = tokens.shape
    axes = ("seq", "grp")
    devices = lax.axis_size("seq") * lax.axis_size("grp")
    rows = qkv_weight.shape[0]
    ff_rows = shrink_weight.shape[0]
    chunks = FF // D
    total = piece * lax.axis_size("seq")
    start = lax.axis_index("seq") * piece
    info = jnp.concatenate(
        [jnp.stack([start, jnp.int32(total)]).astype(jnp.int32), seq_lengths.astype(jnp.int32)]
    )
    smalls = small_params.shape[1]

    packed = whole_call(
        pack_kernel,
        [((rows, 9 * D), BF16)],
        (merge_weight, expand_weight, shrink_weight),
        "pack",
        2,
        [pltpu.VMEM((GROUPS, ff_rows, LANES), F32)],
    )[0]
    packed = lax.all_gather(packed, axes, axis=0, tiled=True)
    early = jnp.concatenate(
        [qkv_weight.astype(BF16), jnp.pad(small_params.astype(BF16), ((0, 0), (0, LANES - smalls)))],
        axis=1,
    )
    last, ahead = (tokens[:, piece - WIN :], tokens[:, :WIN])
    beside = near_swap(last, ahead)
    across = diagonal_swap(ahead, last)
    early, done = gather_far(early)
    weight_a = gather_near(early[..., :CUT], done, "grp")
    weight_b = gather_near(early[..., CUT:], done, "seq")
    flat = tokens.reshape(seqs * piece, width)
    cot = (out_grad * answer_mask[:, :, None].astype(BF16)).reshape(seqs * piece, width)

    turned = flat.T
    old_rows = [entry[None, :] for entry in (qkv_rows, merge_rows, expand_rows, shrink_rows)]
    old_cols = [entry[None, :] for entry in (qkv_cols, merge_cols, expand_cols, shrink_cols)]
    turned, old_rows, old_cols, info = lax.optimization_barrier((turned, old_rows, old_cols, info))
    query, key, value, pool, rim_near, rim_across, vectors = project(
        info, beside, tokens, across, weight_a, weight_b
    )
    mixed, near_lse = near_attend(info, query, key, value)
    att, pkey, pvalue, far_lse = far_attend(
        info, query, pool, swap(rim_near, "seq", 0), across_swap(rim_across), mixed
    )
    att_flat = att.reshape(seqs * piece, width)
    (
        block_out, first_grad, hidden_low, active, up_grad, branch_grad, mixed_grad, att_grad, sums,
    ) = feed(flat, att_flat, cot, packed, vectors)

    shrink_local = outer(active, branch_grad).astype(BF16).reshape(chunks, devices, rows, D)
    merge_local = outer(att_flat, mixed_grad).astype(BF16).reshape(1, devices, rows, D)
    shrink_local, merge_local, up_grad = lax.optimization_barrier((shrink_local, merge_local, up_grad))
    shrink_chain = scatter_step(scatter_begin(shrink_local, late_steps(True), 1))
    merge_chain = scatter_step(scatter_begin(merge_local, late_steps(True), 1))
    late_chain = (jnp.concatenate([shrink_chain[0], merge_chain[0]], axis=0),) + shrink_chain[1:]
    expand_local = outer(hidden_low, up_grad).astype(BF16).reshape(devices, rows, FF)
    expand_chain = scatter_begin(expand_local, late_steps(False))
    chains = [late_chain, scatter_step(expand_chain)]

    def seq_rows(value, which):
        return value[which * piece : (which + 1) * piece]

    def advance(states, gate):
        return [scatter_step(state, gate) if len(state[2]) > 1 else state for state in states]

    att_grad = att_grad.reshape(seqs, piece, width)
    chains, info = after(chains, info)
    full_parts, parts, rims = ([], [], [])
    for which in range(seqs):
        parts.append(back(which, info, query, key, value, pkey, pvalue, att_grad, near_lse, far_lse))
        info, _ = lax.optimization_barrier((info, parts[which][0]))
    for which in range(seqs):
        query_part, near_grad, far_grad, rim_near, rim_across = parts[which]
        if which:
            rim_near, rim_across, _ = lax.optimization_barrier((rim_near, rim_across, rims[which - 1][3:]))
        rims.append((query_part, near_grad, far_grad, swap(rim_near, "seq", 0), across_swap(rim_across)))
    chains = advance(chains, (parts[-1][0], rims[0][3:]))
    chains, vectors = after(chains, vectors)
    before = None
    for which in range(seqs):
        full_part, *before = pool_back(
            which, seqs, info, rims[which], key, value, vectors, turned, before, sums
        )
        full_parts.append(full_part.reshape(piece, 3 * width))
        if which == 0:
            while len(chains[0][2]) > bits_of("seq") - 1:
                chains = advance(chains, (full_part, rims[-1][3:]))
            chains, vectors = after(chains, vectors)
    late_parts = [chains[0][0][j] for j in range(chunks + 1)] + [chains[1][0]]
    late_chain = (jnp.concatenate(late_parts, axis=-1),) + chains[1][1:]
    late_chain = advance([late_chain], None)[0]
    (late_chain,), before = after([late_chain], before)
    early_chains = [
        scatter_step(scatter_begin(entry.reshape(devices, rows, -1), scatter_steps(first)))
        for entry, first in zip(before, ("seq", "grp"))
    ]
    for _ in range(bits_of("grp")):
        early_chains = [scatter_step(state) for state in early_chains]
    early_chain = (
        jnp.concatenate([state[0] for state in early_chains], axis=-1),
    ) + early_chains[0][1:]
    late_sum = scatter_end(late_chain, early_chain[0])
    early_sum = scatter_end(early_chain)
    full_parts, _ = lax.optimization_barrier((full_parts, early_chain[0]))
    input_grad = jnp.stack(
        [
            seq_rows(first_grad, which)
            + nt(full_parts[which][:, :CUT], weight_a)
            + nt(full_parts[which][:, CUT:], weight_b[:, : 3 * D - CUT])
            for which in range(seqs)
        ]
    )

    masters = (qkv_weight, merge_weight, expand_weight, shrink_weight)
    base, expand_sum, shrink_sum = whole_call(
        late_kernel,
        [((1, 9 * D + LANES), F32), ((rows, FF), F32), ((ff_rows, D), F32)],
        (late_sum,) + tuple(old_rows),
        "late_stats",
        3,
        [pltpu.VMEM((GROUPS, ff_rows, LANES), F32)],
    )
    payload = whole_call(
        stats_kernel, [((1, 9 * D + LANES), F32)], (early_sum, base), "stats", 1
    )[0]
    payload = summed_all(payload)
    outs = [((1, 1), F32)]
    for master in masters:
        high, wide = master.shape
        outs += [((high, wide), F32), ((1, high), F32), ((wide // LANES, LANES), F32), ((high, wide), F32)]
        outs += [((high, wide), BF16)]
    outs += [((smalls, rows), F32)] * 3 + [((smalls, rows), BF16)]
    fresh = whole_call(
        update_kernel,
        outs,
        (payload, early_sum, late_sum, expand_sum, shrink_sum)
        + tuple(old_rows)
        + tuple(old_cols)
        + masters
        + (small_params.T, small_moment.T),
        "update",
        5,
    )
    results = []
    for index in range(4):
        grad, rows_new, cols_new, new, low_new = fresh[1 + 5 * index : 6 + 5 * index]
        results += [grad, rows_new.reshape(-1), cols_new.reshape(-1), new, low_new]
    return (
        block_out.reshape(seqs, piece, width),
        input_grad,
        fresh[0].reshape(()),
        *results,
        *[entry.T for entry in fresh[21:]],
    )


def solution(mesh):
    whole = ("seq", "grp")
    matrix = P(whole, None)
    vector = P(whole)
    in_specs = (
        P("grp", "seq", None),
        P("grp"),
        P("grp", "seq"),
        P("grp", "seq", None),
        *[matrix] * 5,
        *[vector, P()] * 4,
        matrix,
    )
    out_specs = (
        P("grp", "seq", None),
        P("grp", "seq", None),
        P(),
        *[matrix, vector, P(), matrix, matrix] * 4,
        *[matrix] * 4,
    )
    return jax.shard_map(local, mesh=mesh, in_specs=in_specs, out_specs=out_specs, check_vma=False)
```

```python
import functools

import jax
import jax.numpy as jnp
from jax import lax
from jax.experimental import pallas as pl
from jax.experimental.pallas import tpu as pltpu
from jax.sharding import PartitionSpec as P

D = 768
HEAD_DIM = 64
FF = 3072
WIN = 64
PWIN = 64
TILE = 128
LANES = 128
NEAR = TILE + 2 * WIN
FAR = TILE // 4 + 2 * PWIN
GROUPS = D // LANES

EPS_NORM = 1e-05
EPS_FACTOR = 1e-30
DECAY = 0.5
RATE = 0.08
CLIP = 1.0
NEG = -1e30
BIG = 3e38
SCALE = HEAD_DIM ** (-0.5)

TAIL_STEP = 0.31
TAIL = (
    0.12367211422929353,
    0.12367030785161068,
    0.11185922254891491,
    0.08691510254396204,
    0.06423540557821411,
    -0.014525970624111314,
    0.08814037010576171,
    -0.154963171944524,
    0.08860162861073731,
    -0.017604979368020673,
)
INV_ROOT = 0.3989422804014327

F32 = jnp.float32
BF16 = jnp.bfloat16
CUT = 1280
TOGETHER = 3
BUFFERS = 4
BACK_TOGETHER = 2
VMEM_LIMIT = 60 * 1024 * 1024


def nn(left, right):
    return jnp.dot(left, right, preferred_element_type=F32)


def nt(left, right):
    return lax.dot_general(left, right, (((1,), (1,)), ((), ())), preferred_element_type=F32)


def outer(left, right):
    return lax.dot_general(left, right, (((0,), (0,)), ((), ())), preferred_element_type=F32)


def from_behind(value, axis, by):
    size = lax.axis_size(axis)
    pairs = [(i, i + by) for i in range(size) if 0 <= i + by < size]
    return lax.ppermute(value, axis, pairs)


def params(**extra):
    return pltpu.CompilerParams(vmem_limit_bytes=VMEM_LIMIT, **extra)


def cost(micros):
    return pl.CostEstimate(flops=int(micros * 8e8), bytes_accessed=0, transcendentals=0)


def fixed(shape):
    zeros = (0,) * len(shape)
    return pl.BlockSpec(shape, lambda *_: zeros, pipeline_mode=pl.Buffered(1))


def lanes_of(index, width=LANES):
    return slice(index * width, (index + 1) * width)


def near_cap(start, total, length, first):
    key = start - WIN + first + lax.broadcasted_iota(jnp.int32, (NEAR, TILE), 0)
    query = start + first + lax.broadcasted_iota(jnp.int32, (NEAR, TILE), 1)
    near = (jnp.abs(query - key) <= WIN) & (key >= 0) & (key < total)
    return jnp.where(near & ((key < length) | (key == query)), BIG, NEG)


def far_cap(start, total, length, first):
    pooled = start // 4 - PWIN + first // 4 + lax.broadcasted_iota(jnp.int32, (FAR, TILE), 0)
    coarse = (start + first + lax.broadcasted_iota(jnp.int32, (FAR, TILE), 1)) // 4
    far = (jnp.abs(coarse - pooled) <= PWIN) & (pooled >= 0) & (pooled < total // 4)
    return jnp.where(far & ((4 * pooled < length) | (pooled == coarse)), BIG, NEG)


def split_pair(pair):
    lane = lax.broadcasted_iota(jnp.int32, pair.shape, 1)
    zero = jnp.zeros_like(pair)
    return jnp.concatenate(
        [jnp.where(lane < HEAD_DIM, pair, zero), jnp.where(lane < HEAD_DIM, zero, pair)], axis=0
    )


LEVELS = ((0, NEAR), (NEAR, NEAR + FAR))


def join_pair(stacked):
    row = lax.broadcasted_iota(jnp.int32, (LANES, TILE), 0)
    return jnp.where(row < HEAD_DIM, stacked[:, :TILE], stacked[:, TILE:])


def project_kernel(
    info, beside, own, across, weight_a, weight_b, query, key, value, pool, rim_near, rim_across,
    vectors, wide,
):
    piece = own.shape[1]
    pools = piece // 4
    even = (info[0] // piece) % 2 == 0
    low = jnp.where(even, across[0], beside[0])
    high = jnp.where(even, beside[0], across[0])
    small = weight_b[:, 3 * D - CUT :].astype(F32).T
    vectors[...] = small[:16]
    taps = small[4:14]

    def weight_chunk(chunk):
        if chunk < CUT // 256:
            return weight_a[:, lanes_of(chunk, 256)]
        return weight_b[:, lanes_of(chunk - CUT // 256, 256)]

    for chunk in range(3):
        cols = lanes_of(chunk, 256)
        query[0, :, cols] = (nn(own[0], weight_chunk(chunk)) * SCALE).astype(BF16)
    for chunk in range(6):
        target = key if chunk < 3 else value
        cols = lanes_of(chunk % 3, 256)
        block = weight_chunk(3 + chunk)
        for source, base, count in ((low, 0, WIN), (own[0], WIN, piece), (high, WIN + piece, WIN)):
            rounded = nn(source, block).astype(BF16)
            held = rounded.astype(F32)
            wide[2 * chunk, base : base + count, :] = held[:, :LANES]
            wide[2 * chunk + 1, base : base + count, :] = held[:, LANES:]
            target[0, base : base + count, cols] = rounded
    for group in range(2 * GROUPS):
        part = group // GROUPS
        cols = lanes_of(group % GROUPS)
        pooled = None
        for tap in range(5):
            term = taps[5 * part + tap : 5 * part + tap + 1, cols] * wide[
                group, pl.ds(WIN - 2 + tap, pools, stride=4), :
            ]
            pooled = term if pooled is None else pooled + term
        pooled = pooled.astype(BF16)
        pool[0, part, :, cols] = pooled
        first, last = (pooled[:PWIN], pooled[pools - PWIN :])
        rim_near[0, part, :, cols] = jnp.where(even, last, first)
        rim_across[0, part, :, cols] = jnp.where(even, first, last)


def level_mixed(queries, keys, values, cap, lse, tile, pairs):
    heads = [(at, head) for at in range(len(pairs)) for head in range(2)]
    scores = [nt(keys[at], queries[at][head * TILE : (head + 1) * TILE]) for at, head in heads]
    scores = [jnp.minimum(entry, cap[...]) for entry in scores]
    tops = [jnp.max(entry, axis=0, keepdims=True) for entry in scores]
    raised = [jnp.exp(entry - top) for entry, top in zip(scores, tops)]
    norms = [jnp.sum(entry, axis=0, keepdims=True) for entry in raised]
    for (at, head), top, norm in zip(heads, tops, norms):
        lse[0, tile, pairs[at] : pairs[at] + 1, lanes_of(head)] = top + jnp.log(norm)
    probs = [(entry * (1.0 / norm)).astype(BF16) for entry, norm in zip(raised, norms)]
    turned = [entry.T for entry in values]
    mixed = [
        nn(entry, jnp.concatenate(probs[2 * at : 2 * at + 2], axis=1)) for at, entry in enumerate(turned)
    ]
    return [join_pair(entry).T for entry in mixed]


def near_kernel(info, query, key, value, mixed, lse, cap):
    piece = query.shape[1]
    which = pl.program_id(0)
    start, total, length = (info[0], info[1], info[2 + which])

    def tile_step(tile, carry):
        first = pl.multiple_of(tile * TILE, TILE)
        cap[...] = near_cap(start, total, length, first)
        for begin in range(0, GROUPS, TOGETHER):
            pairs = range(begin, begin + TOGETHER)
            queries = [split_pair(query[0, pl.ds(first, TILE), lanes_of(pair)]) for pair in pairs]
            keys = [key[0, pl.ds(first, NEAR), lanes_of(pair)] for pair in pairs]
            values = [value[0, pl.ds(first, NEAR), lanes_of(pair)] for pair in pairs]
            parts = level_mixed(queries, keys, values, cap, lse, tile, pairs)
            for pair, part in zip(pairs, parts):
                mixed[0, pl.ds(first, TILE), lanes_of(pair)] = part
        return carry

    lax.fori_loop(0, piece // TILE, tile_step, 0)


def far_kernel(info, query, pool, beside, across, mixed, att, pkey, pvalue, lse, cap):
    piece = query.shape[1]
    pools = piece // 4
    which = pl.program_id(0)
    start, total, length = (info[0], info[1], info[2 + which])
    even = (start // piece) % 2 == 0
    for part, target in enumerate((pkey, pvalue)):
        target[0, :PWIN, :] = jnp.where(even, across[0, part], beside[0, part])
        target[0, PWIN : PWIN + pools, :] = pool[0, part]
        target[0, PWIN + pools :, :] = jnp.where(even, beside[0, part], across[0, part])

    def tile_step(tile, carry):
        first = pl.multiple_of(tile * TILE, TILE)
        coarse = pl.multiple_of(tile * (TILE // 4), TILE // 4)
        cap[...] = far_cap(start, total, length, first)
        for begin in range(0, GROUPS, TOGETHER):
            pairs = range(begin, begin + TOGETHER)
            queries = [split_pair(query[0, pl.ds(first, TILE), lanes_of(pair)]) for pair in pairs]
            keys = [pkey[0, pl.ds(coarse, FAR), lanes_of(pair)] for pair in pairs]
            values = [pvalue[0, pl.ds(coarse, FAR), lanes_of(pair)] for pair in pairs]
            parts = level_mixed(queries, keys, values, cap, lse, tile, pairs)
            for pair, part in zip(pairs, parts):
                place = (0, pl.ds(first, TILE), lanes_of(pair))
                att[place] = (mixed[place] + part).astype(BF16)
        return carry

    lax.fori_loop(0, piece // TILE, tile_step, 0)


def per_seq(body, operands, shapes, micros, name, shared=0, common=(), scratch=()):
    info, *rest = operands
    seqs = rest[0].shape[0]
    split = len(rest) - shared

    def seq_block(shape):
        return pl.BlockSpec((1,) + tuple(shape), lambda s: (s,) + (0,) * len(shape))

    return pl.pallas_call(
        body,
        grid=(seqs,),
        in_specs=[pl.BlockSpec(memory_space=pltpu.SMEM)]
        + [seq_block(entry.shape[1:]) for entry in rest[:split]]
        + [fixed(entry.shape) for entry in rest[split:]],
        out_specs=[seq_block(shape) for shape, _ in shapes]
        + [pl.BlockSpec(shape, lambda s: (0,) * len(shape)) for shape, _ in common],
        out_shape=[jax.ShapeDtypeStruct((seqs,) + shape, dtype) for shape, dtype in shapes]
        + [jax.ShapeDtypeStruct(shape, dtype) for shape, dtype in common],
        scratch_shapes=list(scratch),
        compiler_params=params(),
        cost_estimate=cost(micros),
        name=name,
    )(*operands)


def project(info, beside, own, across, weight_a, weight_b):
    _, piece, width = own.shape
    extent, pools = (piece + 2 * WIN, piece // 4)
    return per_seq(
        project_kernel,
        (info, beside, own, across, weight_a, weight_b),
        [
            ((piece, width), BF16),
            ((extent, width), BF16),
            ((extent, width), BF16),
            ((2, pools, width), BF16),
            ((2, PWIN, width), BF16),
            ((2, PWIN, width), BF16),
        ],
        10,
        "project",
        shared=2,
        common=[((16, width), F32)],
        scratch=[pltpu.VMEM((2 * GROUPS, extent, LANES), F32)],
    )


def near_attend(info, query, key, value):
    _, piece, width = query.shape
    return per_seq(
        near_kernel,
        (info, query, key, value),
        [((piece, width), F32), ((piece // TILE, 8, 2 * TILE), F32)],
        30,
        "near",
        scratch=[pltpu.VMEM((NEAR, TILE), F32)],
    )


def far_attend(info, query, pool, beside, across, mixed):
    _, piece, width = query.shape
    pools = piece // 4 + 2 * PWIN
    return per_seq(
        far_kernel,
        (info, query, pool, beside, across, mixed),
        [
            ((piece, width), BF16),
            ((pools, width), BF16),
            ((pools, width), BF16),
            ((piece // TILE, 8, 2 * TILE), F32),
        ],
        12,
        "far",
        scratch=[pltpu.VMEM((FAR, TILE), F32)],
    )


def layer_stats(values):
    centred = values - jnp.mean(values, axis=-1, keepdims=True)
    inverse = lax.rsqrt(jnp.mean(centred * centred, axis=-1, keepdims=True) + EPS_NORM)
    return (centred * inverse, inverse)


def layer_back(grad, normed, inverse):
    return inverse * (
        grad
        - jnp.mean(grad, axis=-1, keepdims=True)
        - normed * jnp.mean(grad * normed, axis=-1, keepdims=True)
    )


def gelu_parts(up):
    size = jnp.abs(up)
    bell = jnp.exp(-0.5 * (up * up))
    near = 1.0 / (1.0 + TAIL_STEP * size)
    poly = jnp.full_like(up, TAIL[-1])
    for factor in TAIL[-2::-1]:
        poly = poly * near + factor
    tail = bell * (near * poly)
    phi = jnp.where(up >= 0.0, 1.0 - tail, tail)
    return (up * phi, phi + up * (bell * INV_ROOT))


def feed_kernel(
    tokens, att, cot, packed, vectors, block_out, first_grad, hidden_low, active,
    up_grad, branch_grad, mixed_grad, att_grad, sums, slope,
):
    step = pl.program_id(0)
    gain_one, bias_one, gain_two, bias_two = [vectors[i : i + 1, :] for i in range(4)]
    def merge():
        return packed[:, :D]

    def expand(chunk):
        return packed[:, lanes_of(1 + chunk, D)]

    def shrink(chunk):
        return packed[:, lanes_of(1 + FF // D + chunk, D)]

    first_norm, first_inv = layer_stats(tokens[...].astype(F32) + nn(att[...], merge()))
    hidden = first_norm * gain_one + bias_one
    low = hidden.astype(BF16)
    hidden_low[...] = low
    branch = None
    for chunk in range(FF // D):
        cols = lanes_of(chunk, D)
        wide, steep = gelu_parts(nn(low, expand(chunk)))
        narrow = wide.astype(BF16)
        active[:, cols] = narrow
        slope[:, cols] = steep
        term = nn(narrow, shrink(chunk))
        branch = term if branch is None else branch + term
    second_norm, second_inv = layer_stats(hidden + branch)
    block_out[...] = (second_norm * gain_two + bias_two).astype(BF16)
    cotangent = cot[...].astype(F32)

    @pl.when(step == 0)
    def clear():
        sums[...] = jnp.zeros_like(sums)

    def add_sum(row, value):
        sums[row : row + 1, :] += jnp.sum(value, axis=0, keepdims=True)

    add_sum(2, cotangent * second_norm)
    add_sum(3, cotangent)
    second_grad = layer_back(cotangent * gain_two, second_norm, second_inv)
    second_low = second_grad.astype(BF16)
    branch_grad[...] = second_low
    feed = None
    for chunk in range(FF // D):
        cols = lanes_of(chunk, D)
        narrow = (nt(second_low, shrink(chunk)) * slope[:, cols]).astype(BF16)
        up_grad[:, cols] = narrow
        term = nt(narrow, expand(chunk))
        feed = term if feed is None else feed + term
    hidden_grad = second_grad + feed.astype(BF16).astype(F32)
    add_sum(0, hidden_grad * first_norm)
    add_sum(1, hidden_grad)
    grad = layer_back(hidden_grad * gain_one, first_norm, first_inv)
    first_grad[...] = grad
    grad_low = grad.astype(BF16)
    mixed_grad[...] = grad_low
    att_grad[...] = nt(grad_low, merge()).astype(BF16)


def feed(tokens, att, cot, packed, vectors):
    rows, width = tokens.shape
    block = 256
    ff = FF

    def row_block(cols):
        return pl.BlockSpec((block, cols), lambda i: (i, 0))

    outs = [
        (width, BF16),
        (width, F32),
        (width, BF16),
        (ff, BF16),
        (ff, BF16),
        (width, BF16),
        (width, BF16),
        (width, BF16),
    ]
    return pl.pallas_call(
        feed_kernel,
        grid=(rows // block,),
        in_specs=[row_block(width)] * 3
        + [fixed(packed.shape), fixed(vectors.shape)],
        out_specs=[row_block(cols) for cols, _ in outs] + [pl.BlockSpec((8, width), lambda i: (0, 0))],
        out_shape=[jax.ShapeDtypeStruct((rows, cols), dtype) for cols, dtype in outs]
        + [jax.ShapeDtypeStruct((8, width), F32)],
        scratch_shapes=[pltpu.VMEM((block, ff), F32)],
        compiler_params=params(),
        cost_estimate=cost(48),
        name="feed",
    )(tokens, att, cot, packed, vectors)


def back_kernel(
    which, info, query, key, value, pkey, pvalue, grad, near_lse, far_lse, query_grad, near_grad,
    far_grad, rim_near, rim_across, caps,
):
    piece = query.shape[1]
    even = (info[0] // piece) % 2 == 0
    start, total, length = (info[0], info[1], info[2 + which])
    near_grad[...] = jnp.zeros_like(near_grad)
    far_grad[...] = jnp.zeros_like(far_grad)

    def tile_step(tile, carry):
        first = pl.multiple_of(tile * TILE, TILE)
        coarse = pl.multiple_of(tile * (TILE // 4), TILE // 4)
        for cap, (begin, end) in zip((near_cap, far_cap), LEVELS):
            block = cap(start, total, length, first)
            caps[begin:end, :TILE] = block
            caps[begin:end, TILE:] = block
        near_rows, far_rows = (pl.ds(first, NEAR), pl.ds(coarse, FAR))
        place = pl.ds(first, TILE)
        for start_pair in range(0, GROUPS, BACK_TOGETHER):
            pairs = range(start_pair, start_pair + BACK_TOGETHER)
            many = range(BACK_TOGETHER)
            spans = [lanes_of(pair) for pair in pairs]
            queries = [split_pair(query[0, place, cols]) for cols in spans]
            grads = [split_pair(grad[0, place, cols]) for cols in spans]
            keys = [
                jnp.concatenate([key[0, near_rows, cols], pkey[0, far_rows, cols]], axis=0)
                for cols in spans
            ]
            values = [
                jnp.concatenate([value[0, near_rows, cols], pvalue[0, far_rows, cols]], axis=0)
                for cols in spans
            ]
            scores = [nt(keys[at], queries[at]) for at in many]
            prob_grads = [nt(values[at], grads[at]) for at in many]
            probs = [[] for _ in many]
            score_grads = [[] for _ in many]
            for level, (begin, end) in enumerate(LEVELS):
                lse = (near_lse, far_lse)[level]
                exact_probs = [
                    jnp.exp(
                        jnp.minimum(scores[at][begin:end], caps[begin:end, :])
                        - lse[0, tile, pairs[at] : pairs[at] + 1, :]
                    )
                    for at in many
                ]
                weighted = [exact_probs[at] * prob_grads[at][begin:end] for at in many]
                inner = [jnp.sum(entry, axis=0, keepdims=True) for entry in weighted]
                for at in many:
                    score_grads[at].append((weighted[at] - exact_probs[at] * inner[at]).astype(BF16))
                    probs[at].append(exact_probs[at].astype(BF16))
            score_grads = [jnp.concatenate(entry, axis=0) for entry in score_grads]
            key_parts = [nn(score_grads[at], queries[at]) for at in many]
            value_parts = [nn(jnp.concatenate(probs[at], axis=0), grads[at]) for at in many]
            turned = [entry.T for entry in keys]
            query_parts = [nn(turned[at], score_grads[at]) for at in many]
            for at, cols in enumerate(spans):
                near_grad[0, 0, near_rows, cols] += key_parts[at][:NEAR]
                far_grad[0, 0, far_rows, cols] += key_parts[at][NEAR:]
                near_grad[0, 1, near_rows, cols] += value_parts[at][:NEAR]
                far_grad[0, 1, far_rows, cols] += value_parts[at][NEAR:]
                query_grad[0, place, cols] = (join_pair(query_parts[at]) * SCALE).T.astype(BF16)
        return carry

    lax.fori_loop(0, piece // TILE, tile_step, 0)
    pools = far_grad.shape[2]
    blank = jnp.zeros((16, far_grad.shape[3]), BF16)
    for part in range(2):
        low = [near_grad[0, part, :WIN, :], far_grad[0, part, : PWIN + 16, :]]
        low = [entry.astype(BF16) for entry in low]
        high = [near_grad[0, part, WIN + piece :, :], far_grad[0, part, pools - PWIN :, :]]
        high = [entry.astype(BF16) for entry in high]

        @pl.when(even)
        def even_side():
            rim_near[0, part, :WIN, :] = high[0]
            rim_near[0, part, WIN : WIN + PWIN, :] = high[1]
            rim_near[0, part, WIN + PWIN :, :] = blank
            rim_across[0, part, :WIN, :] = low[0]
            rim_across[0, part, WIN:, :] = low[1]

        @pl.when(jnp.logical_not(even))
        def odd_side():
            rim_across[0, part, :WIN, :] = high[0]
            rim_across[0, part, WIN : WIN + PWIN, :] = high[1]
            rim_across[0, part, WIN + PWIN :, :] = blank
            rim_near[0, part, :WIN, :] = low[0]
            rim_near[0, part, WIN:, :] = low[1]


def seq_slice(shape, which):
    return pl.BlockSpec((1,) + tuple(shape[1:]), lambda _: (which,) + (0,) * (len(shape) - 1))


def back(which, info, query, key, value, pkey, pvalue, grad, near_lse, far_lse):
    _, piece, width = query.shape
    extent, pools = (key.shape[1], pkey.shape[1])
    operands = (query, key, value, pkey, pvalue, grad, near_lse, far_lse)
    shapes = [
        ((1, piece, width), BF16),
        ((1, 2, extent, width), F32),
        ((1, 2, pools, width), F32),
        ((1, 2, WIN + PWIN + 16, width), BF16),
        ((1, 2, WIN + PWIN + 16, width), BF16),
    ]
    return pl.pallas_call(
        functools.partial(back_kernel, which),
        grid=(1,),
        in_specs=[pl.BlockSpec(memory_space=pltpu.SMEM)]
        + [seq_slice(entry.shape, which) for entry in operands],
        out_specs=[seq_slice(shape, 0) for shape, _ in shapes],
        out_shape=[jax.ShapeDtypeStruct(shape, dtype) for shape, dtype in shapes],
        scratch_shapes=[pltpu.VMEM((NEAR + FAR, 2 * TILE), F32)],
        compiler_params=params(),
        cost_estimate=cost(0.01 if which else 30),
        name="back",
    )(info, *operands)


def pool_back_kernel(
    first, last, info, query_grad, near_grad, far_grad, beside, across, key, value, taps, turned, *rest
):
    rest = list(rest)
    before, taps_before = (None, None) if first else (rest.pop(0), rest.pop(0))
    sums = rest.pop(0) if last else None
    full_grad = rest.pop(0)
    outs = [rest.pop(0), rest.pop(0)]
    held_all, spread_all, window_all, taps_grad = rest
    piece = full_grad.shape[1]
    pools = piece // 4
    even = (info[0] // piece) % 2 == 0
    full_grad[0, :, :D] = query_grad[0]
    if first:
        taps_grad[...] = jnp.zeros_like(taps_grad)
    else:
        taps_grad[...] = taps_before[...]

    def product(chunk):
        cols = lanes_of(chunk, 256)
        total = nn(turned[...], full_grad[0, :, cols])
        if not first:
            total = total + before[:, cols]
        if not last:
            outs[0][:, cols] = total
        elif chunk < CUT // 256:
            outs[0][:, cols] = total.astype(BF16)
        else:
            outs[1][:, lanes_of(chunk - CUT // 256, 256)] = total.astype(BF16)

    for group in range(2 * GROUPS):
        if group % 4 == 0:
            product(group // 4)
        held, spread, window = [entry.at[group % BUFFERS] for entry in (held_all, spread_all, window_all)]
        part = group // GROUPS
        cols = lanes_of(group % GROUPS)
        source = key if part == 0 else value
        pair = [entry[0, part, :, cols].astype(F32) for entry in (beside, across)]
        from_high = jnp.where(even, pair[0], pair[1])
        from_low = jnp.where(even, pair[1], pair[0])
        tap = [taps[4 + 5 * part + t : 5 + 5 * part + t, cols] for t in range(5)]
        held[0:pools, :] = far_grad[0, part, PWIN : PWIN + pools, cols]
        held[0:PWIN, :] += from_low[WIN : WIN + PWIN]
        held[pools - PWIN : pools, :] += from_high[WIN : WIN + PWIN]
        held[pools : pools + 16, :] = (
            far_grad[0, part, PWIN + pools : PWIN + pools + 16, cols] + from_high[WIN + PWIN :]
        )
        now = held[0:pools, :]
        later = held[1 : pools + 1, :]
        spread[pl.ds(0, pools, stride=4), :] = tap[2] * now
        spread[pl.ds(1, pools, stride=4), :] = tap[3] * now
        spread[pl.ds(2, pools, stride=4), :] = tap[4] * now + tap[0] * later
        spread[pl.ds(3, pools, stride=4), :] = tap[1] * later
        spread[0:WIN, :] += from_low[:WIN]
        spread[piece - WIN : piece, :] += from_high[:WIN]
        total = near_grad[0, part, WIN : WIN + piece, cols] + spread[...]
        full_grad[0, :, lanes_of(GROUPS + group)] = total.astype(BF16)
        window[...] = source[0, WIN - 16 : WIN + piece + 16, cols].astype(F32)
        for t in range(5):
            row = 5 * part + t
            taps_grad[row : row + 1, cols] += jnp.sum(
                now * window[pl.ds(14 + t, pools, stride=4), :], axis=0, keepdims=True
            )
        if group % 2 == 1:
            product((GROUPS + group) // 2)
    if last:
        zeros = jnp.zeros((LANES - 14, D), F32)
        small = jnp.concatenate([sums[0:4, :], taps_grad[0:10, :], zeros], axis=0)
        outs[1][:, 3 * D - CUT :] = small.T.astype(BF16)
    else:
        outs[1][...] = taps_grad[...]


def pool_back(which, seqs, info, entries, key, value, taps, turned, before, sums):
    near_grad = entries[1]
    _, _, extent, width = near_grad.shape
    piece = extent - 2 * WIN
    pools = piece // 4
    first, last = (which == 0, which == seqs - 1)
    extra = (() if first else tuple(before)) + ((sums,) if last else ())
    if last:
        outs = [((width, CUT), BF16), ((width, 3 * width + LANES - CUT), BF16)]
    else:
        outs = [((width, 3 * width), F32), ((16, width), F32)]
    return pl.pallas_call(
        functools.partial(pool_back_kernel, first, last),
        grid=(1,),
        in_specs=[pl.BlockSpec(memory_space=pltpu.SMEM)]
        + [seq_slice(entry.shape, 0) for entry in entries]
        + [seq_slice(entry.shape, which) for entry in (key, value)]
        + [fixed(taps.shape), pl.BlockSpec((width, piece), lambda _: (0, which))]
        + [fixed(entry.shape) for entry in extra],
        out_specs=[seq_slice((1, piece, 3 * width), 0)] + [fixed(shape) for shape, _ in outs],
        out_shape=[jax.ShapeDtypeStruct((1, piece, 3 * width), BF16)]
        + [jax.ShapeDtypeStruct(shape, dtype) for shape, dtype in outs],
        scratch_shapes=[
            pltpu.VMEM((BUFFERS, pools + 16, LANES), F32),
            pltpu.VMEM((BUFFERS, piece, LANES), F32),
            pltpu.VMEM((BUFFERS, piece + 32, LANES), F32),
            pltpu.VMEM((16, width), F32),
        ],
        compiler_params=params(),
        cost_estimate=cost(0.01 if which else 30),
        name="pool_back",
    )(info, *entries, key, value, taps, turned, *extra)


def unmix(width):
    row = lax.broadcasted_iota(jnp.int32, (4 * width, 4 * width), 0)
    col = lax.broadcasted_iota(jnp.int32, (4 * width, 4 * width), 1)
    return jnp.where(row == 4 * (col % width) + col // width, 1.0, 0.0)


def exact(left, right):
    return jnp.dot(left, right, precision=lax.Precision.HIGHEST, preferred_element_type=F32)


def exact_nt(left, right):
    return lax.dot_general(
        left, right, (((1,), (1,)), ((), ())), precision=lax.Precision.HIGHEST, preferred_element_type=F32
    )


def pack_kernel(merge, expand, shrink, out, held):
    rows = merge.shape[0]
    mixer = unmix(LANES).astype(BF16)
    out[:, :D] = merge[...].astype(BF16)
    for group in range(FF // (4 * LANES)):
        block = nn(expand[:, lanes_of(group, 4 * LANES)].astype(BF16), mixer).astype(BF16)
        for j in range(4):
            first = D + j * D + group * LANES
            out[:, first : first + LANES] = block[:, lanes_of(j)]
    for group in range(GROUPS):
        held[group] = shrink[:, lanes_of(group)]
        for j in range(4):
            first = (5 + j) * D + group * LANES
            out[:, first : first + LANES] = held[group, pl.ds(j, rows, stride=4), :].astype(BF16)


def squares(block):
    return jnp.sum(block * block, axis=0, keepdims=True)


def late_kernel(late, *rest):
    olds, (out, expand, shrink, held) = (rest[:4], rest[4:])
    rows = late.shape[0]
    mixer = unmix(LANES).astype(BF16)
    for group in range(FF // (4 * LANES)):
        pieces = []
        for j in range(4):
            first = (5 + j) * D + group * LANES
            pieces.append(late[:, first : first + LANES])
        left = jnp.concatenate(pieces, axis=1)
        total = None
        for _ in range(3):
            top = left.astype(BF16)
            left = left - top.astype(F32)
            term = nt(top, mixer)
            total = term if total is None else total + term
        expand[:, lanes_of(group, 4 * LANES)] = total
    for group in range(GROUPS):
        for j in range(4):
            held[group, pl.ds(j, rows, stride=4), :] = late[:, lanes_of(j * GROUPS + group)]
        shrink[:, lanes_of(group)] = held[group]
    out[:, : 3 * D] = jnp.zeros((1, 3 * D), F32)
    out[:, 3 * D : 4 * D] = squares(late[:, 4 * D : 5 * D])
    for j in range(FF // D):
        out[:, (4 + j) * D : (5 + j) * D] = squares(expand[:, lanes_of(j, D)])
    out[:, 8 * D : 9 * D] = squares(shrink[...])
    lane = lax.broadcasted_iota(jnp.int32, (1, LANES), 1)
    tail = jnp.zeros((1, LANES), F32)
    for slot, entry in enumerate(olds):
        tail = jnp.where(lane == slot + 1, jnp.sum(entry[...], axis=1, keepdims=True), tail)
    out[:, 9 * D :] = tail


def stats_kernel(own, one, two, three, base, out, early):
    early[...] = sum(entry[...].astype(F32) for entry in (own, one, two, three))
    out[:, : 3 * D] = squares(early[:, : 3 * D])
    out[:, 3 * D : 9 * D] = base[:, 3 * D : 9 * D]
    lane = lax.broadcasted_iota(jnp.int32, (1, LANES), 1)
    small = jnp.sum(squares(early[:, 3 * D :]), axis=1, keepdims=True)
    out[:, 9 * D :] = base[:, 9 * D :] + jnp.where(lane == 0, small, 0.0)


def update_kernel(
    total, early, late, expand, shrink, rows_0, rows_1, rows_2, rows_3, cols_0, cols_1,
    cols_2, cols_3, weight_0, weight_1, weight_2, weight_3, small, moment,
    norm_out, grad_0, rows_new_0, cols_new_0, new_0, low_0, grad_1, rows_new_1, cols_new_1, new_1,
    low_1, grad_2, rows_new_2, cols_new_2, new_2, low_2, grad_3, rows_new_3, cols_new_3, new_3,
    low_3, small_grad, moment_new, small_new, small_low,
):
    smalls = small.shape[0]
    tail = total[:, 9 * D :]
    spans = ((0, 3 * D), (3 * D, 4 * D), (4 * D, 8 * D), (8 * D, 9 * D))
    matrix_sums = [jnp.sum(total[:, a:b], axis=1, keepdims=True) for a, b in spans]
    norm = jnp.sqrt(matrix_sums[0] + matrix_sums[1] + matrix_sums[2] + matrix_sums[3] + tail[:, 0:1])
    clip = CLIP / jnp.maximum(norm, CLIP)
    norm_out[...] = norm
    parts = (
        [early[:, lanes_of(j, D)] for j in range(3)],
        [late[:, 4 * D : 5 * D]],
        [expand[:, lanes_of(j, D)] for j in range(FF // D)],
        [shrink[...]],
    )
    heights = (D, D, D, FF)
    olds = (
        (rows_0, cols_0, weight_0, grad_0, rows_new_0, cols_new_0, new_0, low_0),
        (rows_1, cols_1, weight_1, grad_1, rows_new_1, cols_new_1, new_1, low_1),
        (rows_2, cols_2, weight_2, grad_2, rows_new_2, cols_new_2, new_2, low_2),
        (rows_3, cols_3, weight_3, grad_3, rows_new_3, cols_new_3, new_3, low_3),
    )
    for index in range(4):
        old_rows, old_cols, weight, grad, rows_new, cols_new, new, low = olds[index]
        begin, end = spans[index]
        width, height = (end - begin, heights[index])
        mean_cols = (total[:, begin:end] * clip) * clip / height + EPS_FACTOR
        fresh_cols = DECAY * old_cols[...] + (1.0 - DECAY) * mean_cols
        for group in range(width // LANES):
            cols_new[group : group + 1, :] = fresh_cols[:, lanes_of(group)]
        squared = sum(part * part for part in parts[index])
        row_sum = exact_nt(jnp.ones((8, D), F32), squared)[:1]
        mean_rows = (row_sum * clip) * clip / width + EPS_FACTOR
        fresh_rows = DECAY * old_rows[...] + (1.0 - DECAY) * mean_rows
        rows_new[...] = fresh_rows
        row = lax.broadcasted_iota(jnp.int32, (weight.shape[0], weight.shape[0]), 0)
        col = lax.broadcasted_iota(jnp.int32, (weight.shape[0], weight.shape[0]), 1)
        down = jnp.sum(jnp.where(row == col, fresh_rows, 0.0), axis=1, keepdims=True)
        mean_all = (matrix_sums[index] * clip) * clip / (width * height) + EPS_FACTOR
        row_mean = DECAY * (tail[:, 1 + index : 2 + index] / height) + (1.0 - DECAY) * mean_all
        for j, part in enumerate(parts[index]):
            cols = lanes_of(j, D)
            clipped = part * clip
            grad[:, cols] = clipped
            estimate = down * fresh_cols[:, cols] / row_mean
            fresh = weight[:, cols] - RATE * clipped * lax.rsqrt(estimate)
            new[:, cols] = fresh
            low[:, cols] = fresh.astype(BF16)
    row = lax.broadcasted_iota(jnp.int32, (16, LANES), 0)
    col = lax.broadcasted_iota(jnp.int32, (16, LANES), 1)
    turned = exact_nt(jnp.where(row == col, 1.0, 0.0), early[:, 3 * D :])
    clipped = turned[:smalls] * clip
    small_grad[...] = clipped
    fresh_moment = DECAY * moment[...] + (1.0 - DECAY) * (clipped * clipped + EPS_FACTOR)
    moment_new[...] = fresh_moment
    fresh = small[...] - RATE * clipped * lax.rsqrt(fresh_moment)
    small_new[...] = fresh
    small_low[...] = fresh.astype(BF16)


def whole_call(body, outs, operands, name, micros, scratch=()):
    return pl.pallas_call(
        body,
        out_shape=[jax.ShapeDtypeStruct(shape, dtype) for shape, dtype in outs],
        in_specs=[pl.BlockSpec(memory_space=pltpu.VMEM)] * len(operands),
        out_specs=[pl.BlockSpec(memory_space=pltpu.VMEM)] * len(outs),
        scratch_shapes=list(scratch),
        compiler_params=params(),
        cost_estimate=cost(micros),
        name=name,
    )(*operands)


def swap(value, axis, bit):
    size = lax.axis_size(axis)
    return lax.ppermute(value, axis, [(i, i ^ (1 << bit)) for i in range(size)])


def bits_of(axis):
    return lax.axis_size(axis).bit_length() - 1


def side(axis, bit):
    return (lax.axis_index(axis) >> bit) & 1


def doubled(value, axis, bit, dim):
    other = swap(value, axis, bit)
    mine = side(axis, bit)
    return jnp.where(
        mine == 0, jnp.stack([value, other], axis=dim), jnp.stack([other, value], axis=dim)
    )


def halves(value, axis, bit, dim):
    mine = side(axis, bit)
    away = lax.dynamic_index_in_dim(value, 1 - mine, dim, keepdims=False)
    return [lax.dynamic_index_in_dim(value, mine, dim, keepdims=False), swap(away, axis, bit)]


def quarters(value, axis, bit, dim):
    size = lax.axis_size(axis)
    mine = (lax.axis_index(axis) >> bit) & 3
    value = value.reshape(value.shape[:dim] + (4,) + value.shape[dim + 2 :])
    blocks = [lax.dynamic_index_in_dim(value, mine, dim, keepdims=False)]
    for step in range(1, 4):
        away = lax.dynamic_index_in_dim(value, mine ^ step, dim, keepdims=False)
        blocks.append(lax.ppermute(away, axis, [(i, i ^ (step << bit)) for i in range(size)]))
    return blocks


def added(blocks, dtype):
    return sum(block.astype(F32) for block in blocks).astype(dtype)


def place_of(done, step):
    return sum(1 for other in done if other > step)


def order_key(axis, bit):
    return (1 if axis == "seq" else 0, bit)


def gather_pairs(value, steps):
    done = []
    for axis, bit in steps:
        at = order_key(axis, bit)
        value = doubled(value, axis, bit, place_of(done, at))
        done.append(at)
    return (value, done)


def scatter_begin(value, steps, lead=0):
    left = [(axis, bit + k) for axis, bit, count in steps for k in range(count)]
    left = sorted((order_key(axis, bit) for axis, bit in left), reverse=True)
    value = value.reshape(value.shape[:lead] + (2,) * len(left) + value.shape[lead + 1 :])
    return (value, left, list(steps), lead)


def scatter_step(state, gate=None):
    value, left, steps, lead = state
    axis, bit, count = steps[0]
    gone = [order_key(axis, bit + k) for k in range(count)]
    dtype = F32 if len(steps) == 1 else BF16
    dim = lead + min(left.index(entry) for entry in gone)
    blocks = (halves if count == 1 else quarters)(value, axis, bit, dim)
    if gate is not None:
        blocks, _ = lax.optimization_barrier((blocks, gate))
    value = added(blocks, dtype)
    return (value, [other for other in left if other not in gone], steps[1:], lead)


def scatter_blocks(state):
    value, left, ((axis, bit, count),), lead = state
    return (halves if count == 1 else quarters)(value, axis, bit, lead)


def scatter_end(state, gate=None):
    while state[2]:
        state = scatter_step(state, gate)
    return state[0]


def after(states, values):
    blocks, values = lax.optimization_barrier(([state[0] for state in states], values))
    return ([(block,) + tuple(state[1:]) for block, state in zip(blocks, states)], values)


def gather_far(shard):
    steps = [("seq", bit) for bit in reversed(range(1, bits_of("seq")))]
    return gather_pairs(shard, steps)


def gather_near(part, done, first):
    side_bits = [("grp", bit) for bit in range(1, bits_of("grp"))]
    middle = [("seq", 0)] + side_bits if first == "seq" else side_bits + [("seq", 0)]
    done = list(done)
    for axis, bit in middle + [("grp", 0)]:
        at = order_key(axis, bit)
        part = doubled(part, axis, bit, place_of(done, at))
        done.append(at)
    return part.reshape(-1, part.shape[-1])


def near_swap(even, odd):
    mine = side("seq", 0)
    return swap(jnp.where(mine == 0, even, odd), "seq", 0)


def across_swap(value):
    size = lax.axis_size("seq")
    pairs = [(i, i - 1 if i % 2 == 0 else i + 1) for i in range(size)]
    return lax.ppermute(value, "seq", [(i, j) for i, j in pairs if 0 <= j < size])


def diagonal_swap(even, odd):
    return across_swap(jnp.where(side("seq", 0) == 0, even, odd))


def late_steps(side_first):
    side_bits = [("grp", bit, 1) for bit in range(1, bits_of("grp"))]
    far_bits = [("seq", bit, 1) for bit in range(1, bits_of("seq"))]
    start = side_bits + far_bits[:1] if side_first else far_bits[:1] + side_bits
    return [("grp", 0, 1)] + start + [("seq", 0, 1)] + far_bits[1:]


def scatter_steps(first, most=2):
    count = bits_of("seq")
    far_bits = [("seq", bit, min(most, count - bit)) for bit in range(1, count, most)]
    side_bits = [("grp", bit, 1) for bit in range(1, bits_of("grp"))]
    middle = [("seq", 0, 1)] + side_bits if first == "seq" else side_bits + [("seq", 0, 1)]
    return [("grp", 0, 1)] + middle + far_bits


def summed_all(value):
    for axis in ("grp", "seq"):
        count, size = (bits_of(axis), lax.axis_size(axis))
        for bit in range(0, count, 2):
            others = [
                lax.ppermute(value, axis, [(i, i ^ (step << bit)) for i in range(size)])
                for step in range(1, 4 if bit + 1 < count else 2)
            ]
            value = value + others[0]
            if len(others) == 3:
                value = value + (others[1] + others[2])
    return value


def local(
    tokens,
    seq_lengths,
    answer_mask,
    out_grad,
    qkv_weight,
    merge_weight,
    expand_weight,
    shrink_weight,
    small_params,
    qkv_rows,
    qkv_cols,
    merge_rows,
    merge_cols,
    expand_rows,
    expand_cols,
    shrink_rows,
    shrink_cols,
    small_moment,
):
    seqs, piece, width = tokens.shape
    axes = ("seq", "grp")
    devices = lax.axis_size("seq") * lax.axis_size("grp")
    rows = qkv_weight.shape[0]
    ff_rows = shrink_weight.shape[0]
    chunks = FF // D
    total = piece * lax.axis_size("seq")
    start = lax.axis_index("seq") * piece
    info = jnp.concatenate(
        [jnp.stack([start, jnp.int32(total)]).astype(jnp.int32), seq_lengths.astype(jnp.int32)]
    )
    smalls = small_params.shape[1]

    packed = whole_call(
        pack_kernel,
        [((rows, 9 * D), BF16)],
        (merge_weight, expand_weight, shrink_weight),
        "pack",
        2,
        [pltpu.VMEM((GROUPS, ff_rows, LANES), F32)],
    )[0]
    packed = lax.all_gather(packed, axes, axis=0, tiled=True)
    early = jnp.concatenate(
        [qkv_weight.astype(BF16), jnp.pad(small_params.astype(BF16), ((0, 0), (0, LANES - smalls)))],
        axis=1,
    )
    last, ahead = (tokens[:, piece - WIN :], tokens[:, :WIN])
    beside = near_swap(last, ahead)
    across = diagonal_swap(ahead, last)
    early, done = gather_far(early)
    weight_a = gather_near(early[..., :CUT], done, "grp")
    weight_b = gather_near(early[..., CUT:], done, "seq")
    flat = tokens.reshape(seqs * piece, width)
    cot = (out_grad * answer_mask[:, :, None].astype(BF16)).reshape(seqs * piece, width)

    turned = flat.T
    old_rows = [entry[None, :] for entry in (qkv_rows, merge_rows, expand_rows, shrink_rows)]
    old_cols = [entry[None, :] for entry in (qkv_cols, merge_cols, expand_cols, shrink_cols)]
    turned, old_rows, old_cols, info = lax.optimization_barrier((turned, old_rows, old_cols, info))
    query, key, value, pool, rim_near, rim_across, vectors = project(
        info, beside, tokens, across, weight_a, weight_b
    )
    mixed, near_lse = near_attend(info, query, key, value)
    att, pkey, pvalue, far_lse = far_attend(
        info, query, pool, swap(rim_near, "seq", 0), across_swap(rim_across), mixed
    )
    att_flat = att.reshape(seqs * piece, width)
    (
        block_out, first_grad, hidden_low, active, up_grad, branch_grad, mixed_grad, att_grad, sums,
    ) = feed(flat, att_flat, cot, packed, vectors)

    merge_local = outer(att_flat, mixed_grad).astype(BF16).reshape(1, devices, rows, D)
    merge_chain = scatter_step(scatter_begin(merge_local, late_steps(True), 1))
    merge_local, branch_grad = lax.optimization_barrier((merge_local, branch_grad))
    shrink_local = outer(active, branch_grad).astype(BF16).reshape(chunks, devices, rows, D)
    shrink_chain = scatter_step(scatter_begin(shrink_local, late_steps(True), 1))
    (merge_chain,), (shrink_local, up_grad) = after([merge_chain], (shrink_local, up_grad))
    expand_local = outer(hidden_low, up_grad).astype(BF16).reshape(devices, rows, FF)
    expand_chain = scatter_step(scatter_begin(expand_local, late_steps(False)))
    late_chain = (jnp.concatenate([shrink_chain[0], merge_chain[0]], axis=0),) + shrink_chain[1:]
    chains = [late_chain, expand_chain]

    def seq_rows(value, which):
        return value[which * piece : (which + 1) * piece]

    def advance(states, gate):
        return [scatter_step(state, gate) if len(state[2]) > 1 else state for state in states]

    att_grad = att_grad.reshape(seqs, piece, width)
    chains, info = after(chains, info)
    full_parts, parts, rims = ([], [], [])
    for which in range(seqs):
        parts.append(back(which, info, query, key, value, pkey, pvalue, att_grad, near_lse, far_lse))
        info, _ = lax.optimization_barrier((info, parts[which][0]))
    for which in range(seqs):
        query_part, near_grad, far_grad, rim_near, rim_across = parts[which]
        if which:
            rim_near, rim_across, _ = lax.optimization_barrier((rim_near, rim_across, rims[which - 1][3:]))
        rims.append((query_part, near_grad, far_grad, swap(rim_near, "seq", 0), across_swap(rim_across)))
    chains = advance(chains, (parts[-1][0], rims[0][3:]))
    chains, vectors = after(chains, vectors)
    before = None
    for which in range(seqs):
        full_part, *before = pool_back(
            which, seqs, info, rims[which], key, value, vectors, turned, before, sums
        )
        full_parts.append(full_part.reshape(piece, 3 * width))
        if which == 0:
            while len(chains[0][2]) > bits_of("seq") - 1:
                chains = advance(chains, (full_part, rims[-1][3:]))
            chains, vectors = after(chains, vectors)
    late_parts = [chains[0][0][j] for j in range(chunks + 1)] + [chains[1][0]]
    late_chain = (jnp.concatenate(late_parts, axis=-1),) + chains[1][1:]
    late_chain = advance([late_chain], None)[0]
    (late_chain,), before = after([late_chain], before)
    early_chains = [
        scatter_step(scatter_begin(entry.reshape(devices, rows, -1), scatter_steps(first)))
        for entry, first in zip(before, ("seq", "grp"))
    ]
    for _ in range(bits_of("grp")):
        early_gate = early_chains[0][0]
        early_chains = [scatter_step(state) for state in early_chains]
    early_chain = (
        jnp.concatenate([state[0] for state in early_chains], axis=-1),
    ) + early_chains[0][1:]
    late_sum = scatter_end(late_chain, early_gate)
    base, expand_sum, shrink_sum = whole_call(
        late_kernel,
        [((1, 9 * D + LANES), F32), ((rows, FF), F32), ((ff_rows, D), F32)],
        (late_sum,) + tuple(old_rows),
        "late_stats",
        3,
        [pltpu.VMEM((GROUPS, ff_rows, LANES), F32)],
    )
    (early_chain,), base = after([early_chain], base)
    while len(early_chain[2]) > 1:
        early_chain = scatter_step(early_chain)
    early_blocks = scatter_blocks(early_chain)
    early_blocks += [jnp.zeros_like(early_blocks[0])] * (4 - len(early_blocks))
    full_parts, _ = lax.optimization_barrier((full_parts, early_chain[0]))
    input_grad = jnp.stack(
        [
            seq_rows(first_grad, which)
            + nt(full_parts[which][:, :CUT], weight_a)
            + nt(full_parts[which][:, CUT:], weight_b[:, : 3 * D - CUT])
            for which in range(seqs)
        ]
    )

    masters = (qkv_weight, merge_weight, expand_weight, shrink_weight)
    payload, early_sum = whole_call(
        stats_kernel,
        [((1, 9 * D + LANES), F32), (early_blocks[0].shape, F32)],
        (*early_blocks, base),
        "stats",
        1,
    )
    payload = summed_all(payload)
    outs = [((1, 1), F32)]
    for master in masters:
        high, wide = master.shape
        outs += [((high, wide), F32), ((1, high), F32), ((wide // LANES, LANES), F32), ((high, wide), F32)]
        outs += [((high, wide), BF16)]
    outs += [((smalls, rows), F32)] * 3 + [((smalls, rows), BF16)]
    fresh = whole_call(
        update_kernel,
        outs,
        (payload, early_sum, late_sum, expand_sum, shrink_sum)
        + tuple(old_rows)
        + tuple(old_cols)
        + masters
        + (small_params.T, small_moment.T),
        "update",
        5,
    )
    results = []
    for index in range(4):
        grad, rows_new, cols_new, new, low_new = fresh[1 + 5 * index : 6 + 5 * index]
        results += [grad, rows_new.reshape(-1), cols_new.reshape(-1), new, low_new]
    return (
        block_out.reshape(seqs, piece, width),
        input_grad,
        fresh[0].reshape(()),
        *results,
        *[entry.T for entry in fresh[21:]],
    )


def solution(mesh):
    whole = ("seq", "grp")
    matrix = P(whole, None)
    vector = P(whole)
    in_specs = (
        P("grp", "seq", None),
        P("grp"),
        P("grp", "seq"),
        P("grp", "seq", None),
        *[matrix] * 5,
        *[vector, P()] * 4,
        matrix,
    )
    out_specs = (
        P("grp", "seq", None),
        P("grp", "seq", None),
        P(),
        *[matrix, vector, P(), matrix, matrix] * 4,
        *[matrix] * 4,
    )
    return jax.shard_map(local, mesh=mesh, in_specs=in_specs, out_specs=out_specs, check_vma=False)
```

```python
import functools

import jax
import jax.numpy as jnp
from jax import lax
from jax.experimental import pallas as pl
from jax.experimental.pallas import tpu as pltpu
from jax.sharding import PartitionSpec as P

D = 768
HEAD_DIM = 64
FF = 3072
WIN = 64
PWIN = 64
TILE = 128
LANES = 128
NEAR = TILE + 2 * WIN
FAR = TILE // 4 + 2 * PWIN
GROUPS = D // LANES

EPS_NORM = 1e-05
EPS_FACTOR = 1e-30
DECAY = 0.5
RATE = 0.08
CLIP = 1.0
NEG = -1e30
BIG = 3e38
SCALE = HEAD_DIM ** (-0.5)

TAIL_STEP = 0.31
TAIL = (
    0.12367211422929353,
    0.12367030785161068,
    0.11185922254891491,
    0.08691510254396204,
    0.06423540557821411,
    -0.014525970624111314,
    0.08814037010576171,
    -0.154963171944524,
    0.08860162861073731,
    -0.017604979368020673,
)
INV_ROOT = 0.3989422804014327

F32 = jnp.float32
BF16 = jnp.bfloat16
CUT = 1280
TOGETHER = 3
BUFFERS = 4
BACK_TOGETHER = 3
VMEM_LIMIT = 60 * 1024 * 1024


def nn(left, right):
    return jnp.dot(left, right, preferred_element_type=F32)


def nt(left, right):
    return lax.dot_general(left, right, (((1,), (1,)), ((), ())), preferred_element_type=F32)


def outer(left, right):
    return lax.dot_general(left, right, (((0,), (0,)), ((), ())), preferred_element_type=F32)


def from_behind(value, axis, by):
    size = lax.axis_size(axis)
    pairs = [(i, i + by) for i in range(size) if 0 <= i + by < size]
    return lax.ppermute(value, axis, pairs)


def params(**extra):
    return pltpu.CompilerParams(vmem_limit_bytes=VMEM_LIMIT, **extra)


def cost(micros):
    return pl.CostEstimate(flops=int(micros * 8e8), bytes_accessed=0, transcendentals=0)


def fixed(shape):
    zeros = (0,) * len(shape)
    return pl.BlockSpec(shape, lambda *_: zeros, pipeline_mode=pl.Buffered(1))


def lanes_of(index, width=LANES):
    return slice(index * width, (index + 1) * width)


def near_cap(start, total, length, first):
    key = start - WIN + first + lax.broadcasted_iota(jnp.int32, (NEAR, TILE), 0)
    query = start + first + lax.broadcasted_iota(jnp.int32, (NEAR, TILE), 1)
    near = (jnp.abs(query - key) <= WIN) & (key >= 0) & (key < total)
    return jnp.where(near & ((key < length) | (key == query)), BIG, NEG)


def far_cap(start, total, length, first):
    pooled = start // 4 - PWIN + first // 4 + lax.broadcasted_iota(jnp.int32, (FAR, TILE), 0)
    coarse = (start + first + lax.broadcasted_iota(jnp.int32, (FAR, TILE), 1)) // 4
    far = (jnp.abs(coarse - pooled) <= PWIN) & (pooled >= 0) & (pooled < total // 4)
    return jnp.where(far & ((4 * pooled < length) | (pooled == coarse)), BIG, NEG)


def split_pair(pair):
    lane = lax.broadcasted_iota(jnp.int32, pair.shape, 1)
    zero = jnp.zeros_like(pair)
    return jnp.concatenate(
        [jnp.where(lane < HEAD_DIM, pair, zero), jnp.where(lane < HEAD_DIM, zero, pair)], axis=0
    )


LEVELS = ((0, NEAR), (NEAR, NEAR + FAR))


def join_pair(stacked):
    row = lax.broadcasted_iota(jnp.int32, (LANES, TILE), 0)
    return jnp.where(row < HEAD_DIM, stacked[:, :TILE], stacked[:, TILE:])


def project_kernel(
    info, beside, own, across, weight_a, weight_b, query, key, value, pool, rim_near, rim_across,
    vectors, wide,
):
    piece = own.shape[1]
    pools = piece // 4
    even = (info[0] // piece) % 2 == 0
    low = jnp.where(even, across[0], beside[0])
    high = jnp.where(even, beside[0], across[0])
    small = weight_b[:, 3 * D - CUT :].astype(F32).T
    vectors[...] = small[:16]
    taps = small[4:14]

    def weight_chunk(chunk):
        if chunk < CUT // 256:
            return weight_a[:, lanes_of(chunk, 256)]
        return weight_b[:, lanes_of(chunk - CUT // 256, 256)]

    for chunk in range(3):
        cols = lanes_of(chunk, 256)
        query[0, :, cols] = (nn(own[0], weight_chunk(chunk)) * SCALE).astype(BF16)
    for chunk in range(6):
        target = key if chunk < 3 else value
        cols = lanes_of(chunk % 3, 256)
        block = weight_chunk(3 + chunk)
        for source, base, count in ((low, 0, WIN), (own[0], WIN, piece), (high, WIN + piece, WIN)):
            rounded = nn(source, block).astype(BF16)
            held = rounded.astype(F32)
            wide[2 * chunk, base : base + count, :] = held[:, :LANES]
            wide[2 * chunk + 1, base : base + count, :] = held[:, LANES:]
            target[0, base : base + count, cols] = rounded
    for group in range(2 * GROUPS):
        part = group // GROUPS
        cols = lanes_of(group % GROUPS)
        pooled = None
        for tap in range(5):
            term = taps[5 * part + tap : 5 * part + tap + 1, cols] * wide[
                group, pl.ds(WIN - 2 + tap, pools, stride=4), :
            ]
            pooled = term if pooled is None else pooled + term
        pooled = pooled.astype(BF16)
        pool[0, part, :, cols] = pooled
        first, last = (pooled[:PWIN], pooled[pools - PWIN :])
        rim_near[0, part, :, cols] = jnp.where(even, last, first)
        rim_across[0, part, :, cols] = jnp.where(even, first, last)


def level_mixed(queries, keys, values, cap, lse, tile, pairs):
    heads = [(at, head) for at in range(len(pairs)) for head in range(2)]
    scores = [nt(keys[at], queries[at][head * TILE : (head + 1) * TILE]) for at, head in heads]
    scores = [jnp.minimum(entry, cap[...]) for entry in scores]
    tops = [jnp.max(entry, axis=0, keepdims=True) for entry in scores]
    raised = [jnp.exp(entry - top) for entry, top in zip(scores, tops)]
    norms = [jnp.sum(entry, axis=0, keepdims=True) for entry in raised]
    for (at, head), top, norm in zip(heads, tops, norms):
        lse[0, tile, pairs[at] : pairs[at] + 1, lanes_of(head)] = top + jnp.log(norm)
    probs = [(entry * (1.0 / norm)).astype(BF16) for entry, norm in zip(raised, norms)]
    turned = [entry.T for entry in values]
    mixed = [
        nn(entry, jnp.concatenate(probs[2 * at : 2 * at + 2], axis=1)) for at, entry in enumerate(turned)
    ]
    return [join_pair(entry).T for entry in mixed]


def near_kernel(info, query, key, value, mixed, lse, cap):
    piece = query.shape[1]
    which = pl.program_id(0)
    start, total, length = (info[0], info[1], info[2 + which])

    def tile_step(tile, carry):
        first = pl.multiple_of(tile * TILE, TILE)
        cap[...] = near_cap(start, total, length, first)
        for begin in range(0, GROUPS, TOGETHER):
            pairs = range(begin, begin + TOGETHER)
            queries = [split_pair(query[0, pl.ds(first, TILE), lanes_of(pair)]) for pair in pairs]
            keys = [key[0, pl.ds(first, NEAR), lanes_of(pair)] for pair in pairs]
            values = [value[0, pl.ds(first, NEAR), lanes_of(pair)] for pair in pairs]
            parts = level_mixed(queries, keys, values, cap, lse, tile, pairs)
            for pair, part in zip(pairs, parts):
                mixed[0, pl.ds(first, TILE), lanes_of(pair)] = part
        return carry

    lax.fori_loop(0, piece // TILE, tile_step, 0)


def far_kernel(info, query, pool, beside, across, mixed, att, pkey, pvalue, lse, cap):
    piece = query.shape[1]
    pools = piece // 4
    which = pl.program_id(0)
    start, total, length = (info[0], info[1], info[2 + which])
    even = (start // piece) % 2 == 0
    for part, target in enumerate((pkey, pvalue)):
        target[0, :PWIN, :] = jnp.where(even, across[0, part], beside[0, part])
        target[0, PWIN : PWIN + pools, :] = pool[0, part]
        target[0, PWIN + pools :, :] = jnp.where(even, beside[0, part], across[0, part])

    def tile_step(tile, carry):
        first = pl.multiple_of(tile * TILE, TILE)
        coarse = pl.multiple_of(tile * (TILE // 4), TILE // 4)
        cap[...] = far_cap(start, total, length, first)
        for begin in range(0, GROUPS, TOGETHER):
            pairs = range(begin, begin + TOGETHER)
            queries = [split_pair(query[0, pl.ds(first, TILE), lanes_of(pair)]) for pair in pairs]
            keys = [pkey[0, pl.ds(coarse, FAR), lanes_of(pair)] for pair in pairs]
            values = [pvalue[0, pl.ds(coarse, FAR), lanes_of(pair)] for pair in pairs]
            parts = level_mixed(queries, keys, values, cap, lse, tile, pairs)
            for pair, part in zip(pairs, parts):
                place = (0, pl.ds(first, TILE), lanes_of(pair))
                att[place] = (mixed[place] + part).astype(BF16)
        return carry

    lax.fori_loop(0, piece // TILE, tile_step, 0)


def per_seq(body, operands, shapes, micros, name, shared=0, common=(), scratch=()):
    info, *rest = operands
    seqs = rest[0].shape[0]
    split = len(rest) - shared

    def seq_block(shape):
        return pl.BlockSpec((1,) + tuple(shape), lambda s: (s,) + (0,) * len(shape))

    return pl.pallas_call(
        body,
        grid=(seqs,),
        in_specs=[pl.BlockSpec(memory_space=pltpu.SMEM)]
        + [seq_block(entry.shape[1:]) for entry in rest[:split]]
        + [fixed(entry.shape) for entry in rest[split:]],
        out_specs=[seq_block(shape) for shape, _ in shapes]
        + [pl.BlockSpec(shape, lambda s: (0,) * len(shape)) for shape, _ in common],
        out_shape=[jax.ShapeDtypeStruct((seqs,) + shape, dtype) for shape, dtype in shapes]
        + [jax.ShapeDtypeStruct(shape, dtype) for shape, dtype in common],
        scratch_shapes=list(scratch),
        compiler_params=params(),
        cost_estimate=cost(micros),
        name=name,
    )(*operands)


def project(info, beside, own, across, weight_a, weight_b):
    _, piece, width = own.shape
    extent, pools = (piece + 2 * WIN, piece // 4)
    return per_seq(
        project_kernel,
        (info, beside, own, across, weight_a, weight_b),
        [
            ((piece, width), BF16),
            ((extent, width), BF16),
            ((extent, width), BF16),
            ((2, pools, width), BF16),
            ((2, PWIN, width), BF16),
            ((2, PWIN, width), BF16),
        ],
        10,
        "project",
        shared=2,
        common=[((16, width), F32)],
        scratch=[pltpu.VMEM((2 * GROUPS, extent, LANES), F32)],
    )


def near_attend(info, query, key, value):
    _, piece, width = query.shape
    return per_seq(
        near_kernel,
        (info, query, key, value),
        [((piece, width), F32), ((piece // TILE, 8, 2 * TILE), F32)],
        30,
        "near",
        scratch=[pltpu.VMEM((NEAR, TILE), F32)],
    )


def far_attend(info, query, pool, beside, across, mixed):
    _, piece, width = query.shape
    pools = piece // 4 + 2 * PWIN
    return per_seq(
        far_kernel,
        (info, query, pool, beside, across, mixed),
        [
            ((piece, width), BF16),
            ((pools, width), BF16),
            ((pools, width), BF16),
            ((piece // TILE, 8, 2 * TILE), F32),
        ],
        12,
        "far",
        scratch=[pltpu.VMEM((FAR, TILE), F32)],
    )


def layer_stats(values):
    centred = values - jnp.mean(values, axis=-1, keepdims=True)
    inverse = lax.rsqrt(jnp.mean(centred * centred, axis=-1, keepdims=True) + EPS_NORM)
    return (centred * inverse, inverse)


def layer_back(grad, normed, inverse):
    return inverse * (
        grad
        - jnp.mean(grad, axis=-1, keepdims=True)
        - normed * jnp.mean(grad * normed, axis=-1, keepdims=True)
    )


def gelu_parts(up):
    size = jnp.abs(up)
    bell = jnp.exp(-0.5 * (up * up))
    near = 1.0 / (1.0 + TAIL_STEP * size)
    poly = jnp.full_like(up, TAIL[-1])
    for factor in TAIL[-2::-1]:
        poly = poly * near + factor
    tail = bell * (near * poly)
    phi = jnp.where(up >= 0.0, 1.0 - tail, tail)
    return (up * phi, phi + up * (bell * INV_ROOT))


def feed_kernel(
    tokens, att, cot, packed, vectors, block_out, first_grad, hidden_low, active,
    up_grad, branch_grad, mixed_grad, att_grad, sums, slope,
):
    step = pl.program_id(0)
    gain_one, bias_one, gain_two, bias_two = [vectors[i : i + 1, :] for i in range(4)]
    def merge():
        return packed[:, :D]

    def expand(chunk):
        return packed[:, lanes_of(1 + chunk, D)]

    def shrink(chunk):
        return packed[:, lanes_of(1 + FF // D + chunk, D)]

    first_norm, first_inv = layer_stats(tokens[...].astype(F32) + nn(att[...], merge()))
    hidden = first_norm * gain_one + bias_one
    low = hidden.astype(BF16)
    hidden_low[...] = low
    branch = None
    for chunk in range(FF // D):
        cols = lanes_of(chunk, D)
        wide, steep = gelu_parts(nn(low, expand(chunk)))
        narrow = wide.astype(BF16)
        active[:, cols] = narrow
        slope[:, cols] = steep
        term = nn(narrow, shrink(chunk))
        branch = term if branch is None else branch + term
    second_norm, second_inv = layer_stats(hidden + branch)
    block_out[...] = (second_norm * gain_two + bias_two).astype(BF16)
    cotangent = cot[...].astype(F32)

    @pl.when(step == 0)
    def clear():
        sums[...] = jnp.zeros_like(sums)

    def add_sum(row, value):
        sums[row : row + 1, :] += jnp.sum(value, axis=0, keepdims=True)

    add_sum(2, cotangent * second_norm)
    add_sum(3, cotangent)
    second_grad = layer_back(cotangent * gain_two, second_norm, second_inv)
    second_low = second_grad.astype(BF16)
    branch_grad[...] = second_low
    feed = None
    for chunk in range(FF // D):
        cols = lanes_of(chunk, D)
        narrow = (nt(second_low, shrink(chunk)) * slope[:, cols]).astype(BF16)
        up_grad[:, cols] = narrow
        term = nt(narrow, expand(chunk))
        feed = term if feed is None else feed + term
    hidden_grad = second_grad + feed.astype(BF16).astype(F32)
    add_sum(0, hidden_grad * first_norm)
    add_sum(1, hidden_grad)
    grad = layer_back(hidden_grad * gain_one, first_norm, first_inv)
    first_grad[...] = grad
    grad_low = grad.astype(BF16)
    mixed_grad[...] = grad_low
    att_grad[...] = nt(grad_low, merge()).astype(BF16)


def feed(tokens, att, cot, packed, vectors):
    rows, width = tokens.shape
    block = 256
    ff = FF

    def row_block(cols):
        return pl.BlockSpec((block, cols), lambda i: (i, 0))

    outs = [
        (width, BF16),
        (width, F32),
        (width, BF16),
        (ff, BF16),
        (ff, BF16),
        (width, BF16),
        (width, BF16),
        (width, BF16),
    ]
    return pl.pallas_call(
        feed_kernel,
        grid=(rows // block,),
        in_specs=[row_block(width)] * 3
        + [fixed(packed.shape), fixed(vectors.shape)],
        out_specs=[row_block(cols) for cols, _ in outs] + [pl.BlockSpec((8, width), lambda i: (0, 0))],
        out_shape=[jax.ShapeDtypeStruct((rows, cols), dtype) for cols, dtype in outs]
        + [jax.ShapeDtypeStruct((8, width), F32)],
        scratch_shapes=[pltpu.VMEM((block, ff), F32)],
        compiler_params=params(),
        cost_estimate=cost(48),
        name="feed",
    )(tokens, att, cot, packed, vectors)


def back_kernel(
    which, info, query, key, value, pkey, pvalue, grad, near_lse, far_lse, query_grad, near_grad,
    far_grad, rim_near, rim_across, caps,
):
    piece = query.shape[1]
    even = (info[0] // piece) % 2 == 0
    start, total, length = (info[0], info[1], info[2 + which])
    near_grad[...] = jnp.zeros_like(near_grad)
    far_grad[...] = jnp.zeros_like(far_grad)

    def tile_step(tile, carry):
        first = pl.multiple_of(tile * TILE, TILE)
        coarse = pl.multiple_of(tile * (TILE // 4), TILE // 4)
        for cap, (begin, end) in zip((near_cap, far_cap), LEVELS):
            block = cap(start, total, length, first)
            caps[begin:end, :TILE] = block
            caps[begin:end, TILE:] = block
        near_rows, far_rows = (pl.ds(first, NEAR), pl.ds(coarse, FAR))
        place = pl.ds(first, TILE)
        for start_pair in range(0, GROUPS, BACK_TOGETHER):
            pairs = range(start_pair, start_pair + BACK_TOGETHER)
            many = range(BACK_TOGETHER)
            spans = [lanes_of(pair) for pair in pairs]
            queries = [split_pair(query[0, place, cols]) for cols in spans]
            grads = [split_pair(grad[0, place, cols]) for cols in spans]
            keys = [
                jnp.concatenate([key[0, near_rows, cols], pkey[0, far_rows, cols]], axis=0)
                for cols in spans
            ]
            values = [
                jnp.concatenate([value[0, near_rows, cols], pvalue[0, far_rows, cols]], axis=0)
                for cols in spans
            ]
            scores = [nt(keys[at], queries[at]) for at in many]
            prob_grads = [nt(values[at], grads[at]) for at in many]
            probs = [[] for _ in many]
            score_grads = [[] for _ in many]
            for level, (begin, end) in enumerate(LEVELS):
                lse = (near_lse, far_lse)[level]
                exact_probs = [
                    jnp.exp(
                        jnp.minimum(scores[at][begin:end], caps[begin:end, :])
                        - lse[0, tile, pairs[at] : pairs[at] + 1, :]
                    )
                    for at in many
                ]
                weighted = [exact_probs[at] * prob_grads[at][begin:end] for at in many]
                inner = [jnp.sum(entry, axis=0, keepdims=True) for entry in weighted]
                for at in many:
                    score_grads[at].append((weighted[at] - exact_probs[at] * inner[at]).astype(BF16))
                    probs[at].append(exact_probs[at].astype(BF16))
            score_grads = [jnp.concatenate(entry, axis=0) for entry in score_grads]
            key_parts = [nn(score_grads[at], queries[at]) for at in many]
            value_parts = [nn(jnp.concatenate(probs[at], axis=0), grads[at]) for at in many]
            turned = [entry.T for entry in keys]
            query_parts = [nn(turned[at], score_grads[at]) for at in many]
            for at, cols in enumerate(spans):
                near_grad[0, 0, near_rows, cols] += key_parts[at][:NEAR]
                far_grad[0, 0, far_rows, cols] += key_parts[at][NEAR:]
                near_grad[0, 1, near_rows, cols] += value_parts[at][:NEAR]
                far_grad[0, 1, far_rows, cols] += value_parts[at][NEAR:]
                query_grad[0, place, cols] = (join_pair(query_parts[at]) * SCALE).T.astype(BF16)
        return carry

    lax.fori_loop(0, piece // TILE, tile_step, 0)
    pools = far_grad.shape[2]
    blank = jnp.zeros((16, far_grad.shape[3]), BF16)
    for part in range(2):
        low = [near_grad[0, part, :WIN, :], far_grad[0, part, : PWIN + 16, :]]
        low = [entry.astype(BF16) for entry in low]
        high = [near_grad[0, part, WIN + piece :, :], far_grad[0, part, pools - PWIN :, :]]
        high = [entry.astype(BF16) for entry in high]

        @pl.when(even)
        def even_side():
            rim_near[0, part, :WIN, :] = high[0]
            rim_near[0, part, WIN : WIN + PWIN, :] = high[1]
            rim_near[0, part, WIN + PWIN :, :] = blank
            rim_across[0, part, :WIN, :] = low[0]
            rim_across[0, part, WIN:, :] = low[1]

        @pl.when(jnp.logical_not(even))
        def odd_side():
            rim_across[0, part, :WIN, :] = high[0]
            rim_across[0, part, WIN : WIN + PWIN, :] = high[1]
            rim_across[0, part, WIN + PWIN :, :] = blank
            rim_near[0, part, :WIN, :] = low[0]
            rim_near[0, part, WIN:, :] = low[1]


def seq_slice(shape, which):
    return pl.BlockSpec((1,) + tuple(shape[1:]), lambda _: (which,) + (0,) * (len(shape) - 1))


def back(which, info, query, key, value, pkey, pvalue, grad, near_lse, far_lse):
    _, piece, width = query.shape
    extent, pools = (key.shape[1], pkey.shape[1])
    operands = (query, key, value, pkey, pvalue, grad, near_lse, far_lse)
    shapes = [
        ((1, piece, width), BF16),
        ((1, 2, extent, width), F32),
        ((1, 2, pools, width), F32),
        ((1, 2, WIN + PWIN + 16, width), BF16),
        ((1, 2, WIN + PWIN + 16, width), BF16),
    ]
    return pl.pallas_call(
        functools.partial(back_kernel, which),
        grid=(1,),
        in_specs=[pl.BlockSpec(memory_space=pltpu.SMEM)]
        + [seq_slice(entry.shape, which) for entry in operands],
        out_specs=[seq_slice(shape, 0) for shape, _ in shapes],
        out_shape=[jax.ShapeDtypeStruct(shape, dtype) for shape, dtype in shapes],
        scratch_shapes=[pltpu.VMEM((NEAR + FAR, 2 * TILE), F32)],
        compiler_params=params(),
        cost_estimate=cost(0.01 if which else 30),
        name="back",
    )(info, *operands)


def pool_back_kernel(
    first, last, info, query_grad, near_grad, far_grad, beside, across, key, value, taps, turned, *rest
):
    rest = list(rest)
    before, taps_before = (None, None) if first else (rest.pop(0), rest.pop(0))
    sums = rest.pop(0) if last else None
    full_grad = rest.pop(0)
    outs = [rest.pop(0), rest.pop(0)]
    held_all, spread_all, window_all, taps_grad = rest
    piece = full_grad.shape[1]
    pools = piece // 4
    even = (info[0] // piece) % 2 == 0
    full_grad[0, :, :D] = query_grad[0]
    if first:
        taps_grad[...] = jnp.zeros_like(taps_grad)
    else:
        taps_grad[...] = taps_before[...]

    def product(chunk):
        cols = lanes_of(chunk, 256)
        total = nn(turned[...], full_grad[0, :, cols])
        if not first:
            total = total + before[:, cols].astype(F32)
        if not last:
            outs[0][:, cols] = total.astype(BF16)
        elif chunk < CUT // 256:
            outs[0][:, cols] = total.astype(BF16)
        else:
            outs[1][:, lanes_of(chunk - CUT // 256, 256)] = total.astype(BF16)

    for group in range(2 * GROUPS):
        if group % 4 == 0:
            product(group // 4)
        held, spread, window = [entry.at[group % BUFFERS] for entry in (held_all, spread_all, window_all)]
        part = group // GROUPS
        cols = lanes_of(group % GROUPS)
        source = key if part == 0 else value
        pair = [entry[0, part, :, cols].astype(F32) for entry in (beside, across)]
        from_high = jnp.where(even, pair[0], pair[1])
        from_low = jnp.where(even, pair[1], pair[0])
        tap = [taps[4 + 5 * part + t : 5 + 5 * part + t, cols] for t in range(5)]
        held[0:pools, :] = far_grad[0, part, PWIN : PWIN + pools, cols]
        held[0:PWIN, :] += from_low[WIN : WIN + PWIN]
        held[pools - PWIN : pools, :] += from_high[WIN : WIN + PWIN]
        held[pools : pools + 16, :] = (
            far_grad[0, part, PWIN + pools : PWIN + pools + 16, cols] + from_high[WIN + PWIN :]
        )
        now = held[0:pools, :]
        later = held[1 : pools + 1, :]
        spread[pl.ds(0, pools, stride=4), :] = tap[2] * now
        spread[pl.ds(1, pools, stride=4), :] = tap[3] * now
        spread[pl.ds(2, pools, stride=4), :] = tap[4] * now + tap[0] * later
        spread[pl.ds(3, pools, stride=4), :] = tap[1] * later
        spread[0:WIN, :] += from_low[:WIN]
        spread[piece - WIN : piece, :] += from_high[:WIN]
        total = near_grad[0, part, WIN : WIN + piece, cols] + spread[...]
        full_grad[0, :, lanes_of(GROUPS + group)] = total.astype(BF16)
        window[...] = source[0, WIN - 16 : WIN + piece + 16, cols].astype(F32)
        for t in range(5):
            row = 5 * part + t
            taps_grad[row : row + 1, cols] += jnp.sum(
                now * window[pl.ds(14 + t, pools, stride=4), :], axis=0, keepdims=True
            )
        if group % 2 == 1:
            product((GROUPS + group) // 2)
    if last:
        zeros = jnp.zeros((LANES - 14, D), F32)
        small = jnp.concatenate([sums[0:4, :], taps_grad[0:10, :], zeros], axis=0)
        outs[1][:, 3 * D - CUT :] = small.T.astype(BF16)
    else:
        outs[1][...] = taps_grad[...]


def pool_back(which, seqs, info, entries, key, value, taps, turned, before, sums):
    near_grad = entries[1]
    _, _, extent, width = near_grad.shape
    piece = extent - 2 * WIN
    pools = piece // 4
    first, last = (which == 0, which == seqs - 1)
    extra = (() if first else tuple(before)) + ((sums,) if last else ())
    if last:
        outs = [((width, CUT), BF16), ((width, 3 * width + LANES - CUT), BF16)]
    else:
        outs = [((width, 3 * width), BF16), ((16, width), F32)]
    return pl.pallas_call(
        functools.partial(pool_back_kernel, first, last),
        grid=(1,),
        in_specs=[pl.BlockSpec(memory_space=pltpu.SMEM)]
        + [seq_slice(entry.shape, 0) for entry in entries]
        + [seq_slice(entry.shape, which) for entry in (key, value)]
        + [fixed(taps.shape), pl.BlockSpec((width, piece), lambda _: (0, which))]
        + [fixed(entry.shape) for entry in extra],
        out_specs=[seq_slice((1, piece, 3 * width), 0)] + [fixed(shape) for shape, _ in outs],
        out_shape=[jax.ShapeDtypeStruct((1, piece, 3 * width), BF16)]
        + [jax.ShapeDtypeStruct(shape, dtype) for shape, dtype in outs],
        scratch_shapes=[
            pltpu.VMEM((BUFFERS, pools + 16, LANES), F32),
            pltpu.VMEM((BUFFERS, piece, LANES), F32),
            pltpu.VMEM((BUFFERS, piece + 32, LANES), F32),
            pltpu.VMEM((16, width), F32),
        ],
        compiler_params=params(),
        cost_estimate=cost(0.01 if which else 30),
        name="pool_back",
    )(info, *entries, key, value, taps, turned, *extra)


def unmix(width):
    row = lax.broadcasted_iota(jnp.int32, (4 * width, 4 * width), 0)
    col = lax.broadcasted_iota(jnp.int32, (4 * width, 4 * width), 1)
    return jnp.where(row == 4 * (col % width) + col // width, 1.0, 0.0)


def exact(left, right):
    return jnp.dot(left, right, precision=lax.Precision.HIGHEST, preferred_element_type=F32)


def exact_nt(left, right):
    return lax.dot_general(
        left, right, (((1,), (1,)), ((), ())), precision=lax.Precision.HIGHEST, preferred_element_type=F32
    )


def pack_kernel(merge, expand, shrink, out, held):
    rows = merge.shape[0]
    mixer = unmix(LANES).astype(BF16)
    out[:, :D] = merge[...].astype(BF16)
    for group in range(FF // (4 * LANES)):
        block = nn(expand[:, lanes_of(group, 4 * LANES)].astype(BF16), mixer).astype(BF16)
        for j in range(4):
            first = D + j * D + group * LANES
            out[:, first : first + LANES] = block[:, lanes_of(j)]
    for group in range(GROUPS):
        held[group] = shrink[:, lanes_of(group)]
        for j in range(4):
            first = (5 + j) * D + group * LANES
            out[:, first : first + LANES] = held[group, pl.ds(j, rows, stride=4), :].astype(BF16)


def squares(block):
    return jnp.sum(block * block, axis=0, keepdims=True)


def late_kernel(late, *rest):
    olds, (out, expand, shrink, held) = (rest[:4], rest[4:])
    rows = late.shape[0]
    mixer = unmix(LANES).astype(BF16)
    for group in range(FF // (4 * LANES)):
        pieces = []
        for j in range(4):
            first = (5 + j) * D + group * LANES
            pieces.append(late[:, first : first + LANES])
        left = jnp.concatenate(pieces, axis=1)
        total = None
        for _ in range(3):
            top = left.astype(BF16)
            left = left - top.astype(F32)
            term = nt(top, mixer)
            total = term if total is None else total + term
        expand[:, lanes_of(group, 4 * LANES)] = total
    for group in range(GROUPS):
        for j in range(4):
            held[group, pl.ds(j, rows, stride=4), :] = late[:, lanes_of(j * GROUPS + group)]
        shrink[:, lanes_of(group)] = held[group]
    out[:, : 3 * D] = jnp.zeros((1, 3 * D), F32)
    out[:, 3 * D : 4 * D] = squares(late[:, 4 * D : 5 * D])
    for j in range(FF // D):
        out[:, (4 + j) * D : (5 + j) * D] = squares(expand[:, lanes_of(j, D)])
    out[:, 8 * D : 9 * D] = squares(shrink[...])
    lane = lax.broadcasted_iota(jnp.int32, (1, LANES), 1)
    tail = jnp.zeros((1, LANES), F32)
    for slot, entry in enumerate(olds):
        tail = jnp.where(lane == slot + 1, jnp.sum(entry[...], axis=1, keepdims=True), tail)
    out[:, 9 * D :] = tail


def stats_kernel(own, one, two, three, base, out, early):
    early[...] = sum(entry[...].astype(F32) for entry in (own, one, two, three))
    out[:, : 3 * D] = squares(early[:, : 3 * D])
    out[:, 3 * D : 9 * D] = base[:, 3 * D : 9 * D]
    lane = lax.broadcasted_iota(jnp.int32, (1, LANES), 1)
    small = jnp.sum(squares(early[:, 3 * D :]), axis=1, keepdims=True)
    out[:, 9 * D :] = base[:, 9 * D :] + jnp.where(lane == 0, small, 0.0)


def update_kernel(
    total, early, late, expand, shrink, rows_0, rows_1, rows_2, rows_3, cols_0, cols_1,
    cols_2, cols_3, weight_0, weight_1, weight_2, weight_3, small, moment,
    norm_out, grad_0, rows_new_0, cols_new_0, new_0, low_0, grad_1, rows_new_1, cols_new_1, new_1,
    low_1, grad_2, rows_new_2, cols_new_2, new_2, low_2, grad_3, rows_new_3, cols_new_3, new_3,
    low_3, small_grad, moment_new, small_new, small_low,
):
    smalls = small.shape[0]
    tail = total[:, 9 * D :]
    spans = ((0, 3 * D), (3 * D, 4 * D), (4 * D, 8 * D), (8 * D, 9 * D))
    matrix_sums = [jnp.sum(total[:, a:b], axis=1, keepdims=True) for a, b in spans]
    norm = jnp.sqrt(matrix_sums[0] + matrix_sums[1] + matrix_sums[2] + matrix_sums[3] + tail[:, 0:1])
    clip = CLIP / jnp.maximum(norm, CLIP)
    norm_out[...] = norm
    parts = (
        [early[:, lanes_of(j, D)] for j in range(3)],
        [late[:, 4 * D : 5 * D]],
        [expand[:, lanes_of(j, D)] for j in range(FF // D)],
        [shrink[...]],
    )
    heights = (D, D, D, FF)
    olds = (
        (rows_0, cols_0, weight_0, grad_0, rows_new_0, cols_new_0, new_0, low_0),
        (rows_1, cols_1, weight_1, grad_1, rows_new_1, cols_new_1, new_1, low_1),
        (rows_2, cols_2, weight_2, grad_2, rows_new_2, cols_new_2, new_2, low_2),
        (rows_3, cols_3, weight_3, grad_3, rows_new_3, cols_new_3, new_3, low_3),
    )
    for index in range(4):
        old_rows, old_cols, weight, grad, rows_new, cols_new, new, low = olds[index]
        begin, end = spans[index]
        width, height = (end - begin, heights[index])
        mean_cols = (total[:, begin:end] * clip) * clip / height + EPS_FACTOR
        fresh_cols = DECAY * old_cols[...] + (1.0 - DECAY) * mean_cols
        for group in range(width // LANES):
            cols_new[group : group + 1, :] = fresh_cols[:, lanes_of(group)]
        squared = sum(part * part for part in parts[index])
        row_sum = exact_nt(jnp.ones((8, D), F32), squared)[:1]
        mean_rows = (row_sum * clip) * clip / width + EPS_FACTOR
        fresh_rows = DECAY * old_rows[...] + (1.0 - DECAY) * mean_rows
        rows_new[...] = fresh_rows
        row = lax.broadcasted_iota(jnp.int32, (weight.shape[0], weight.shape[0]), 0)
        col = lax.broadcasted_iota(jnp.int32, (weight.shape[0], weight.shape[0]), 1)
        down = jnp.sum(jnp.where(row == col, fresh_rows, 0.0), axis=1, keepdims=True)
        mean_all = (matrix_sums[index] * clip) * clip / (width * height) + EPS_FACTOR
        row_mean = DECAY * (tail[:, 1 + index : 2 + index] / height) + (1.0 - DECAY) * mean_all
        for j, part in enumerate(parts[index]):
            cols = lanes_of(j, D)
            clipped = part * clip
            grad[:, cols] = clipped
            estimate = down * fresh_cols[:, cols] / row_mean
            fresh = weight[:, cols] - RATE * clipped * lax.rsqrt(estimate)
            new[:, cols] = fresh
            low[:, cols] = fresh.astype(BF16)
    row = lax.broadcasted_iota(jnp.int32, (16, LANES), 0)
    col = lax.broadcasted_iota(jnp.int32, (16, LANES), 1)
    turned = exact_nt(jnp.where(row == col, 1.0, 0.0), early[:, 3 * D :])
    clipped = turned[:smalls] * clip
    small_grad[...] = clipped
    fresh_moment = DECAY * moment[...] + (1.0 - DECAY) * (clipped * clipped + EPS_FACTOR)
    moment_new[...] = fresh_moment
    fresh = small[...] - RATE * clipped * lax.rsqrt(fresh_moment)
    small_new[...] = fresh
    small_low[...] = fresh.astype(BF16)


def whole_call(body, outs, operands, name, micros, scratch=()):
    return pl.pallas_call(
        body,
        out_shape=[jax.ShapeDtypeStruct(shape, dtype) for shape, dtype in outs],
        in_specs=[pl.BlockSpec(memory_space=pltpu.VMEM)] * len(operands),
        out_specs=[pl.BlockSpec(memory_space=pltpu.VMEM)] * len(outs),
        scratch_shapes=list(scratch),
        compiler_params=params(),
        cost_estimate=cost(micros),
        name=name,
    )(*operands)


def swap(value, axis, bit):
    size = lax.axis_size(axis)
    return lax.ppermute(value, axis, [(i, i ^ (1 << bit)) for i in range(size)])


def bits_of(axis):
    return lax.axis_size(axis).bit_length() - 1


def side(axis, bit):
    return (lax.axis_index(axis) >> bit) & 1


def doubled(value, axis, bit, dim):
    other = swap(value, axis, bit)
    mine = side(axis, bit)
    return jnp.where(
        mine == 0, jnp.stack([value, other], axis=dim), jnp.stack([other, value], axis=dim)
    )


def halves(value, axis, bit, dim):
    mine = side(axis, bit)
    away = lax.dynamic_index_in_dim(value, 1 - mine, dim, keepdims=False)
    return [lax.dynamic_index_in_dim(value, mine, dim, keepdims=False), swap(away, axis, bit)]


def quarters(value, axis, bit, dim):
    size = lax.axis_size(axis)
    mine = (lax.axis_index(axis) >> bit) & 3
    value = value.reshape(value.shape[:dim] + (4,) + value.shape[dim + 2 :])
    blocks = [lax.dynamic_index_in_dim(value, mine, dim, keepdims=False)]
    for step in range(1, 4):
        away = lax.dynamic_index_in_dim(value, mine ^ step, dim, keepdims=False)
        blocks.append(lax.ppermute(away, axis, [(i, i ^ (step << bit)) for i in range(size)]))
    return blocks


def added(blocks, dtype):
    return sum(block.astype(F32) for block in blocks).astype(dtype)


def place_of(done, step):
    return sum(1 for other in done if other > step)


def order_key(axis, bit):
    return (1 if axis == "seq" else 0, bit)


def gather_pairs(value, steps):
    done = []
    for axis, bit in steps:
        at = order_key(axis, bit)
        value = doubled(value, axis, bit, place_of(done, at))
        done.append(at)
    return (value, done)


def scatter_begin(value, steps, lead=0):
    left = [(axis, bit + k) for axis, bit, count in steps for k in range(count)]
    left = sorted((order_key(axis, bit) for axis, bit in left), reverse=True)
    value = value.reshape(value.shape[:lead] + (2,) * len(left) + value.shape[lead + 1 :])
    return (value, left, list(steps), lead)


def scatter_step(state, gate=None):
    value, left, steps, lead = state
    axis, bit, count = steps[0]
    gone = [order_key(axis, bit + k) for k in range(count)]
    dtype = F32 if len(steps) == 1 else BF16
    dim = lead + min(left.index(entry) for entry in gone)
    blocks = (halves if count == 1 else quarters)(value, axis, bit, dim)
    if gate is not None:
        blocks, _ = lax.optimization_barrier((blocks, gate))
    value = added(blocks, dtype)
    return (value, [other for other in left if other not in gone], steps[1:], lead)


def scatter_blocks(state):
    value, left, ((axis, bit, count),), lead = state
    return (halves if count == 1 else quarters)(value, axis, bit, lead)


def scatter_end(state, gate=None):
    while state[2]:
        state = scatter_step(state, gate)
    return state[0]


def after(states, values):
    blocks, values = lax.optimization_barrier(([state[0] for state in states], values))
    return ([(block,) + tuple(state[1:]) for block, state in zip(blocks, states)], values)


def gather_far(shard):
    steps = [("seq", bit) for bit in reversed(range(1, bits_of("seq")))]
    return gather_pairs(shard, steps)


def gather_near(part, done, first):
    side_bits = [("grp", bit) for bit in range(1, bits_of("grp"))]
    middle = [("seq", 0)] + side_bits if first == "seq" else side_bits + [("seq", 0)]
    done = list(done)
    for axis, bit in middle + [("grp", 0)]:
        at = order_key(axis, bit)
        part = doubled(part, axis, bit, place_of(done, at))
        done.append(at)
    return part.reshape(-1, part.shape[-1])


def near_swap(even, odd):
    mine = side("seq", 0)
    return swap(jnp.where(mine == 0, even, odd), "seq", 0)


def across_swap(value):
    size = lax.axis_size("seq")
    pairs = [(i, i - 1 if i % 2 == 0 else i + 1) for i in range(size)]
    return lax.ppermute(value, "seq", [(i, j) for i, j in pairs if 0 <= j < size])


def diagonal_swap(even, odd):
    return across_swap(jnp.where(side("seq", 0) == 0, even, odd))


def late_steps(side_first):
    side_bits = [("grp", bit, 1) for bit in range(1, bits_of("grp"))]
    far_bits = [("seq", bit, 1) for bit in range(1, bits_of("seq"))]
    start = side_bits + far_bits[:1] if side_first else far_bits[:1] + side_bits
    return [("grp", 0, 1)] + start + [("seq", 0, 1)] + far_bits[1:]


def scatter_steps(first, most=2):
    count = bits_of("seq")
    far_bits = [("seq", bit, min(most, count - bit)) for bit in range(1, count, most)]
    side_bits = [("grp", bit, 1) for bit in range(1, bits_of("grp"))]
    middle = [("seq", 0, 1)] + side_bits if first == "seq" else side_bits + [("seq", 0, 1)]
    return [("grp", 0, 1)] + middle + far_bits


def summed_all(value):
    for axis in ("grp", "seq"):
        count, size = (bits_of(axis), lax.axis_size(axis))
        for bit in range(0, count, 2):
            others = [
                lax.ppermute(value, axis, [(i, i ^ (step << bit)) for i in range(size)])
                for step in range(1, 4 if bit + 1 < count else 2)
            ]
            value = value + others[0]
            if len(others) == 3:
                value = value + (others[1] + others[2])
    return value


def local(
    tokens,
    seq_lengths,
    answer_mask,
    out_grad,
    qkv_weight,
    merge_weight,
    expand_weight,
    shrink_weight,
    small_params,
    qkv_rows,
    qkv_cols,
    merge_rows,
    merge_cols,
    expand_rows,
    expand_cols,
    shrink_rows,
    shrink_cols,
    small_moment,
):
    seqs, piece, width = tokens.shape
    axes = ("seq", "grp")
    devices = lax.axis_size("seq") * lax.axis_size("grp")
    rows = qkv_weight.shape[0]
    ff_rows = shrink_weight.shape[0]
    chunks = FF // D
    total = piece * lax.axis_size("seq")
    start = lax.axis_index("seq") * piece
    info = jnp.concatenate(
        [jnp.stack([start, jnp.int32(total)]).astype(jnp.int32), seq_lengths.astype(jnp.int32)]
    )
    smalls = small_params.shape[1]

    packed = whole_call(
        pack_kernel,
        [((rows, 9 * D), BF16)],
        (merge_weight, expand_weight, shrink_weight),
        "pack",
        2,
        [pltpu.VMEM((GROUPS, ff_rows, LANES), F32)],
    )[0]
    packed = lax.all_gather(packed, axes, axis=0, tiled=True)
    early = jnp.concatenate(
        [qkv_weight.astype(BF16), jnp.pad(small_params.astype(BF16), ((0, 0), (0, LANES - smalls)))],
        axis=1,
    )
    last, ahead = (tokens[:, piece - WIN :], tokens[:, :WIN])
    beside = near_swap(last, ahead)
    across = diagonal_swap(ahead, last)
    early, done = gather_far(early)
    weight_a = gather_near(early[..., :CUT], done, "grp")
    weight_b = gather_near(early[..., CUT:], done, "seq")
    flat = tokens.reshape(seqs * piece, width)
    cot = (out_grad * answer_mask[:, :, None].astype(BF16)).reshape(seqs * piece, width)

    turned = flat.T
    old_rows = [entry[None, :] for entry in (qkv_rows, merge_rows, expand_rows, shrink_rows)]
    old_cols = [entry[None, :] for entry in (qkv_cols, merge_cols, expand_cols, shrink_cols)]
    turned, old_rows, old_cols, info = lax.optimization_barrier((turned, old_rows, old_cols, info))
    query, key, value, pool, rim_near, rim_across, vectors = project(
        info, beside, tokens, across, weight_a, weight_b
    )
    mixed, near_lse = near_attend(info, query, key, value)
    att, pkey, pvalue, far_lse = far_attend(
        info, query, pool, swap(rim_near, "seq", 0), across_swap(rim_across), mixed
    )
    att_flat = att.reshape(seqs * piece, width)
    (
        block_out, first_grad, hidden_low, active, up_grad, branch_grad, mixed_grad, att_grad, sums,
    ) = feed(flat, att_flat, cot, packed, vectors)

    merge_local = outer(att_flat, mixed_grad).astype(BF16).reshape(1, devices, rows, D)
    merge_chain = scatter_step(scatter_begin(merge_local, late_steps(True), 1))
    merge_local, branch_grad = lax.optimization_barrier((merge_local, branch_grad))
    shrink_local = outer(active, branch_grad).astype(BF16).reshape(chunks, devices, rows, D)
    shrink_chain = scatter_step(scatter_begin(shrink_local, late_steps(True), 1))
    (merge_chain,), (shrink_local, up_grad) = after([merge_chain], (shrink_local, up_grad))
    expand_local = outer(hidden_low, up_grad).astype(BF16).reshape(devices, rows, FF)
    expand_chain = scatter_step(scatter_begin(expand_local, late_steps(False)))
    late_chain = (jnp.concatenate([shrink_chain[0], merge_chain[0]], axis=0),) + shrink_chain[1:]
    chains = [late_chain, expand_chain]

    def seq_rows(value, which):
        return value[which * piece : (which + 1) * piece]

    def advance(states, gate):
        return [scatter_step(state, gate) if len(state[2]) > 1 else state for state in states]

    att_grad = att_grad.reshape(seqs, piece, width)
    chains, info = after(chains, info)
    full_parts, parts, rims = ([], [], [])
    for which in range(seqs):
        parts.append(back(which, info, query, key, value, pkey, pvalue, att_grad, near_lse, far_lse))
        info, _ = lax.optimization_barrier((info, parts[which][0]))
    for which in range(seqs):
        query_part, near_grad, far_grad, rim_near, rim_across = parts[which]
        if which:
            rim_near, rim_across, _ = lax.optimization_barrier((rim_near, rim_across, rims[which - 1][3:]))
        rims.append((query_part, near_grad, far_grad, swap(rim_near, "seq", 0), across_swap(rim_across)))
    chains = advance(chains, (parts[-1][0], rims[0][3:]))
    chains, vectors = after(chains, vectors)
    before = None
    for which in range(seqs):
        full_part, *before = pool_back(
            which, seqs, info, rims[which], key, value, vectors, turned, before, sums
        )
        full_parts.append(full_part.reshape(piece, 3 * width))
        if which == 0:
            while len(chains[0][2]) > bits_of("seq") - 1:
                chains = advance(chains, (full_part, rims[-1][3:]))
            chains, vectors = after(chains, vectors)
    late_parts = [chains[0][0][j] for j in range(chunks + 1)] + [chains[1][0]]
    late_chain = (jnp.concatenate(late_parts, axis=-1),) + chains[1][1:]
    late_chain = advance([late_chain], None)[0]
    (late_chain,), before = after([late_chain], before)
    early_chains = [
        scatter_step(scatter_begin(entry.reshape(devices, rows, -1), scatter_steps(first)))
        for entry, first in zip(before, ("seq", "grp"))
    ]
    for _ in range(bits_of("grp")):
        early_gate = early_chains[0][0]
        early_chains = [scatter_step(state) for state in early_chains]
    early_chain = (
        jnp.concatenate([state[0] for state in early_chains], axis=-1),
    ) + early_chains[0][1:]
    late_sum = scatter_end(late_chain, early_gate)
    base, expand_sum, shrink_sum = whole_call(
        late_kernel,
        [((1, 9 * D + LANES), F32), ((rows, FF), F32), ((ff_rows, D), F32)],
        (late_sum,) + tuple(old_rows),
        "late_stats",
        3,
        [pltpu.VMEM((GROUPS, ff_rows, LANES), F32)],
    )
    (early_chain,), base = after([early_chain], base)
    while len(early_chain[2]) > 1:
        early_chain = scatter_step(early_chain)
    early_blocks = scatter_blocks(early_chain)
    early_blocks += [jnp.zeros_like(early_blocks[0])] * (4 - len(early_blocks))
    full_parts, _ = lax.optimization_barrier((full_parts, early_chain[0]))
    input_grad = jnp.stack(
        [
            seq_rows(first_grad, which)
            + nt(full_parts[which][:, :CUT], weight_a)
            + nt(full_parts[which][:, CUT:], weight_b[:, : 3 * D - CUT])
            for which in range(seqs)
        ]
    )

    masters = (qkv_weight, merge_weight, expand_weight, shrink_weight)
    payload, early_sum = whole_call(
        stats_kernel,
        [((1, 9 * D + LANES), F32), (early_blocks[0].shape, F32)],
        (*early_blocks, base),
        "stats",
        1,
    )
    payload = summed_all(payload)
    outs = [((1, 1), F32)]
    for master in masters:
        high, wide = master.shape
        outs += [((high, wide), F32), ((1, high), F32), ((wide // LANES, LANES), F32), ((high, wide), F32)]
        outs += [((high, wide), BF16)]
    outs += [((smalls, rows), F32)] * 3 + [((smalls, rows), BF16)]
    fresh = whole_call(
        update_kernel,
        outs,
        (payload, early_sum, late_sum, expand_sum, shrink_sum)
        + tuple(old_rows)
        + tuple(old_cols)
        + masters
        + (small_params.T, small_moment.T),
        "update",
        5,
    )
    results = []
    for index in range(4):
        grad, rows_new, cols_new, new, low_new = fresh[1 + 5 * index : 6 + 5 * index]
        results += [grad, rows_new.reshape(-1), cols_new.reshape(-1), new, low_new]
    return (
        block_out.reshape(seqs, piece, width),
        input_grad,
        fresh[0].reshape(()),
        *results,
        *[entry.T for entry in fresh[21:]],
    )


def solution(mesh):
    whole = ("seq", "grp")
    matrix = P(whole, None)
    vector = P(whole)
    in_specs = (
        P("grp", "seq", None),
        P("grp"),
        P("grp", "seq"),
        P("grp", "seq", None),
        *[matrix] * 5,
        *[vector, P()] * 4,
        matrix,
    )
    out_specs = (
        P("grp", "seq", None),
        P("grp", "seq", None),
        P(),
        *[matrix, vector, P(), matrix, matrix] * 4,
        *[matrix] * 4,
    )
    return jax.shard_map(local, mesh=mesh, in_specs=in_specs, out_specs=out_specs, check_vma=False)
```
